256 devices in a mesh: dp: 16 (over y, x_lo, core), ctx: 16 (over x_hi, z).
Axes of the slice: x: 4 (x_hi: 2, x_lo: 2; x = x_hi * 2 + x_lo), y: 4, z: 8, core: 2. Of those that a mesh axis runs over, the one named last changes fastest.
Arguments:
- signal: bfloat16 [16, 4096, 4096], P('dp', 'ctx'), may hold values from -11 to 11
- cotangent: bfloat16 [16, 4096, 4096], P('dp', 'ctx'), may hold values from -6 to 6
- input_map: bfloat16 [16, 4096, 1024], P('dp', 'ctx'), may hold values from -1.75 to 1.75
- output_map: bfloat16 [16, 4096, 1024], P('dp', 'ctx'), may hold values from -1.75 to 1.75
- step_raw: float32 [16, 64, 4096], P('dp', None, 'ctx'), may hold values from -3 to 3
- decay_log: float32 [64], replicated, may hold values from -12 to 0
- step_bias: float32 [64], replicated, may hold values from -4 to -2.5
- skip_gain: float32 [64], replicated, may hold values from 0.5 to 2
- checkpoints: bfloat16 [16, 16, 64, 64, 128], P('dp', 'ctx'), may hold values from -1.75 to 1.75
Outputs:
- signal_grad: float32 [16, 4096, 4096], P('dp', 'ctx')
- input_map_grad: float32 [16, 4096, 1024], P('dp', 'ctx')
- output_map_grad: float32 [16, 4096, 1024], P('dp', 'ctx')
- step_raw_grad: float32 [16, 64, 4096], P('dp', None, 'ctx')
- decay_log_grad: float32 [64], replicated
- skip_gain_grad: float32 [64], replicated
- step_bias_grad: float32 [64], replicated
The draws below stay inside these ranges and needn't reach their ends.
All inputs are finite; a program needn't handle non-finite values.
Results may differ from the reference program's by a relative error of at most 0.0003.
Values sent between devices are 32-bit elements; how exact they have to be, the bound alone decides.
No kernel may reach another device: no remote copies, remote signals or barrier semaphores. Data moves between devices by JAX's collectives and lax.ppermute only.
A program may use at most 128 MiB of HBM per device.

```python
import jax
import jax.numpy as jnp
from jax import lax

H = 64
P_SIZE = 64
N = 128
G = 8
TOK_DEV = 256
SEQS = 16
LENGTH = 4096
N_CTX = 16


def common_field(key):
    return jnp.clip(jax.random.normal(key, (SEQS, LENGTH, H * P_SIZE), jnp.float32), -5.0, 5.0)


def draw_signal(key, part):
    shared = common_field(key)
    return shared.astype(jnp.bfloat16)


def draw_cotangent(key, part):
    shared = common_field(key)
    key = jax.random.fold_in(key, 12)
    own_noise = jnp.clip(jax.random.normal(key, (SEQS, LENGTH, H * P_SIZE), jnp.float32), -5.0, 5.0)
    return (own_noise + 0.05 * shared).astype(jnp.bfloat16)


def draw_decay_log(key, part):
    key = jax.random.fold_in(key, 13)
    key_pick, key_fast, key_slow = jax.random.split(key, 3)
    fast_share = 0.5
    fast_pick = jax.random.uniform(key_pick, (H,), jnp.float32) < fast_share
    fast_rate = jax.random.uniform(key_fast, (H,), jnp.float32, -1.386, 0.0)
    slow_rate = jnp.log(20.0 / LENGTH) + jax.random.uniform(key_slow, (H,), jnp.float32, -1.609, 0.693)
    slow_rate = jnp.minimum(slow_rate, -0.01)
    return jnp.where(fast_pick, fast_rate, slow_rate)


def draw_step_raw(key, part):
    key = jax.random.fold_in(key, 14)
    key_base, key_offset = jax.random.split(key)
    base_noise = jnp.clip(0.4 * jax.random.normal(key_base, (SEQS, H, LENGTH), jnp.float32), -1.2, 1.2)
    offsets = jax.random.uniform(key_offset, (SEQS, H, LENGTH // TOK_DEV), jnp.float32, -0.5, 0.5)
    return base_noise + jnp.repeat(offsets, TOK_DEV, axis=2)


def level_of(own_key, shape, cuts, low, top_value):
    loudness = 1.0
    for position, blocks in cuts:
        steps = jax.random.uniform(jax.random.fold_in(jax.random.fold_in(own_key, 6), position), (blocks,), jnp.float32, low / len(cuts), top_value / len(cuts))
        loudness = loudness * jnp.repeat(jnp.exp(steps), shape[position] // blocks).reshape((-1,) + (1,) * (len(shape) - 1 - position))
    return loudness


def gaussian(rng, extent, deviation, bound, cuts=(), kind=jnp.bfloat16):
    factor_of = level_of(rng, extent, cuts, -0.22, 0.18) if cuts else 1.0
    values = jax.random.normal(rng, extent, jnp.float32) * deviation * factor_of
    return jnp.minimum(jnp.maximum(values, -bound), bound).astype(kind)


def setup_inputs(seed: int = 0) -> dict:
    streams_of = jax.random.split(jax.random.key(seed), 10)
    return {
        "signal": draw_signal(jax.random.fold_in(streams_of[9], 71), 0),
        "cotangent": draw_cotangent(jax.random.fold_in(streams_of[9], 71), 0),
        "input_map": gaussian(streams_of[2], (SEQS, LENGTH, G * N), 0.3, 1.75, ((0, 16), (1, 16))),
        "output_map": gaussian(streams_of[3], (SEQS, LENGTH, G * N), 0.3, 1.75, ((0, 16), (1, 16))),
        "step_raw": draw_step_raw(jax.random.fold_in(streams_of[9], 71), 0),
        "decay_log": draw_decay_log(jax.random.fold_in(streams_of[9], 71), 0),
        "step_bias": jnp.clip(jax.random.uniform(streams_of[6], (H,), jnp.float32, -4.0, -2.5), -4.0, -2.5),
        "skip_gain": jnp.clip(jax.random.uniform(streams_of[7], (H,), jnp.float32, 0.5, 2.0), 0.5, 2.0),
        "checkpoints": gaussian(streams_of[8], (SEQS, N_CTX, H, P_SIZE, N), 0.3, 1.75, ((0, 16), (1, 16))),
    }


highest = lax.Precision.HIGHEST


def prepare(raw_steps, decay_log, step_bias):
    pre_act = raw_steps + step_bias[:, None]
    step_size = jax.nn.softplus(pre_act)
    rate = -jnp.exp(decay_log)[:, None] * step_size
    cumul = jnp.cumsum(rate, axis=1)
    return pre_act, step_size, cumul


def local_state(grads_out, out_block, cumul, group_count):
    length = out_block.shape[0]
    head_count = cumul.shape[0]
    per_group = head_count // group_count
    weights = jnp.exp(cumul).reshape(group_count, per_group, length)
    grad_float = grads_out.astype(jnp.float32).reshape(length, group_count, per_group, -1)
    out_float = out_block.astype(jnp.float32).reshape(length, group_count, -1)
    state = jnp.einsum('ghl,lghp,lgn->ghpn', weights, grad_float, out_float, precision=highest)
    return state.reshape(head_count, grad_float.shape[3], out_float.shape[2]), jnp.exp(cumul[:, -1])


def group_grads(sig_group, grad_group, in_group, out_group, steps_group, cumul_group, rates, skips, start_group, end_group):
    sig_float = sig_group.astype(jnp.float32)
    grad_float = grad_group.astype(jnp.float32)
    in_float = in_group.astype(jnp.float32)
    out_float = out_group.astype(jnp.float32)
    length = sig_float.shape[0]
    rows_index = lax.broadcasted_iota(jnp.int32, (length, length), 0)
    cols_index = lax.broadcasted_iota(jnp.int32, (length, length), 1)
    lower = (rows_index >= cols_index)[None]
    scores = jnp.dot(out_float, in_float.T, precision=highest)
    differ = cumul_group[:, :, None] - cumul_group[:, None, :]
    decay = jnp.where(lower, jnp.exp(jnp.where(lower, differ, 0.0)), 0.0)
    mixing = decay * scores[None] * steps_group[:, None, :]
    mix_grad = jnp.einsum('thp,shp->hts', grad_float, sig_float, precision=highest)
    final = cumul_group[:, -1:]
    carry_weight = jnp.exp(final - cumul_group) * steps_group
    end_in = jnp.einsum('hpn,sn->shp', end_group, in_float, precision=highest)
    sig_grad = jnp.einsum('hts,thp->shp', mixing, grad_float, precision=highest)
    sig_grad = sig_grad + skips[None, :, None] * grad_float + carry_weight.T[:, :, None] * end_in
    weighted = mix_grad * decay
    score_grad = jnp.sum(weighted * steps_group[:, None, :], axis=0)
    entry = jnp.exp(cumul_group)
    start_out = jnp.einsum('hpn,tn->thp', start_group, out_float, precision=highest)
    out_grad = jnp.dot(score_grad, in_float, precision=highest)
    out_grad = out_grad + jnp.einsum('hpn,thp,ht->tn', start_group, grad_float, entry, precision=highest)
    in_grad = jnp.dot(score_grad.T, out_float, precision=highest)
    in_grad = in_grad + jnp.einsum('hpn,shp,hs->sn', end_group, sig_float, carry_weight, precision=highest)
    product = mix_grad * mixing
    cumul_grad = jnp.sum(product, axis=2) - jnp.sum(product, axis=1)
    cumul_grad = cumul_grad + entry * jnp.einsum('thp,thp->ht', grad_float, start_out)
    pushed = jnp.einsum('shp,shp->hs', sig_float, end_in)
    cumul_grad = cumul_grad - carry_weight * pushed
    tail = jnp.exp(final[:, 0]) * jnp.sum(end_group * start_group, axis=(1, 2)) + jnp.sum(carry_weight * pushed, axis=1)
    cumul_grad = jnp.concatenate([cumul_grad[:, :-1], cumul_grad[:, -1:] + tail[:, None]], axis=1)
    rate_grad = jnp.cumsum(cumul_grad[:, ::-1], axis=1)[:, ::-1]
    step_grad = jnp.einsum('hts,ts->hs', weighted, scores, precision=highest)
    step_grad = step_grad + jnp.exp(final - cumul_group) * pushed - rate_grad * rates[:, None]
    decay_grad = jnp.sum(rate_grad * (-rates[:, None] * steps_group), axis=1)
    skip_grad = jnp.einsum('thp,thp->h', grad_float, sig_float)
    return sig_grad, in_grad, out_grad, step_grad, decay_grad, skip_grad


def block_grads(sig_block, grad_block, in_block, out_block, raw_steps, decay_log, step_bias, skip_gain, start_state, end_state, group_count):
    length = sig_block.shape[0]
    head_count = raw_steps.shape[0]
    per_group = head_count // group_count
    head_width = sig_block.shape[1] // head_count
    state_width = in_block.shape[1] // group_count
    pre_act, step_size, cumul = prepare(raw_steps, decay_log, step_bias)
    sig_groups = sig_block.reshape(length, group_count, per_group, head_width).transpose(1, 0, 2, 3)
    grad_groups = grad_block.reshape(length, group_count, per_group, head_width).transpose(1, 0, 2, 3)
    in_groups = in_block.reshape(length, group_count, state_width).transpose(1, 0, 2)
    out_groups = out_block.reshape(length, group_count, state_width).transpose(1, 0, 2)
    step_groups = step_size.reshape(group_count, per_group, length)
    cumul_groups = cumul.reshape(group_count, per_group, length)
    rate_groups = jnp.exp(decay_log).reshape(group_count, per_group)
    skip_groups = skip_gain.reshape(group_count, per_group)
    start_groups = start_state.astype(jnp.float32).reshape(group_count, per_group, head_width, state_width)
    end_groups = end_state.reshape(group_count, per_group, head_width, state_width)
    results = lax.map(lambda pieces: group_grads(*pieces), (sig_groups, grad_groups, in_groups, out_groups, step_groups, cumul_groups, rate_groups, skip_groups, start_groups, end_groups))
    sig_grad = results[0].transpose(1, 0, 2, 3).reshape(length, head_count * head_width)
    in_grad = results[1].transpose(1, 0, 2).reshape(length, group_count * state_width)
    out_grad = results[2].transpose(1, 0, 2).reshape(length, group_count * state_width)
    pre_grad = results[3].reshape(head_count, length) * jax.nn.sigmoid(pre_act)
    return sig_grad, in_grad, out_grad, pre_grad, results[4].reshape(head_count), results[5].reshape(head_count), jnp.sum(pre_grad, axis=1)


def reference(signal, cotangent, input_map, output_map, step_raw, decay_log, step_bias, skip_gain, checkpoints):
    blocks = LENGTH // TOK_DEV

    def one_sequence(pieces):
        sig_seq, grad_seq, in_seq, out_seq, raw_seq, start_seq = pieces
        sig_blocks = sig_seq.reshape(blocks, TOK_DEV, -1)
        grad_blocks = grad_seq.reshape(blocks, TOK_DEV, -1)
        in_blocks = in_seq.reshape(blocks, TOK_DEV, -1)
        out_blocks = out_seq.reshape(blocks, TOK_DEV, -1)
        raw_blocks = raw_seq.reshape(H, blocks, TOK_DEV).transpose(1, 0, 2)

        def first_pass(parts):
            grad_block, out_block, raw_block = parts
            cumul = prepare(raw_block, decay_log, step_bias)[2]
            return local_state(grad_block, out_block, cumul, G)

        states, totals = lax.map(first_pass, (grad_blocks, out_blocks, raw_blocks))

        def chain_link(carry, parts):
            state, total = parts
            return state + total[:, None, None] * carry, carry

        ends = lax.scan(chain_link, jnp.zeros_like(states[0]), (states, totals), reverse=True)[1]

        def second_pass(parts):
            return block_grads(parts[0], parts[1], parts[2], parts[3], parts[4], decay_log, step_bias, skip_gain, parts[5], parts[6], G)

        results = lax.map(second_pass, (sig_blocks, grad_blocks, in_blocks, out_blocks, raw_blocks, start_seq, ends))
        raw_grad = results[3].transpose(1, 0, 2).reshape(H, LENGTH)
        return (results[0].reshape(LENGTH, -1), results[1].reshape(LENGTH, -1), results[2].reshape(LENGTH, -1), raw_grad,
                jnp.sum(results[4], axis=0), jnp.sum(results[5], axis=0), jnp.sum(results[6], axis=0))

    outs = lax.map(one_sequence, (signal, cotangent, input_map, output_map, step_raw, checkpoints))
    factor = 1.0 / (SEQS * LENGTH)
    return (outs[0], outs[1], outs[2], outs[3], jnp.sum(outs[4], axis=0) * factor,
            jnp.sum(outs[5], axis=0) * factor, jnp.sum(outs[6], axis=0) * factor)
```

```python
import jax
import jax.numpy as jnp
from jax import lax
from jax.experimental import pallas as pl
from jax.experimental.pallas import tpu as pltpu
from jax.sharding import PartitionSpec as P

T = 256
H = 64
G = 8
D = 64
N = 128
PER = H // G
WIDE = PER * D
F32 = jnp.float32
BF16 = jnp.bfloat16
VMEM_LIMIT = 40 * 1024 * 1024


def split(x, parts):
    pieces = []
    for _ in range(parts):
        piece = x.astype(BF16)
        pieces.append(piece)
        x = x - piece.astype(F32)
    return pieces


def mm(a, b):
    return lax.dot_general(a, b, (((1,), (0,)), ((), ())), preferred_element_type=F32)


def mm_nt(a, b):
    return lax.dot_general(a, b, (((1,), (1,)), ((), ())), preferred_element_type=F32)


def mm_tn(a, b):
    return lax.dot_general(a, b, (((0,), (0,)), ((), ())), preferred_element_type=F32)


def rows_times_mask(rows, mask):
    out = mm(jnp.concatenate(split(rows, 3), axis=0), mask)
    return out[:PER] + out[PER : 2 * PER] + out[2 * PER :]


def mask_of(relation):
    i = lax.broadcasted_iota(jnp.int32, (T, T), 0)
    j = lax.broadcasted_iota(jnp.int32, (T, T), 1)
    return jnp.where(relation(i, j), 1.0, 0.0).astype(BF16)


def steps_of(raw, bias, decay_log):
    pre_act = raw + bias
    step = jnp.maximum(pre_act, 0.0) + jnp.log1p(jnp.exp(-jnp.abs(pre_act)))
    decay = jnp.exp(decay_log)
    rate = -decay * step
    cumul = rows_times_mask(rate, mask_of(lambda i, j: i <= j))
    return pre_act, step, decay, cumul


def spread(rows):
    head = lax.broadcasted_iota(jnp.int32, (PER, WIDE), 0)
    column = lax.broadcasted_iota(jnp.int32, (PER, WIDE), 1)
    own = jnp.where(column // D == head, 1.0, 0.0).astype(BF16)
    return mm_tn(jnp.concatenate(split(rows, 3), axis=0), jnp.concatenate([own] * 3, axis=0))


def columns(rows):
    pad = jnp.zeros((128 - PER * len(rows), T), F32)
    return jnp.transpose(jnp.concatenate(list(rows) + [pad], axis=0))


def state_kernel(cot_ref, out_ref, raw_ref, decay_ref, bias_ref, sent_ref):
    cumul = steps_of(raw_ref[...], bias_ref[...], decay_ref[...])[3]
    entry = jnp.exp(cumul)
    weighted = cot_ref[...].astype(F32) * spread(entry)
    out_map = out_ref[...]
    high, low = split(weighted, 2)
    state = mm_tn(high, out_map) + mm_tn(low, out_map)
    total = jnp.broadcast_to(entry[:, T - 1 :], (PER, N))
    half = WIDE // 2
    sent_ref[0, :half] = state[:half]
    sent_ref[1, :half] = state[half:]
    sent_ref[0, half:] = total
    sent_ref[1, half:] = jnp.concatenate([total[PER // 2 :], total[: PER // 2]], axis=0)


def scan_kernel(state_ref, total_ref, end_ref):
    head = pl.program_id(0)
    carry = jnp.zeros((D, N), F32)
    for b in reversed(range(state_ref.shape[0])):
        end_ref[b] = carry
        carry = state_ref[b] + total_ref[b, pl.ds(head, 1), :] * carry


def inner_kernel(
    sig_ref,
    cot_ref,
    in_ref,
    out_ref,
    raw_ref,
    decay_ref,
    bias_ref,
    skip_ref,
    start_ref,
    sig_grad_ref,
    in_grad_ref,
    out_grad_ref,
    step_grad_ref,
    by_decay_ref,
    by_bias_ref,
    sums_ref,
):
    pre_act, step, decay, cumul = steps_of(raw_ref[...], bias_ref[...], decay_ref[...])
    slope = jax.nn.sigmoid(pre_act)
    entry = jnp.exp(cumul)
    final = cumul[:, T - 1 :]
    total = jnp.exp(final)
    leave = jnp.exp(final - cumul)
    later = rows_times_mask(slope, mask_of(lambda i, j: i > j))
    cols = columns([cumul - jnp.log(step), entry])
    in_map = in_ref[...]
    out_map = out_ref[...]
    out_float = out_map.astype(F32)
    scores = mm_nt(in_map, out_map)
    valid = lax.broadcasted_iota(jnp.int32, (T, T), 0) <= lax.broadcasted_iota(jnp.int32, (T, T), 1)
    lane = lax.broadcasted_iota(jnp.int32, (T, N), 1)
    first = lane < D
    score_grad = jnp.zeros((T, T), F32)
    out_grad = jnp.zeros((T, N), F32)
    found = jnp.zeros((T, N), F32)
    row_sums = []
    for pair in range(PER // 2):
        at = slice(pair * N, (pair + 1) * N)
        sig = sig_ref[:, at]
        cot = cot_ref[:, at]
        zero = jnp.zeros_like(sig)
        sig_grad = jnp.zeros((T, N), F32)
        start = start_ref[at, :]
        top = lax.broadcasted_iota(jnp.int32, (N, N), 0) < D
        none = jnp.zeros_like(start)
        both = jnp.concatenate(
            [jnp.where(top, start, none), jnp.where(top, none, start)], axis=1
        )
        began = mm(cot, both)
        for k in range(2):
            j = 2 * pair + k
            mine = first if k == 0 else jnp.logical_not(first)
            own_sig = jnp.where(mine, sig, zero)
            own_cot = jnp.where(mine, cot, zero)
            mix_grad = mm_nt(own_sig, cot)
            fade = jnp.where(valid, jnp.exp(cumul[j : j + 1, :] - cols[:, j : j + 1]), 0.0)
            mixing = fade * scores
            high, low = split(mixing, 2)
            sig_grad = sig_grad + (mm(high, own_cot) + mm(low, own_cot))
            score_grad = score_grad + mix_grad * fade
            product = mix_grad * mixing
            row_sums.append(jnp.sum(product, axis=0, keepdims=True))
            found = jnp.where(lane == j, jnp.sum(product, axis=1, keepdims=True), found)
            own = began[:, k * N : (k + 1) * N]
            out_grad = out_grad + own * cols[:, PER + j : PER + j + 1]
            found = jnp.where(
                lane == PER + j, jnp.sum(own * out_float, axis=1, keepdims=True), found
            )
        sig_grad_ref[:, at] = sig_grad
    sig_float = sig_ref[...].astype(F32)
    cot_float = cot_ref[...].astype(F32)
    skip = skip_ref[...]
    sig_grad_ref[...] = sig_grad_ref[...] + skip * cot_float
    high, low = split(score_grad, 2)
    in_grad_ref[...] = mm(high, out_map) + mm(low, out_map)
    out_grad_ref[...] = out_grad + (mm_tn(high, in_map) + mm_tn(low, in_map))
    found = jnp.transpose(found)
    col_sum = found[:PER]
    from_start = found[PER : 2 * PER]
    cumul_grad = jnp.concatenate(row_sums, axis=0) - col_sum + entry * from_start
    rate_grad = rows_times_mask(cumul_grad, mask_of(lambda i, j: i >= j))
    step_grad = col_sum / step - rate_grad * decay
    step_grad_ref[...] = step_grad
    into_decay = (final - cumul) * leave * step
    into_bias = leave * (slope - decay * step * later)
    start = start_ref[...].astype(F32).reshape(PER, D, N)
    for rows, weight, ref in (
        (into_decay, final * total, by_decay_ref),
        (into_bias, -decay * total * jnp.sum(slope, axis=1, keepdims=True), by_bias_ref),
    ):
        high, low = split(sig_float * spread(rows), 2)
        grown = mm_tn(high, in_map) + mm_tn(low, in_map)
        ref[...] = grown + (start * weight[:, :, None]).reshape(WIDE, N)
    own = jnp.where(
        lax.broadcasted_iota(jnp.int32, (PER, WIDE), 1) // D
        == lax.broadcasted_iota(jnp.int32, (PER, WIDE), 0),
        1.0,
        0.0,
    )
    skip_sum = jnp.sum(
        own * jnp.sum(sig_float * cot_float, axis=0, keepdims=True), axis=1, keepdims=True
    )
    decay_sum = -decay * jnp.sum(rate_grad * step, axis=1, keepdims=True)
    bias_sum = jnp.sum(step_grad * slope, axis=1, keepdims=True)
    which = lax.broadcasted_iota(jnp.int32, (PER, N), 1)
    sums_ref[...] = jnp.where(
        which == 0, decay_sum, jnp.where(which == 1, bias_sum, jnp.where(which == 2, skip_sum, 0.0))
    )


def sums_kernel(end_ref, by_decay_ref, by_bias_ref, sums_ref, sent_ref, kept):
    group = pl.program_id(0)
    end = end_ref[...]
    which = lax.broadcasted_iota(jnp.int32, (PER, N), 1)
    sums = sums_ref[...]
    for k, ref in enumerate((by_decay_ref, by_bias_ref)):
        partial = jnp.sum((end * ref[...]).reshape(PER, D, N), axis=1)
        sums = sums + jnp.where(which == k, jnp.sum(partial, axis=1, keepdims=True), 0.0)

    @pl.when(group == 0)
    def _():
        kept[...] = jnp.zeros_like(kept)

    kept[pl.ds(pl.multiple_of(group * PER, PER), PER), :] = sums

    @pl.when(group == G - 1)
    def _():
        rows = jnp.transpose(kept[...])[:8]
        sent_ref[...] = jnp.broadcast_to(rows[None], sent_ref.shape)


def outer_kernel(
    end_ref,
    sig_ref,
    in_ref,
    raw_ref,
    decay_ref,
    bias_ref,
    start_ref,
    sig_part_ref,
    in_part_ref,
    step_part_ref,
    sig_grad_ref,
    in_grad_ref,
    step_grad_ref,
):
    pre_act, step, decay, cumul = steps_of(raw_ref[...], bias_ref[...], decay_ref[...])
    slope = jax.nn.sigmoid(pre_act)
    final = cumul[:, T - 1 :]
    leave = jnp.exp(final - cumul)
    carry = leave * step
    end = end_ref[...]
    in_map = in_ref[...]
    sig = sig_ref[...].astype(F32)
    wide = spread(carry)
    end_high, end_low = split(end, 2)
    end_in = mm_nt(in_map, end_high) + mm_nt(in_map, end_low)
    sig_grad_ref[...] = sig_part_ref[...] + wide * end_in
    high, low = split(sig * wide, 2)
    in_grad_ref[...] = (
        in_part_ref[...] + mm(high, end_high) + (mm(high, end_low) + mm(low, end_high))
    )
    own = jnp.where(
        lax.broadcasted_iota(jnp.int32, (PER, WIDE), 1) // D
        == lax.broadcasted_iota(jnp.int32, (PER, WIDE), 0),
        1.0,
        0.0,
    ).astype(BF16)
    high, low = split(sig * end_in, 2)
    pushed = mm_nt(own, high) + mm_nt(own, low)
    before = rows_times_mask(carry * pushed, mask_of(lambda i, j: i < j))
    held = jnp.sum((end * start_ref[...].astype(F32)).reshape(PER, D, N), axis=1)
    held = jnp.exp(final) * jnp.sum(held, axis=1, keepdims=True)
    step_grad = step_part_ref[...] + leave * pushed - decay * (before + held)
    step_grad_ref[...] = step_grad * slope


def call(kernel, grid, ins, outs, args, flops, scratch=()):
    moved = sum(a.size * a.dtype.itemsize for a in args) + sum(4 * s.size for _, s in outs)
    return pl.pallas_call(
        kernel,
        grid=(grid,),
        in_specs=ins,
        out_specs=[spec for spec, _ in outs],
        out_shape=[shape for _, shape in outs],
        scratch_shapes=list(scratch),
        compiler_params=pltpu.CompilerParams(
            dimension_semantics=("arbitrary",), vmem_limit_bytes=VMEM_LIMIT
        ),
        cost_estimate=pl.CostEstimate(flops=flops, bytes_accessed=moved, transcendentals=0),
    )(*args)


def f32(*shape):
    return jax.ShapeDtypeStruct(shape, F32)


WIDE_COLS = pl.BlockSpec((T, WIDE), lambda g: (0, g))
MAP_COLS = pl.BlockSpec((T, N), lambda g: (0, g))
HEAD_ROWS = pl.BlockSpec((PER, T), lambda g: (g, 0))
HEAD_ONE = pl.BlockSpec((PER, 1), lambda g: (g, 0))
HEAD_LANES = pl.BlockSpec((PER, N), lambda g: (g, 0))
STATE_ROWS = pl.BlockSpec((WIDE, N), lambda g: (g, 0))
SKIP_COLS = pl.BlockSpec((1, WIDE), lambda g: (0, g))


def local(
    signal, cotangent, input_map, output_map, step_raw, decay_log, step_bias, skip_gain, checkpoints
):
    sig, cot, in_map, out_map, raw = (
        signal[0],
        cotangent[0],
        input_map[0],
        output_map[0],
        step_raw[0],
    )
    decay_col, bias_col = decay_log[:, None], step_bias[:, None]
    skip_row = jnp.repeat(skip_gain, D)[None, :]
    start = checkpoints.reshape(H * D, N)
    blocks = lax.axis_size("ctx")
    rows = H * D // blocks
    own = H // blocks

    sent = call(
        state_kernel,
        G,
        [WIDE_COLS, MAP_COLS, HEAD_ROWS, HEAD_ONE, HEAD_ONE],
        [
            (
                pl.BlockSpec((blocks // G, rows + 8, N), lambda g: (g, 0, 0)),
                f32(blocks, rows + 8, N),
            )
        ],
        (cot, out_map, raw, decay_col, bias_col),
        4 * H * D * N * T,
    )[0]
    states = lax.all_to_all(sent, "ctx", 0, 0)
    ends = call(
        scan_kernel,
        own,
        [
            pl.BlockSpec((blocks, D, N), lambda i: (0, i, 0)),
            pl.BlockSpec((blocks, 8, N), lambda i: (0, rows // 8, 0)),
        ],
        [(pl.BlockSpec((blocks, D, N), lambda i: (0, i, 0)), f32(blocks, rows, N))],
        (states, states),
        2 * H * D * N,
    )[0]
    end = lax.all_to_all(ends, "ctx", 0, 0).reshape(H * D, N)

    sig_part, in_part, out_grad, step_part, by_decay, by_bias, sums = call(
        inner_kernel,
        G,
        [
            WIDE_COLS,
            WIDE_COLS,
            MAP_COLS,
            MAP_COLS,
            HEAD_ROWS,
            HEAD_ONE,
            HEAD_ONE,
            SKIP_COLS,
            STATE_ROWS,
        ],
        [
            (WIDE_COLS, f32(T, H * D)),
            (MAP_COLS, f32(T, G * N)),
            (MAP_COLS, f32(T, G * N)),
            (HEAD_ROWS, f32(H, T)),
            (STATE_ROWS, f32(H * D, N)),
            (STATE_ROWS, f32(H * D, N)),
            (HEAD_LANES, f32(H, N)),
        ],
        (sig, cot, in_map, out_map, raw, decay_col, bias_col, skip_row, start),
        H * T * T * N * 20,
    )

    sent = call(
        sums_kernel,
        G,
        [STATE_ROWS, STATE_ROWS, STATE_ROWS, HEAD_LANES],
        [(pl.BlockSpec((blocks, 8, N), lambda g: (0, 0, 0)), f32(blocks, 8, N))],
        (end, by_decay, by_bias, sums),
        4 * H * D * N,
        [pltpu.VMEM((N, N), F32)],
    )[0]
    summed = jnp.sum(lax.all_to_all(sent, "ctx", 0, 0), axis=0)
    sent = jnp.broadcast_to(summed[None], (lax.axis_size("dp"),) + summed.shape)
    summed = jnp.sum(lax.all_to_all(sent, "dp", 0, 0), axis=0)
    summed = summed * (1.0 / (lax.axis_size("dp") * blocks * T))

    sig_grad, in_grad, step_grad = call(
        outer_kernel,
        G,
        [
            STATE_ROWS,
            WIDE_COLS,
            MAP_COLS,
            HEAD_ROWS,
            HEAD_ONE,
            HEAD_ONE,
            STATE_ROWS,
            WIDE_COLS,
            MAP_COLS,
            HEAD_ROWS,
        ],
        [(WIDE_COLS, f32(T, H * D)), (MAP_COLS, f32(T, G * N)), (HEAD_ROWS, f32(H, T))],
        (end, sig, in_map, raw, decay_col, bias_col, start, sig_part, in_part, step_part),
        8 * H * D * N * T,
    )
    return (
        sig_grad[None],
        in_grad[None],
        out_grad[None],
        step_grad[None],
        summed[0, :H],
        summed[2, :H],
        summed[1, :H],
    )


def solution(mesh):
    rows = P("dp", "ctx", None)
    placed = (rows, rows, rows, rows, P("dp", None, "ctx"), P(), P(), P())
    return jax.shard_map(
        local,
        mesh=mesh,
        in_specs=placed + (P("dp", "ctx", None, None, None),),
        out_specs=(rows, rows, rows, P("dp", None, "ctx"), P(), P(), P()),
        check_vma=False,
    )
```

```python
import math

import jax
import jax.numpy as jnp
from jax import lax
from jax.experimental import pallas as pl
from jax.experimental.pallas import tpu as pltpu
from jax.sharding import PartitionSpec as P

T = 256
H = 64
G = 8
D = 64
N = 128
PER = H // G
WIDE = PER * D
F32 = jnp.float32
BF16 = jnp.bfloat16
AT_ONCE = 2
MIB = 1024 * 1024


def split(x, parts):
    pieces = []
    for _ in range(parts):
        piece = x.astype(BF16)
        pieces.append(piece)
        x = x - piece.astype(F32)
    return pieces


def mm(a, b):
    return lax.dot_general(a, b, (((1,), (0,)), ((), ())), preferred_element_type=F32)


def mm_nt(a, b):
    return lax.dot_general(a, b, (((1,), (1,)), ((), ())), preferred_element_type=F32)


def mm_tn(a, b):
    return lax.dot_general(a, b, (((0,), (0,)), ((), ())), preferred_element_type=F32)


def rows_times_mask(rows, mask):
    n = rows.shape[0]
    out = mm(jnp.concatenate(split(rows, 3), axis=0), mask)
    return out[:n] + out[n : 2 * n] + out[2 * n :]


def mask_of(relation):
    i = lax.broadcasted_iota(jnp.int32, (T, T), 0)
    j = lax.broadcasted_iota(jnp.int32, (T, T), 1)
    return jnp.where(relation(i, j), 1.0, 0.0).astype(BF16)


def column_of(row, first, count):
    i = lax.broadcasted_iota(jnp.int32, (count, H), 0) + first
    j = lax.broadcasted_iota(jnp.int32, (count, H), 1)
    return jnp.sum(jnp.where(i == j, row, 0.0), axis=1, keepdims=True)


def steps_of(raw, bias, decay_log):
    pre_act = raw + bias
    step = jnp.maximum(pre_act, 0.0) + jnp.log1p(jnp.exp(-jnp.abs(pre_act)))
    decay = jnp.exp(decay_log)
    rate = -decay * step
    cumul = rows_times_mask(rate, mask_of(lambda i, j: i <= j))
    return pre_act, step, decay, cumul


def spread(rows):
    head = lax.broadcasted_iota(jnp.int32, (PER, WIDE), 0)
    column = lax.broadcasted_iota(jnp.int32, (PER, WIDE), 1)
    own = jnp.where(column // D == head, 1.0, 0.0).astype(BF16)
    return mm_tn(jnp.concatenate(split(rows, 3), axis=0), jnp.concatenate([own] * 3, axis=0))


def columns(rows):
    pad = jnp.zeros((128 - PER * len(rows), T), F32)
    return jnp.transpose(jnp.concatenate(list(rows) + [pad], axis=0))


def state_kernel(cot_ref, out_ref, raw_ref, decay_ref, bias_ref, sent_ref, entry_ref):
    step = pl.program_id(0)

    @pl.when(step == 0)
    def _():
        bias = column_of(bias_ref[...], 0, H)
        decay_log = column_of(decay_ref[...], 0, H)
        entry_ref[...] = jnp.exp(steps_of(raw_ref[...], bias, decay_log)[3])

    half = WIDE // 2
    for k in range(AT_ONCE):
        at = pl.multiple_of((step * AT_ONCE + k) * PER, PER)
        entry = entry_ref[pl.ds(at, PER), :]
        cot = jnp.transpose(cot_ref[:, k * WIDE : (k + 1) * WIDE]).astype(F32)
        weighted = (cot.reshape(PER, D, T) * entry[:, None, :]).reshape(WIDE, T)
        out_map = out_ref[:, k * N : (k + 1) * N]
        high, low = split(weighted, 2)
        state = mm(high, out_map) + mm(low, out_map)
        total = jnp.broadcast_to(entry[:, T - 1 :], (PER, N))
        sent_ref[2 * k, :half] = state[:half]
        sent_ref[2 * k + 1, :half] = state[half:]
        sent_ref[2 * k, half:] = total
        sent_ref[2 * k + 1, half:] = jnp.concatenate(
            [total[PER // 2 :], total[: PER // 2]], axis=0
        )


def scan_kernel(state_ref, total_ref, end_ref):
    head = pl.program_id(0)
    carry = jnp.zeros((D, N), F32)
    for b in reversed(range(state_ref.shape[0])):
        end_ref[b] = carry
        carry = state_ref[b] + total_ref[b, pl.ds(head, 1), :] * carry


def inner_kernel(
    sig_ref,
    cot_ref,
    in_ref,
    out_ref,
    raw_ref,
    decay_ref,
    bias_ref,
    skip_ref,
    start_ref,
    sig_grad_ref,
    in_grad_ref,
    out_grad_ref,
    step_grad_ref,
    by_decay_ref,
    by_bias_ref,
    sums_ref,
    carry_ref,
    leave_ref,
    slope_ref,
    sig_high_ref,
    sig_low_ref,
):
    head = pl.program_id(0) * PER
    bias = column_of(bias_ref[...], head, PER)
    decay_log = column_of(decay_ref[...], head, PER)
    pre_act, step, decay, cumul = steps_of(raw_ref[...], bias, decay_log)
    slope = jax.nn.sigmoid(pre_act)
    entry = jnp.exp(cumul)
    final = cumul[:, T - 1 :]
    total = jnp.exp(final)
    leave = jnp.exp(final - cumul)
    carry = leave * step
    carry_ref[...] = carry
    leave_ref[...] = leave
    slope_ref[...] = slope
    later = rows_times_mask(slope, mask_of(lambda i, j: i > j))
    cols = columns([cumul - jnp.log(step), entry])
    in_map = in_ref[...]
    out_map = out_ref[...]
    out_float = out_map.astype(F32)
    scores = mm_nt(in_map, out_map)
    valid = lax.broadcasted_iota(jnp.int32, (T, T), 0) <= lax.broadcasted_iota(jnp.int32, (T, T), 1)
    lane = lax.broadcasted_iota(jnp.int32, (T, N), 1)
    first = lane < D
    score_grad = jnp.zeros((T, T), F32)
    out_grad = jnp.zeros((T, N), F32)
    found = jnp.zeros((T, N), F32)
    row_sums = []
    for pair in range(PER // 2):
        at = slice(pair * N, (pair + 1) * N)
        sig = sig_ref[:, at]
        cot = cot_ref[:, at]
        zero = jnp.zeros_like(sig)
        sig_grad = jnp.zeros((T, N), F32)
        start = start_ref[at, :]
        top = lax.broadcasted_iota(jnp.int32, (N, N), 0) < D
        none = jnp.zeros_like(start)
        both = jnp.concatenate(
            [jnp.where(top, start, none), jnp.where(top, none, start)], axis=1
        )
        began = mm(cot, both)
        for k in range(2):
            j = 2 * pair + k
            mine = first if k == 0 else jnp.logical_not(first)
            own_sig = jnp.where(mine, sig, zero)
            own_cot = jnp.where(mine, cot, zero)
            mix_grad = mm_nt(own_sig, cot)
            fade = jnp.where(valid, jnp.exp(cumul[j : j + 1, :] - cols[:, j : j + 1]), 0.0)
            mixing = fade * scores
            high, low = split(mixing, 2)
            sig_grad = sig_grad + (mm(high, own_cot) + mm(low, own_cot))
            score_grad = score_grad + mix_grad * fade
            product = mix_grad * mixing
            row_sums.append(jnp.sum(product, axis=0, keepdims=True))
            found = jnp.where(lane == j, jnp.sum(product, axis=1, keepdims=True), found)
            own = began[:, k * N : (k + 1) * N]
            out_grad = out_grad + own * cols[:, PER + j : PER + j + 1]
            found = jnp.where(
                lane == PER + j, jnp.sum(own * out_float, axis=1, keepdims=True), found
            )
        sig_grad_ref[:, at] = sig_grad
    sig_float = sig_ref[...].astype(F32)
    cot_float = cot_ref[...].astype(F32)
    own = jnp.where(
        lax.broadcasted_iota(jnp.int32, (PER, WIDE), 1) // D
        == lax.broadcasted_iota(jnp.int32, (PER, WIDE), 0),
        1.0,
        0.0,
    )
    skip = jnp.sum(own * column_of(skip_ref[...], head, PER), axis=0, keepdims=True)
    sig_grad_ref[...] = sig_grad_ref[...] + skip * cot_float
    sig_high_ref[...], sig_low_ref[...] = split(sig_float * spread(carry), 2)
    high, low = split(score_grad, 2)
    in_grad_ref[...] = mm(high, out_map) + mm(low, out_map)
    out_grad_ref[...] = out_grad + (mm_tn(high, in_map) + mm_tn(low, in_map))
    found = jnp.transpose(found)
    col_sum = found[:PER]
    from_start = found[PER : 2 * PER]
    cumul_grad = jnp.concatenate(row_sums, axis=0) - col_sum + entry * from_start
    rate_grad = rows_times_mask(cumul_grad, mask_of(lambda i, j: i >= j))
    step_grad = col_sum / step - rate_grad * decay
    step_grad_ref[...] = step_grad
    into_decay = (final - cumul) * carry
    into_bias = leave * (slope - decay * step * later)
    start = start_ref[...].astype(F32).reshape(PER, D, N)
    for rows, weight, ref in (
        (into_decay, final * total, by_decay_ref),
        (into_bias, -decay * total * jnp.sum(slope, axis=1, keepdims=True), by_bias_ref),
    ):
        high, low = split(sig_float * spread(rows), 2)
        grown = mm_tn(high, in_map) + mm_tn(low, in_map)
        ref[...] = grown + (start * weight[:, :, None]).reshape(WIDE, N)
    skip_sum = jnp.sum(
        own * jnp.sum(sig_float * cot_float, axis=0, keepdims=True), axis=1, keepdims=True
    )
    decay_sum = -decay * jnp.sum(rate_grad * step, axis=1, keepdims=True)
    bias_sum = jnp.sum(step_grad * slope, axis=1, keepdims=True)
    which = lax.broadcasted_iota(jnp.int32, (PER, N), 1)
    sums = jnp.zeros((PER, N), F32)
    for k, column in enumerate((decay_sum, bias_sum, skip_sum, total, decay)):
        sums = jnp.where(which == k, column, sums)
    sums_ref[...] = sums


def sums_kernel(end_ref, by_decay_ref, by_bias_ref, sums_ref, sent_ref, kept):
    step = pl.program_id(0)
    heads = sums_ref.shape[0]
    end = end_ref[...]
    which = lax.broadcasted_iota(jnp.int32, (heads, N), 1)
    sums = sums_ref[...]
    for k, ref in enumerate((by_decay_ref, by_bias_ref)):
        partial = jnp.sum((end * ref[...]).reshape(heads, D, N), axis=1)
        sums = sums + jnp.where(which == k, jnp.sum(partial, axis=1, keepdims=True), 0.0)

    @pl.when(step == 0)
    def _():
        kept[...] = jnp.zeros_like(kept)

    kept[pl.ds(pl.multiple_of(step * heads, heads), heads), :] = sums

    @pl.when(step == pl.num_programs(0) - 1)
    def _():
        rows = jnp.transpose(kept[...])[:8]
        sent_ref[...] = jnp.broadcast_to(rows[None], sent_ref.shape)


def relay_kernel(received_ref, after_ref, sent_ref):
    summed = jnp.sum(received_ref[...], axis=0)
    sent_ref[...] = jnp.broadcast_to(summed[None], sent_ref.shape)


def signal_kernel(
    end_ref,
    sig_ref,
    in_ref,
    start_ref,
    sums_ref,
    carry_ref,
    leave_ref,
    slope_ref,
    sig_part_ref,
    step_part_ref,
    sig_grad_ref,
    step_grad_ref,
):
    own = jnp.where(
        lax.broadcasted_iota(jnp.int32, (PER, WIDE), 1) // D
        == lax.broadcasted_iota(jnp.int32, (PER, WIDE), 0),
        1.0,
        0.0,
    ).astype(BF16)
    earlier = mask_of(lambda i, j: i < j)
    for k in range(AT_ONCE):
        wide = slice(k * WIDE, (k + 1) * WIDE)
        head = slice(k * PER, (k + 1) * PER)
        end = end_ref[wide, :]
        in_map = in_ref[:, k * N : (k + 1) * N]
        carry = carry_ref[head, :]
        total = sums_ref[head, 3:4]
        decay = sums_ref[head, 4:5]
        end_high, end_low = split(end, 2)
        end_in = mm_nt(in_map, end_high) + mm_nt(in_map, end_low)
        sig_grad_ref[:, wide] = sig_part_ref[:, wide] + spread(carry) * end_in
        high, low = split(sig_ref[:, wide].astype(F32) * end_in, 2)
        pushed = mm_nt(own, high) + mm_nt(own, low)
        before = rows_times_mask(carry * pushed, earlier)
        held = jnp.sum((end * start_ref[wide, :].astype(F32)).reshape(PER, D, N), axis=1)
        held = total * jnp.sum(held, axis=1, keepdims=True)
        step_grad = step_part_ref[head, :] + leave_ref[head, :] * pushed - decay * (before + held)
        step_grad_ref[head, :] = step_grad * slope_ref[head, :]


def input_kernel(end_ref, sig_high_ref, sig_low_ref, in_part_ref, after_ref, in_grad_ref):
    for k in range(AT_ONCE):
        wide = slice(k * WIDE, (k + 1) * WIDE)
        cols = slice(k * N, (k + 1) * N)
        end_high, end_low = split(end_ref[wide, :], 2)
        high = sig_high_ref[:, wide]
        in_grad_ref[:, cols] = in_part_ref[:, cols] + (
            mm(high, end_high) + (mm(high, end_low) + mm(sig_low_ref[:, wide], end_high))
        )


def call(kernel, grid, ins, outs, args, flops, mib, scratch=()):
    moved = sum(a.size * a.dtype.itemsize for a in args)
    moved += sum(math.prod(s.shape) * s.dtype.itemsize for _, s in outs)
    return pl.pallas_call(
        kernel,
        grid=(grid,),
        in_specs=ins,
        out_specs=[spec for spec, _ in outs],
        out_shape=[shape for _, shape in outs],
        scratch_shapes=list(scratch),
        compiler_params=pltpu.CompilerParams(
            dimension_semantics=("arbitrary",), vmem_limit_bytes=mib * MIB
        ),
        cost_estimate=pl.CostEstimate(flops=flops, bytes_accessed=moved, transcendentals=0),
    )(*args)


def far(*arrays):
    return [pltpu.with_memory_space_constraint(a, pltpu.HBM) for a in arrays]


def near(*arrays):
    return [pltpu.with_memory_space_constraint(a, pltpu.VMEM) for a in arrays]


def f32(*shape):
    return pltpu.HBM(shape, F32)


def f32_near(*shape):
    return pltpu.VMEM(shape, F32)


WIDE_COLS = pl.BlockSpec((T, WIDE), lambda g: (0, g))
MAP_COLS = pl.BlockSpec((T, N), lambda g: (0, g))
HEAD_ROWS = pl.BlockSpec((PER, T), lambda g: (g, 0))
HEAD_LANES = pl.BlockSpec((PER, N), lambda g: (g, 0))
HEAD_ALL = pl.BlockSpec((1, H), lambda g: (0, 0))
HALF_ROWS = pl.BlockSpec((H * D // 2, N), lambda g: (g, 0))
STATE_ROWS = pl.BlockSpec((WIDE, N), lambda g: (g, 0))


def many(rows, cols):
    if rows == T:
        return pl.BlockSpec((rows, AT_ONCE * cols), lambda g: (0, g))
    return pl.BlockSpec((AT_ONCE * rows, cols), lambda g: (g, 0))


ELSEWHERE = pl.BlockSpec(memory_space=pl.ANY)


def local(
    signal, cotangent, input_map, output_map, step_raw, decay_log, step_bias, skip_gain, checkpoints
):
    sig, cot, in_map, out_map, raw = (
        signal[0],
        cotangent[0],
        input_map[0],
        output_map[0],
        step_raw[0],
    )
    decay_row, bias_row, skip_row = decay_log[None], step_bias[None], skip_gain[None]
    start = checkpoints.reshape(H * D, N)
    blocks = lax.axis_size("ctx")
    rows = H * D // blocks
    own = H // blocks

    sent = call(
        state_kernel,
        G // AT_ONCE,
        [
            pl.BlockSpec((T, AT_ONCE * WIDE), lambda g: (0, g)),
            pl.BlockSpec((T, AT_ONCE * N), lambda g: (0, g)),
            pl.BlockSpec((H, T), lambda g: (0, 0)),
            HEAD_ALL,
            HEAD_ALL,
        ],
        [
            (
                pl.BlockSpec((AT_ONCE * blocks // G, rows + 8, N), lambda g: (g, 0, 0)),
                f32(blocks, rows + 8, N),
            )
        ],
        far(cot, out_map, raw, decay_row, bias_row),
        4 * H * D * N * T,
        60,
        [pltpu.VMEM((H, T), F32)],
    )[0]
    states = lax.all_to_all(sent, "ctx", 0, 0)
    ends = call(
        scan_kernel,
        own,
        [
            pl.BlockSpec((blocks, D, N), lambda i: (0, i, 0)),
            pl.BlockSpec((blocks, 8, N), lambda i: (0, rows // 8, 0)),
        ],
        [(pl.BlockSpec((blocks, D, N), lambda i: (0, i, 0)), f32(blocks, rows, N))],
        (states, states),
        2 * H * D * N,
        16,
    )[0]
    end = lax.all_to_all(ends, "ctx", 0, 0).reshape(H * D, N)

    (
        sig_part,
        in_part,
        out_grad,
        step_part,
        by_decay,
        by_bias,
        sums,
        carry,
        leave,
        slope,
        sig_high,
        sig_low,
    ) = call(
        inner_kernel,
        G,
        [
            WIDE_COLS,
            WIDE_COLS,
            MAP_COLS,
            MAP_COLS,
            HEAD_ROWS,
            HEAD_ALL,
            HEAD_ALL,
            HEAD_ALL,
            STATE_ROWS,
        ],
        [
            (WIDE_COLS, f32(T, H * D)),
            (MAP_COLS, f32(T, G * N)),
            (MAP_COLS, f32(T, G * N)),
            (HEAD_ROWS, f32_near(H, T)),
            (STATE_ROWS, f32(H * D, N)),
            (STATE_ROWS, f32(H * D, N)),
            (HEAD_LANES, f32_near(H, N)),
            (HEAD_ROWS, f32_near(H, T)),
            (HEAD_ROWS, f32_near(H, T)),
            (HEAD_ROWS, f32_near(H, T)),
            (WIDE_COLS, pltpu.HBM((T, H * D), BF16)),
            (WIDE_COLS, pltpu.HBM((T, H * D), BF16)),
        ],
        far(sig, cot, in_map, out_map, raw, decay_row, bias_row, skip_row, start),
        H * T * T * N * 20,
        24,
    )

    sent = call(
        sums_kernel,
        2,
        [HALF_ROWS, HALF_ROWS, HALF_ROWS, pl.BlockSpec((H // 2, N), lambda g: (g, 0))],
        [(pl.BlockSpec((blocks, 8, N), lambda g: (0, 0, 0)), f32(blocks, 8, N))],
        near(end) + far(by_decay, by_bias) + near(sums),
        4 * H * D * N,
        24,
        [pltpu.VMEM((N, N), F32)],
    )[0]
    received = lax.all_to_all(sent, "ctx", 0, 0)
    sig_grad, step_grad = call(
        signal_kernel,
        G // AT_ONCE,
        [
            many(WIDE, N),
            many(T, WIDE),
            many(T, N),
            many(WIDE, N),
            many(PER, N),
            many(PER, T),
            many(PER, T),
            many(PER, T),
            many(T, WIDE),
            many(PER, T),
        ],
        [(many(T, WIDE), f32(T, H * D)), (many(PER, T), f32(H, T))],
        near(end)
        + far(sig, in_map, start)
        + near(sums, carry, leave, slope)
        + far(sig_part)
        + near(step_part),
        8 * H * D * N * T,
        32,
    )
    deals = lax.axis_size("dp")
    sent = call(
        relay_kernel,
        1,
        [pl.BlockSpec((blocks, 8, N), lambda i: (0, 0, 0)), ELSEWHERE],
        [(pl.BlockSpec((deals, 8, N), lambda i: (0, 0, 0)), f32(deals, 8, N))],
        [received] + far(step_grad),
        blocks * 8 * N,
        16,
    )[0]
    summed = jnp.sum(lax.all_to_all(sent, "dp", 0, 0), axis=0)
    summed = summed * (1.0 / (deals * blocks * T))
    in_grad = call(
        input_kernel,
        G // AT_ONCE,
        [many(WIDE, N), many(T, WIDE), many(T, WIDE), many(T, N), ELSEWHERE],
        [(many(T, N), f32(T, G * N))],
        near(end) + far(sig_high, sig_low, in_part, sent),
        6 * H * D * N * T,
        32,
    )[0]
    return (
        sig_grad[None],
        in_grad[None],
        out_grad[None],
        step_grad[None],
        summed[0, :H],
        summed[2, :H],
        summed[1, :H],
    )


def solution(mesh):
    rows = P("dp", "ctx", None)
    placed = (rows, rows, rows, rows, P("dp", None, "ctx"), P(), P(), P())
    return jax.shard_map(
        local,
        mesh=mesh,
        in_specs=placed + (P("dp", "ctx", None, None, None),),
        out_specs=(rows, rows, rows, P("dp", None, "ctx"), P(), P(), P()),
        check_vma=False,
    )
```

```python
import math

import jax
import jax.numpy as jnp
from jax import lax
from jax.experimental import pallas as pl
from jax.experimental.pallas import tpu as pltpu
from jax.sharding import PartitionSpec as P

T = 256
H = 64
G = 8
D = 64
N = 128
PER = H // G
WIDE = PER * D
F32 = jnp.float32
BF16 = jnp.bfloat16
MIB = 1024 * 1024
STATE_BATCH = 4
SUMS_BATCH = 2
SIGNAL_BATCH = 3
INPUT_BATCH = 3


def split(x, parts):
    pieces = []
    for _ in range(parts):
        piece = x.astype(BF16)
        pieces.append(piece)
        x = x - piece.astype(F32)
    return pieces


def mm(a, b):
    return lax.dot_general(a, b, (((1,), (0,)), ((), ())), preferred_element_type=F32)


def mm_nt(a, b):
    return lax.dot_general(a, b, (((1,), (1,)), ((), ())), preferred_element_type=F32)


def mm_tn(a, b):
    return lax.dot_general(a, b, (((0,), (0,)), ((), ())), preferred_element_type=F32)


def rows_times_mask(rows, mask):
    n = rows.shape[0]
    out = mm(jnp.concatenate(split(rows, 3), axis=0), mask)
    return out[:n] + out[n : 2 * n] + out[2 * n :]


def mask_of(relation):
    i = lax.broadcasted_iota(jnp.int32, (T, T), 0)
    j = lax.broadcasted_iota(jnp.int32, (T, T), 1)
    return jnp.where(relation(i, j), 1.0, 0.0).astype(BF16)


def column_of(row, first, count):
    i = lax.broadcasted_iota(jnp.int32, (count, H), 0) + first
    j = lax.broadcasted_iota(jnp.int32, (count, H), 1)
    return jnp.sum(jnp.where(i == j, row, 0.0), axis=1, keepdims=True)


def steps_of(raw, bias, decay_log):
    pre_act = raw + bias
    step = jnp.maximum(pre_act, 0.0) + jnp.log1p(jnp.exp(-jnp.abs(pre_act)))
    decay = jnp.exp(decay_log)
    rate = -decay * step
    cumul = rows_times_mask(rate, mask_of(lambda i, j: i <= j))
    return pre_act, step, decay, cumul


def spread(rows):
    head = lax.broadcasted_iota(jnp.int32, (PER, WIDE), 0)
    column = lax.broadcasted_iota(jnp.int32, (PER, WIDE), 1)
    own = jnp.where(column // D == head, 1.0, 0.0).astype(BF16)
    return mm_tn(jnp.concatenate(split(rows, 3), axis=0), jnp.concatenate([own] * 3, axis=0))


def columns(rows):
    pad = jnp.zeros((128 - PER * len(rows), T), F32)
    return jnp.transpose(jnp.concatenate(list(rows) + [pad], axis=0))


def fetch(sems, pairs):
    copies = [pltpu.make_async_copy(a, b, sems.at[k]) for k, (a, b) in enumerate(pairs)]
    for copy in copies:
        copy.start()
    return copies


def batches(size):
    return [range(g, min(g + size, G)) for g in range(0, G, size)]


def wide(g):
    return pl.ds(g * WIDE, WIDE)


def narrow(g):
    return pl.ds(g * N, N)


def state_kernel(
    cot_ref,
    out_ref,
    raw_ref,
    decay_ref,
    bias_ref,
    sent_ref,
    cot,
    out,
    raw,
    decay,
    bias,
    got,
):
    half = WIDE // 2
    pairs = [(raw_ref, raw), (decay_ref, decay), (bias_ref, bias)]
    for g in range(G):
        pairs.append((cot_ref.at[:, wide(g)], cot.at[:, wide(g)]))
        pairs.append((out_ref.at[:, narrow(g)], out.at[:, narrow(g)]))
    copies = fetch(got, pairs)
    for copy in copies[:3]:
        copy.wait()
    bias_column = column_of(bias[...], 0, H)
    decay_log = column_of(decay[...], 0, H)
    entries = jnp.exp(steps_of(raw[...], bias_column, decay_log)[3])
    for batch in batches(STATE_BATCH):
        for g in batch:
            copies[2 * g + 3].wait()
            copies[2 * g + 4].wait()
        for g in batch:
            entry = entries[g * PER : (g + 1) * PER]
            turned = jnp.transpose(cot[:, wide(g)]).astype(F32)
            weighted = (turned.reshape(PER, D, T) * entry[:, None, :]).reshape(WIDE, T)
            out_map = out[:, narrow(g)]
            high, low = split(weighted, 2)
            state = mm(high, out_map) + mm(low, out_map)
            total = jnp.broadcast_to(entry[:, T - 1 :], (PER, N))
            sent_ref[2 * g, :half] = state[:half]
            sent_ref[2 * g + 1, :half] = state[half:]
            sent_ref[2 * g, half:] = total
            sent_ref[2 * g + 1, half:] = jnp.concatenate(
                [total[PER // 2 :], total[: PER // 2]], axis=0
            )


def scan_kernel(state_ref, end_ref, end, gone):
    blocks, rows, _ = end.shape
    leaving = []
    for h in range(rows // D):
        at = pl.ds(h * D, D)
        carry = jnp.zeros((D, N), F32)
        for b in reversed(range(blocks)):
            end[b, at, :] = carry
            carry = state_ref[b, at, :] + state_ref[b, rows + h : rows + h + 1, :] * carry
        leaving.append(pltpu.make_async_copy(end.at[:, at], end_ref.at[:, at], gone.at[h]))
        leaving[-1].start()
    for copy in leaving:
        copy.wait()


def inner_kernel(
    sig_ref,
    cot_ref,
    in_ref,
    out_ref,
    raw_ref,
    decay_ref,
    bias_ref,
    skip_ref,
    start_ref,
    sig_grad_ref,
    in_grad_ref,
    out_grad_ref,
    step_grad_ref,
    by_decay_ref,
    by_bias_ref,
    sums_ref,
    carry_ref,
    leave_ref,
    slope_ref,
    sig_high_ref,
    sig_low_ref,
    sig_turned_ref,
):
    head = pl.program_id(0) * PER
    bias = column_of(bias_ref[...], head, PER)
    decay_log = column_of(decay_ref[...], head, PER)
    pre_act, step, decay, cumul = steps_of(raw_ref[...], bias, decay_log)
    slope = jax.nn.sigmoid(pre_act)
    entry = jnp.exp(cumul)
    final = cumul[:, T - 1 :]
    total = jnp.exp(final)
    leave = jnp.exp(final - cumul)
    carry = leave * step
    carry_ref[...] = carry
    leave_ref[...] = leave
    slope_ref[...] = slope
    later = rows_times_mask(slope, mask_of(lambda i, j: i > j))
    cols = columns([cumul - jnp.log(step), entry])
    in_map = in_ref[...]
    out_map = out_ref[...]
    out_float = out_map.astype(F32)
    scores = mm_nt(in_map, out_map)
    valid = lax.broadcasted_iota(jnp.int32, (T, T), 0) <= lax.broadcasted_iota(jnp.int32, (T, T), 1)
    lane = lax.broadcasted_iota(jnp.int32, (T, N), 1)
    first = lane < D
    score_grad = jnp.zeros((T, T), F32)
    out_grad = jnp.zeros((T, N), F32)
    found = jnp.zeros((T, N), F32)
    row_sums = []
    for pair in range(PER // 2):
        at = slice(pair * N, (pair + 1) * N)
        sig = sig_ref[:, at]
        cot = cot_ref[:, at]
        zero = jnp.zeros_like(sig)
        sig_grad = jnp.zeros((T, N), F32)
        start = start_ref[at, :]
        top = lax.broadcasted_iota(jnp.int32, (N, N), 0) < D
        none = jnp.zeros_like(start)
        both = jnp.concatenate(
            [jnp.where(top, start, none), jnp.where(top, none, start)], axis=1
        )
        began = mm(cot, both)
        for k in range(2):
            j = 2 * pair + k
            mine = first if k == 0 else jnp.logical_not(first)
            own_sig = jnp.where(mine, sig, zero)
            own_cot = jnp.where(mine, cot, zero)
            mix_grad = mm_nt(own_sig, cot)
            fade = jnp.where(valid, jnp.exp(cumul[j : j + 1, :] - cols[:, j : j + 1]), 0.0)
            mixing = fade * scores
            high, low = split(mixing, 2)
            sig_grad = sig_grad + (mm(high, own_cot) + mm(low, own_cot))
            score_grad = score_grad + mix_grad * fade
            product = mix_grad * mixing
            row_sums.append(jnp.sum(product, axis=0, keepdims=True))
            found = jnp.where(lane == j, jnp.sum(product, axis=1, keepdims=True), found)
            own = began[:, k * N : (k + 1) * N]
            out_grad = out_grad + own * cols[:, PER + j : PER + j + 1]
            found = jnp.where(
                lane == PER + j, jnp.sum(own * out_float, axis=1, keepdims=True), found
            )
        sig_grad_ref[:, at] = sig_grad
    sig_float = sig_ref[...].astype(F32)
    cot_float = cot_ref[...].astype(F32)
    own = jnp.where(
        lax.broadcasted_iota(jnp.int32, (PER, WIDE), 1) // D
        == lax.broadcasted_iota(jnp.int32, (PER, WIDE), 0),
        1.0,
        0.0,
    )
    skip = jnp.sum(own * column_of(skip_ref[...], head, PER), axis=0, keepdims=True)
    sig_grad_ref[...] = sig_grad_ref[...] + skip * cot_float
    sig_turned_ref[...] = jnp.transpose(sig_ref[...])
    sig_high_ref[...], sig_low_ref[...] = split(sig_float * spread(carry), 2)
    high, low = split(score_grad, 2)
    in_grad_ref[...] = mm(high, out_map) + mm(low, out_map)
    out_grad_ref[...] = out_grad + (mm_tn(high, in_map) + mm_tn(low, in_map))
    found = jnp.transpose(found)
    col_sum = found[:PER]
    from_start = found[PER : 2 * PER]
    cumul_grad = jnp.concatenate(row_sums, axis=0) - col_sum + entry * from_start
    rate_grad = rows_times_mask(cumul_grad, mask_of(lambda i, j: i >= j))
    step_grad = col_sum / step - rate_grad * decay
    step_grad_ref[...] = step_grad
    into_decay = (final - cumul) * carry
    into_bias = leave * (slope - decay * step * later)
    start = start_ref[...].astype(F32).reshape(PER, D, N)
    for rows, weight, ref in (
        (into_decay, final * total, by_decay_ref),
        (into_bias, -decay * total * jnp.sum(slope, axis=1, keepdims=True), by_bias_ref),
    ):
        high, low = split(sig_float * spread(rows), 2)
        grown = mm_tn(high, in_map) + mm_tn(low, in_map)
        ref[...] = grown + (start * weight[:, :, None]).reshape(WIDE, N)
    skip_sum = jnp.sum(
        own * jnp.sum(sig_float * cot_float, axis=0, keepdims=True), axis=1, keepdims=True
    )
    decay_sum = -decay * jnp.sum(rate_grad * step, axis=1, keepdims=True)
    bias_sum = jnp.sum(step_grad * slope, axis=1, keepdims=True)
    which = lax.broadcasted_iota(jnp.int32, (PER, N), 1)
    sums = jnp.zeros((PER, N), F32)
    for k, column in enumerate((decay_sum, bias_sum, skip_sum, total, decay)):
        sums = jnp.where(which == k, column, sums)
    sums_ref[...] = sums


def sums_kernel(
    end_ref, sums_ref, by_decay_ref, by_bias_ref, sent_ref, by_decay, by_bias, kept, got
):
    pairs = []
    for g in range(0, G, SUMS_BATCH):
        at = pl.ds(g * WIDE, SUMS_BATCH * WIDE)
        pairs.append((by_decay_ref.at[at], by_decay.at[at]))
        pairs.append((by_bias_ref.at[at], by_bias.at[at]))
    copies = fetch(got, pairs)
    which = lax.broadcasted_iota(jnp.int32, (PER, N), 1)
    kept[...] = jnp.zeros_like(kept)
    for g in range(G):
        if g % SUMS_BATCH == 0:
            copies[2 * (g // SUMS_BATCH)].wait()
            copies[2 * (g // SUMS_BATCH) + 1].wait()
        end = end_ref[wide(g), :]
        sums = sums_ref[g * PER : (g + 1) * PER, :]
        for k, held in enumerate((by_decay, by_bias)):
            partial = jnp.sum((end * held[wide(g), :]).reshape(PER, D, N), axis=1)
            sums = sums + jnp.where(which == k, jnp.sum(partial, axis=1, keepdims=True), 0.0)
        kept[g * PER : (g + 1) * PER, :] = sums
    rows = jnp.transpose(kept[...])
    first = jnp.concatenate([rows[0:1, :H], rows[1:2, :H]], axis=1)
    odd = lax.broadcasted_iota(jnp.int32, (8, N), 0) % 2 == 1
    both = jnp.where(odd, rows[2:3], first)
    sent_ref[...] = jnp.broadcast_to(both[None], sent_ref.shape)


def signal_kernel(
    end_ref,
    sums_ref,
    carry_ref,
    leave_ref,
    slope_ref,
    step_part_ref,
    sig_turned_ref,
    in_ref,
    start_ref,
    sig_part_ref,
    step_grad_ref,
    sig_grad_ref,
    sig_turned,
    in_maps,
    start,
    sig_part,
    sig_grad,
    step_grads,
    got,
    gone,
):
    pairs = []
    for g in range(G):
        pairs.append((in_ref.at[:, narrow(g)], in_maps.at[:, narrow(g)]))
        pairs.append((sig_turned_ref.at[wide(g)], sig_turned.at[wide(g)]))
        pairs.append((start_ref.at[wide(g)], start.at[wide(g)]))
        pairs.append((sig_part_ref.at[:, wide(g)], sig_part.at[:, wide(g)]))
    copies = fetch(got, pairs)
    earlier = mask_of(lambda i, j: i < j)
    leaving = []
    for batch in batches(SIGNAL_BATCH):
        for g in batch:
            for copy in copies[4 * g : 4 * g + 4]:
                copy.wait()
        for g in batch:
            head = slice(g * PER, (g + 1) * PER)
            end = end_ref[wide(g), :]
            in_map = in_maps[:, narrow(g)]
            carry = carry_ref[head, :]
            total = sums_ref[head, 3:4]
            decay = sums_ref[head, 4:5]
            in_twice = jnp.concatenate([in_map, in_map], axis=1)
            pieces = jnp.concatenate(split(end, 2), axis=1)
            sig_grad[:, wide(g)] = sig_part[:, wide(g)] + spread(carry) * mm_nt(in_twice, pieces)
            turned = mm_nt(pieces, in_twice)
            pushed = (sig_turned[wide(g), :].astype(F32) * turned).reshape(PER, D, T)
            pushed = jnp.sum(pushed, axis=1)
            before = rows_times_mask(carry * pushed, earlier)
            held = jnp.sum((end * start[wide(g), :].astype(F32)).reshape(PER, D, N), axis=1)
            held = total * jnp.sum(held, axis=1, keepdims=True)
            step_grad = leave_ref[head, :] * pushed - decay * (before + held)
            step_grads[head, :] = (step_part_ref[head, :] + step_grad) * slope_ref[head, :]
        at = pl.ds(batch[0] * WIDE, len(batch) * WIDE)
        leaving.append(
            pltpu.make_async_copy(sig_grad.at[:, at], sig_grad_ref.at[:, at], gone.at[batch[0]])
        )
        leaving[-1].start()
    leaving.append(pltpu.make_async_copy(step_grads, step_grad_ref, gone.at[G]))
    leaving[-1].start()
    for copy in leaving:
        copy.wait()


def input_kernel(
    end_ref,
    sig_high_ref,
    sig_low_ref,
    in_part_ref,
    in_grad_ref,
    sig_high,
    sig_low,
    in_part,
    in_grad,
    got,
    gone,
):
    pairs = []
    for g in range(G):
        pairs.append((sig_high_ref.at[:, wide(g)], sig_high.at[:, wide(g)]))
        pairs.append((sig_low_ref.at[:, wide(g)], sig_low.at[:, wide(g)]))
        pairs.append((in_part_ref.at[:, narrow(g)], in_part.at[:, narrow(g)]))
    copies = fetch(got, pairs)
    leaving = []
    for batch in batches(INPUT_BATCH):
        for g in batch:
            for copy in copies[3 * g : 3 * g + 3]:
                copy.wait()
        for g in batch:
            end_high, end_low = split(end_ref[wide(g), :], 2)
            both = mm(sig_high[:, wide(g)], jnp.concatenate([end_high, end_low], axis=1))
            in_grad[:, narrow(g)] = in_part[:, narrow(g)] + (
                both[:, :N] + (both[:, N:] + mm(sig_low[:, wide(g)], end_high))
            )
        at = pl.ds(batch[0] * N, len(batch) * N)
        leaving.append(
            pltpu.make_async_copy(in_grad.at[:, at], in_grad_ref.at[:, at], gone.at[batch[0]])
        )
        leaving[-1].start()
    for copy in leaving:
        copy.wait()


def call(kernel, grid, ins, outs, args, flops, mib, scratch=()):
    moved = sum(a.size * a.dtype.itemsize for a in args)
    moved += sum(math.prod(s.shape) * s.dtype.itemsize for _, s in outs)
    return pl.pallas_call(
        kernel,
        grid=(grid,) if grid else (),
        in_specs=ins,
        out_specs=[spec for spec, _ in outs],
        out_shape=[shape for _, shape in outs],
        scratch_shapes=list(scratch),
        compiler_params=pltpu.CompilerParams(
            dimension_semantics=("arbitrary",) if grid else None, vmem_limit_bytes=mib * MIB
        ),
        cost_estimate=pl.CostEstimate(flops=flops, bytes_accessed=moved, transcendentals=0),
    )(*args)


def far(*arrays):
    return [pltpu.with_memory_space_constraint(a, pltpu.HBM) for a in arrays]


def near(*arrays):
    return [pltpu.with_memory_space_constraint(a, pltpu.VMEM) for a in arrays]


def f32(*shape):
    return pltpu.HBM(shape, F32)


def bf16(*shape):
    return pltpu.HBM(shape, BF16)


def f32_near(*shape):
    return pltpu.VMEM(shape, F32)


WIDE_COLS = pl.BlockSpec((T, WIDE), lambda g: (0, g))
MAP_COLS = pl.BlockSpec((T, N), lambda g: (0, g))
HEAD_ROWS = pl.BlockSpec((PER, T), lambda g: (g, 0))
HEAD_LANES = pl.BlockSpec((PER, N), lambda g: (g, 0))
HEAD_ALL = pl.BlockSpec((1, H), lambda g: (0, 0))
STATE_COLS = pl.BlockSpec((WIDE, T), lambda g: (g, 0))
STATE_ROWS = pl.BlockSpec((WIDE, N), lambda g: (g, 0))


ELSEWHERE = pl.BlockSpec(memory_space=pl.ANY)
HERE = pl.BlockSpec(memory_space=pltpu.VMEM)
COPIES = pltpu.SemaphoreType.DMA


def send_states(cot, out_map, raw, decay_row, bias_row, blocks):
    rows = H * D // blocks + 8
    return call(
        state_kernel,
        0,
        [ELSEWHERE] * 5,
        [(HERE, f32_near(blocks, rows, N))],
        far(cot, out_map, raw, decay_row, bias_row),
        4 * H * D * N * T,
        24,
        [
            pltpu.VMEM((T, H * D), BF16),
            pltpu.VMEM((T, G * N), BF16),
            pltpu.VMEM((H, T), F32),
            pltpu.VMEM((1, H), F32),
            pltpu.VMEM((1, H), F32),
            COPIES((2 * G + 3,)),
        ],
    )[0]


def scan_states(states):
    blocks, rows, _ = states.shape
    rows -= 8
    return call(
        scan_kernel,
        0,
        [HERE],
        [(ELSEWHERE, f32(blocks, rows, N))],
        near(states),
        2 * H * D * N,
        16,
        [pltpu.VMEM((blocks, rows, N), F32), COPIES((rows // D,))],
    )[0]


def inner_part(sig, cot, in_map, out_map, raw, decay_row, bias_row, skip_row, start):
    return call(
        inner_kernel,
        G,
        [
            WIDE_COLS,
            WIDE_COLS,
            MAP_COLS,
            MAP_COLS,
            HEAD_ROWS,
            HEAD_ALL,
            HEAD_ALL,
            HEAD_ALL,
            STATE_ROWS,
        ],
        [
            (WIDE_COLS, f32(T, H * D)),
            (MAP_COLS, f32(T, G * N)),
            (MAP_COLS, f32(T, G * N)),
            (HEAD_ROWS, f32_near(H, T)),
            (STATE_ROWS, f32(H * D, N)),
            (STATE_ROWS, f32(H * D, N)),
            (HEAD_LANES, f32_near(H, N)),
            (HEAD_ROWS, f32_near(H, T)),
            (HEAD_ROWS, f32_near(H, T)),
            (HEAD_ROWS, f32_near(H, T)),
            (WIDE_COLS, bf16(T, H * D)),
            (WIDE_COLS, bf16(T, H * D)),
            (STATE_COLS, bf16(H * D, T)),
        ],
        far(sig, cot, in_map, out_map, raw, decay_row, bias_row, skip_row, start),
        H * T * T * N * 20,
        24,
    )


def send_sums(end, by_decay, by_bias, sums, devices):
    return call(
        sums_kernel,
        0,
        [HERE, HERE, ELSEWHERE, ELSEWHERE],
        [(HERE, f32_near(devices // 4, 8, N))],
        near(end, sums) + far(by_decay, by_bias),
        4 * H * D * N,
        16,
        [
            pltpu.VMEM((H * D, N), F32),
            pltpu.VMEM((H * D, N), F32),
            pltpu.VMEM((N, N), F32),
            COPIES((2 * (G // SUMS_BATCH),)),
        ],
    )[0].reshape(devices, 2, N)


def signal_part(end, sig_turned, in_map, start, sums, carry, leave, slope, sig_part, step_part):
    step_grad, sig_grad = call(
        signal_kernel,
        0,
        [HERE] * 6 + [ELSEWHERE] * 4,
        [(ELSEWHERE, f32(H, T)), (ELSEWHERE, f32(T, H * D))],
        near(end, sums, carry, leave, slope, step_part) + far(sig_turned, in_map, start, sig_part),
        8 * H * D * N * T,
        28,
        [
            pltpu.VMEM((H * D, T), BF16),
            pltpu.VMEM((T, G * N), BF16),
            pltpu.VMEM((H * D, N), BF16),
            pltpu.VMEM((T, H * D), F32),
            pltpu.VMEM((T, H * D), F32),
            pltpu.VMEM((H, T), F32),
            COPIES((4 * G,)),
            COPIES((G + 1,)),
        ],
    )
    return sig_grad, step_grad


def input_part(end, sig_high, sig_low, in_part):
    return call(
        input_kernel,
        0,
        [HERE] + [ELSEWHERE] * 3,
        [(ELSEWHERE, f32(T, G * N))],
        near(end) + far(sig_high, sig_low, in_part),
        6 * H * D * N * T,
        20,
        [
            pltpu.VMEM((T, H * D), BF16),
            pltpu.VMEM((T, H * D), BF16),
            pltpu.VMEM((T, G * N), F32),
            pltpu.VMEM((T, G * N), F32),
            COPIES((3 * G,)),
            COPIES((G,)),
        ],
    )[0]


def local(
    signal, cotangent, input_map, output_map, step_raw, decay_log, step_bias, skip_gain, checkpoints
):
    sig, cot, in_map, out_map, raw = (
        signal[0],
        cotangent[0],
        input_map[0],
        output_map[0],
        step_raw[0],
    )
    decay_row, bias_row, skip_row = decay_log[None], step_bias[None], skip_gain[None]
    start = checkpoints.reshape(H * D, N)
    blocks, deals = lax.axis_size("ctx"), lax.axis_size("dp")

    sent = send_states(cot, out_map, raw, decay_row, bias_row, blocks)
    ends = scan_states(lax.all_to_all(sent, "ctx", 0, 0))
    end = lax.all_to_all(ends, "ctx", 0, 0).reshape(H * D, N)
    (
        sig_part,
        in_part,
        out_grad,
        step_part,
        by_decay,
        by_bias,
        sums,
        carry,
        leave,
        slope,
        sig_high,
        sig_low,
        sig_turned,
    ) = inner_part(sig, cot, in_map, out_map, raw, decay_row, bias_row, skip_row, start)

    devices = blocks * deals
    sent = send_sums(end, by_decay, by_bias, sums, devices)
    received = lax.all_to_all(sent, ("dp", "ctx"), 0, 0)
    sig_grad, step_grad = signal_part(
        end, sig_turned, in_map, start, sums, carry, leave, slope, sig_part, step_part
    )
    in_grad = input_part(end, sig_high, sig_low, in_part)
    summed = jnp.sum(received, axis=0) * (1.0 / (devices * T))
    return (
        sig_grad[None],
        in_grad[None],
        out_grad[None],
        step_grad[None],
        summed[0, :H],
        summed[1, :H],
        summed[0, H:],
    )


def solution(mesh):
    rows = P("dp", "ctx", None)
    placed = (rows, rows, rows, rows, P("dp", None, "ctx"), P(), P(), P())
    return jax.shard_map(
        local,
        mesh=mesh,
        in_specs=placed + (P("dp", "ctx", None, None, None),),
        out_specs=(rows, rows, rows, P("dp", None, "ctx"), P(), P(), P()),
        check_vma=False,
    )
```

```python
import math

import jax
import jax.numpy as jnp
from jax import lax
from jax.experimental import pallas as pl
from jax.experimental.pallas import tpu as pltpu
from jax.sharding import PartitionSpec as P

T = 256
H = 64
G = 8
D = 64
N = 128
PER = H // G
WIDE = PER * D
F32 = jnp.float32
BF16 = jnp.bfloat16
MIB = 1024 * 1024
STATE_BATCH = 4
SUMS_BATCH = 2
FINISH_BATCH = 3


def split(x, parts):
    pieces = []
    for _ in range(parts):
        piece = x.astype(BF16)
        pieces.append(piece)
        x = x - piece.astype(F32)
    return pieces


def mm(a, b):
    return lax.dot_general(a, b, (((1,), (0,)), ((), ())), preferred_element_type=F32)


def mm_nt(a, b):
    return lax.dot_general(a, b, (((1,), (1,)), ((), ())), preferred_element_type=F32)


def mm_tn(a, b):
    return lax.dot_general(a, b, (((0,), (0,)), ((), ())), preferred_element_type=F32)


def rows_times_mask(rows, mask):
    n = rows.shape[0]
    out = mm(jnp.concatenate(split(rows, 3), axis=0), mask)
    return out[:n] + out[n : 2 * n] + out[2 * n :]


def mask_of(relation):
    i = lax.broadcasted_iota(jnp.int32, (T, T), 0)
    j = lax.broadcasted_iota(jnp.int32, (T, T), 1)
    return jnp.where(relation(i, j), 1.0, 0.0).astype(BF16)


def column_of(row, first, count):
    i = lax.broadcasted_iota(jnp.int32, (count, H), 0) + first
    j = lax.broadcasted_iota(jnp.int32, (count, H), 1)
    return jnp.sum(jnp.where(i == j, row, 0.0), axis=1, keepdims=True)


def steps_of(raw, bias, decay_log):
    pre_act = raw + bias
    step = jnp.maximum(pre_act, 0.0) + jnp.log1p(jnp.exp(-jnp.abs(pre_act)))
    decay = jnp.exp(decay_log)
    rate = -decay * step
    cumul = rows_times_mask(rate, mask_of(lambda i, j: i <= j))
    return pre_act, step, decay, cumul


def spread(rows):
    head = lax.broadcasted_iota(jnp.int32, (PER, WIDE), 0)
    column = lax.broadcasted_iota(jnp.int32, (PER, WIDE), 1)
    own = jnp.where(column // D == head, 1.0, 0.0).astype(BF16)
    return mm_tn(jnp.concatenate(split(rows, 3), axis=0), jnp.concatenate([own] * 3, axis=0))


def columns(rows):
    pad = jnp.zeros((128 - PER * len(rows), T), F32)
    return jnp.transpose(jnp.concatenate(list(rows) + [pad], axis=0))


def fetch(sems, pairs):
    copies = [pltpu.make_async_copy(a, b, sems.at[k]) for k, (a, b) in enumerate(pairs)]
    for copy in copies:
        copy.start()
    return copies


def batches(size):
    return [range(g, min(g + size, G)) for g in range(0, G, size)]


def wide(g):
    return pl.ds(g * WIDE, WIDE)


def narrow(g):
    return pl.ds(g * N, N)


def state_kernel(
    cot_ref,
    out_ref,
    raw_ref,
    decay_ref,
    bias_ref,
    sent_ref,
    cot,
    out,
    raw,
    decay,
    bias,
    got,
):
    half = WIDE // 2
    pairs = [(raw_ref, raw), (decay_ref, decay), (bias_ref, bias)]
    for g in range(G):
        pairs.append((cot_ref.at[:, wide(g)], cot.at[:, wide(g)]))
        pairs.append((out_ref.at[:, narrow(g)], out.at[:, narrow(g)]))
    copies = fetch(got, pairs)
    for copy in copies[:3]:
        copy.wait()
    bias_column = column_of(bias[...], 0, H)
    decay_log = column_of(decay[...], 0, H)
    entries = jnp.exp(steps_of(raw[...], bias_column, decay_log)[3])
    for batch in batches(STATE_BATCH):
        for g in batch:
            copies[2 * g + 3].wait()
            copies[2 * g + 4].wait()
        for g in batch:
            entry = entries[g * PER : (g + 1) * PER]
            turned = jnp.transpose(cot[:, wide(g)]).astype(F32)
            weighted = (turned.reshape(PER, D, T) * entry[:, None, :]).reshape(WIDE, T)
            out_map = out[:, narrow(g)]
            high, low = split(weighted, 2)
            state = mm(high, out_map) + mm(low, out_map)
            total = jnp.broadcast_to(entry[:, T - 1 :], (PER, N))
            sent_ref[2 * g, :half] = state[:half]
            sent_ref[2 * g + 1, :half] = state[half:]
            sent_ref[2 * g, half:] = total
            sent_ref[2 * g + 1, half:] = jnp.concatenate(
                [total[PER // 2 :], total[: PER // 2]], axis=0
            )


def scan_kernel(state_ref, end_ref, end, gone):
    blocks, rows, _ = end.shape
    leaving = []
    for h in range(rows // D):
        at = pl.ds(h * D, D)
        carry = jnp.zeros((D, N), F32)
        for b in reversed(range(blocks)):
            end[b, at, :] = carry
            carry = state_ref[b, at, :] + state_ref[b, rows + h : rows + h + 1, :] * carry
        leaving.append(pltpu.make_async_copy(end.at[:, at], end_ref.at[:, at], gone.at[h]))
        leaving[-1].start()
    for copy in leaving:
        copy.wait()


def inner_kernel(
    sig_ref,
    cot_ref,
    in_ref,
    out_ref,
    raw_ref,
    decay_ref,
    bias_ref,
    skip_ref,
    start_ref,
    sig_grad_ref,
    in_grad_ref,
    out_grad_ref,
    step_grad_ref,
    by_decay_ref,
    by_bias_ref,
    sums_ref,
    carry_ref,
    leave_ref,
    slope_ref,
    sig_high_ref,
    sig_low_ref,
    sig_turned_ref,
):
    head = pl.program_id(0) * PER
    bias = column_of(bias_ref[...], head, PER)
    decay_log = column_of(decay_ref[...], head, PER)
    pre_act, step, decay, cumul = steps_of(raw_ref[...], bias, decay_log)
    slope = jax.nn.sigmoid(pre_act)
    entry = jnp.exp(cumul)
    final = cumul[:, T - 1 :]
    total = jnp.exp(final)
    leave = jnp.exp(final - cumul)
    carry = leave * step
    carry_ref[...] = carry
    leave_ref[...] = leave
    slope_ref[...] = slope
    later = rows_times_mask(slope, mask_of(lambda i, j: i > j))
    cols = columns([cumul - jnp.log(step), entry])
    in_map = in_ref[...]
    out_map = out_ref[...]
    out_float = out_map.astype(F32)
    scores = mm_nt(in_map, out_map)
    valid = lax.broadcasted_iota(jnp.int32, (T, T), 0) <= lax.broadcasted_iota(jnp.int32, (T, T), 1)
    lane = lax.broadcasted_iota(jnp.int32, (T, N), 1)
    first = lane < D
    score_grad = jnp.zeros((T, T), F32)
    out_grad = jnp.zeros((T, N), F32)
    found = jnp.zeros((T, N), F32)
    row_sums = []
    for pair in range(PER // 2):
        at = slice(pair * N, (pair + 1) * N)
        sig = sig_ref[:, at]
        cot = cot_ref[:, at]
        zero = jnp.zeros_like(sig)
        sig_grad = jnp.zeros((T, N), F32)
        start = start_ref[at, :]
        top = lax.broadcasted_iota(jnp.int32, (N, N), 0) < D
        none = jnp.zeros_like(start)
        both = jnp.concatenate(
            [jnp.where(top, start, none), jnp.where(top, none, start)], axis=1
        )
        began = mm(cot, both)
        for k in range(2):
            j = 2 * pair + k
            mine = first if k == 0 else jnp.logical_not(first)
            own_sig = jnp.where(mine, sig, zero)
            own_cot = jnp.where(mine, cot, zero)
            mix_grad = mm_nt(own_sig, cot)
            fade = jnp.where(valid, jnp.exp(cumul[j : j + 1, :] - cols[:, j : j + 1]), 0.0)
            mixing = fade * scores
            high, low = split(mixing, 2)
            sig_grad = sig_grad + (mm(high, own_cot) + mm(low, own_cot))
            score_grad = score_grad + mix_grad * fade
            product = mix_grad * mixing
            row_sums.append(jnp.sum(product, axis=0, keepdims=True))
            found = jnp.where(lane == j, jnp.sum(product, axis=1, keepdims=True), found)
            own = began[:, k * N : (k + 1) * N]
            out_grad = out_grad + own * cols[:, PER + j : PER + j + 1]
            found = jnp.where(
                lane == PER + j, jnp.sum(own * out_float, axis=1, keepdims=True), found
            )
        sig_grad_ref[:, at] = sig_grad
    sig_float = sig_ref[...].astype(F32)
    cot_float = cot_ref[...].astype(F32)
    own = jnp.where(
        lax.broadcasted_iota(jnp.int32, (PER, WIDE), 1) // D
        == lax.broadcasted_iota(jnp.int32, (PER, WIDE), 0),
        1.0,
        0.0,
    )
    skip = jnp.sum(own * column_of(skip_ref[...], head, PER), axis=0, keepdims=True)
    sig_grad_ref[...] = sig_grad_ref[...] + skip * cot_float
    sig_turned_ref[...] = jnp.transpose(sig_ref[...])
    sig_high_ref[...], sig_low_ref[...] = split(sig_float * spread(carry), 2)
    high, low = split(score_grad, 2)
    in_grad_ref[...] = mm(high, out_map) + mm(low, out_map)
    out_grad_ref[...] = out_grad + (mm_tn(high, in_map) + mm_tn(low, in_map))
    found = jnp.transpose(found)
    col_sum = found[:PER]
    from_start = found[PER : 2 * PER]
    cumul_grad = jnp.concatenate(row_sums, axis=0) - col_sum + entry * from_start
    rate_grad = rows_times_mask(cumul_grad, mask_of(lambda i, j: i >= j))
    step_grad = col_sum / step - rate_grad * decay
    step_grad_ref[...] = step_grad
    into_decay = (final - cumul) * carry
    into_bias = leave * (slope - decay * step * later)
    start = start_ref[...].astype(F32).reshape(PER, D, N)
    for rows, weight, ref in (
        (into_decay, final * total, by_decay_ref),
        (into_bias, -decay * total * jnp.sum(slope, axis=1, keepdims=True), by_bias_ref),
    ):
        high, low = split(sig_float * spread(rows), 2)
        grown = mm_tn(high, in_map) + mm_tn(low, in_map)
        ref[...] = grown + (start * weight[:, :, None]).reshape(WIDE, N)
    skip_sum = jnp.sum(
        own * jnp.sum(sig_float * cot_float, axis=0, keepdims=True), axis=1, keepdims=True
    )
    decay_sum = -decay * jnp.sum(rate_grad * step, axis=1, keepdims=True)
    bias_sum = jnp.sum(step_grad * slope, axis=1, keepdims=True)
    which = lax.broadcasted_iota(jnp.int32, (PER, N), 1)
    sums = jnp.zeros((PER, N), F32)
    for k, column in enumerate((decay_sum, bias_sum, skip_sum, total, decay)):
        sums = jnp.where(which == k, column, sums)
    sums_ref[...] = sums


def sums_kernel(
    end_ref, sums_ref, by_decay_ref, by_bias_ref, sent_ref, by_decay, by_bias, kept, got
):
    pairs = []
    for g in range(0, G, SUMS_BATCH):
        at = pl.ds(g * WIDE, SUMS_BATCH * WIDE)
        pairs.append((by_decay_ref.at[at], by_decay.at[at]))
        pairs.append((by_bias_ref.at[at], by_bias.at[at]))
    copies = fetch(got, pairs)
    which = lax.broadcasted_iota(jnp.int32, (PER, N), 1)
    kept[...] = jnp.zeros_like(kept)
    for g in range(G):
        if g % SUMS_BATCH == 0:
            copies[2 * (g // SUMS_BATCH)].wait()
            copies[2 * (g // SUMS_BATCH) + 1].wait()
        end = end_ref[wide(g), :]
        sums = sums_ref[g * PER : (g + 1) * PER, :]
        for k, held in enumerate((by_decay, by_bias)):
            partial = jnp.sum((end * held[wide(g), :]).reshape(PER, D, N), axis=1)
            sums = sums + jnp.where(which == k, jnp.sum(partial, axis=1, keepdims=True), 0.0)
        kept[g * PER : (g + 1) * PER, :] = sums
    rows = jnp.transpose(kept[...])
    first = jnp.concatenate([rows[0:1, :H], rows[1:2, :H]], axis=1)
    odd = lax.broadcasted_iota(jnp.int32, (8, N), 0) % 2 == 1
    sent_ref[...] = jnp.where(odd, rows[2:3], first)


def finish_kernel(
    end_ref,
    sums_ref,
    carry_ref,
    leave_ref,
    slope_ref,
    step_part_ref,
    in_ref,
    sig_turned_ref,
    start_ref,
    sig_part_ref,
    sig_high_ref,
    sig_low_ref,
    in_part_ref,
    step_grad_ref,
    sig_grad_ref,
    in_grad_ref,
    in_maps,
    sig_turned,
    start,
    sig_part,
    sig_high,
    sig_low,
    in_part,
    step_grads,
    sig_grad,
    in_grad,
    got,
    gone,
):
    pairs = []
    for g in range(G):
        cols, rows, few = (slice(None), wide(g)), wide(g), (slice(None), narrow(g))
        for at, source, target in (
            (few, in_ref, in_maps),
            (cols, sig_part_ref, sig_part),
            (rows, sig_turned_ref, sig_turned),
            (rows, start_ref, start),
            (cols, sig_high_ref, sig_high),
            (cols, sig_low_ref, sig_low),
            (few, in_part_ref, in_part),
        ):
            pairs.append((source.at[at], target.at[at]))
    each = len(pairs) // G
    copies = fetch(got, pairs)
    earlier = mask_of(lambda i, j: i < j)
    leaving = []
    for batch in batches(FINISH_BATCH):
        for g in batch:
            for copy in copies[each * g : each * (g + 1)]:
                copy.wait()
        for g in batch:
            head = slice(g * PER, (g + 1) * PER)
            end = end_ref[wide(g), :]
            in_map = in_maps[:, narrow(g)]
            carry = carry_ref[head, :]
            total = sums_ref[head, 3:4]
            decay = sums_ref[head, 4:5]
            in_twice = jnp.concatenate([in_map, in_map], axis=1)
            end_high, end_low = split(end, 2)
            pieces = jnp.concatenate([end_high, end_low], axis=1)
            sig_grad[:, wide(g)] = sig_part[:, wide(g)] + spread(carry) * mm_nt(in_twice, pieces)
            both = mm(sig_high[:, wide(g)], pieces)
            in_grad[:, narrow(g)] = in_part[:, narrow(g)] + (
                both[:, :N] + (both[:, N:] + mm(sig_low[:, wide(g)], end_high))
            )
            turned = mm_nt(pieces, in_twice)
            pushed = (sig_turned[wide(g), :].astype(F32) * turned).reshape(PER, D, T)
            pushed = jnp.sum(pushed, axis=1)
            before = rows_times_mask(carry * pushed, earlier)
            held = jnp.sum((end * start[wide(g), :].astype(F32)).reshape(PER, D, N), axis=1)
            held = total * jnp.sum(held, axis=1, keepdims=True)
            step_grad = leave_ref[head, :] * pushed - decay * (before + held)
            step_grads[head, :] = (step_part_ref[head, :] + step_grad) * slope_ref[head, :]
        cols = pl.ds(batch[0] * WIDE, len(batch) * WIDE)
        few = pl.ds(batch[0] * N, len(batch) * N)
        leaving.append(
            pltpu.make_async_copy(
                sig_grad.at[:, cols], sig_grad_ref.at[:, cols], gone.at[2 * batch[0]]
            )
        )
        leaving[-1].start()
        leaving.append(
            pltpu.make_async_copy(
                in_grad.at[:, few], in_grad_ref.at[:, few], gone.at[2 * batch[0] + 1]
            )
        )
        leaving[-1].start()
    leaving.append(pltpu.make_async_copy(step_grads, step_grad_ref, gone.at[2 * G]))
    leaving[-1].start()
    for copy in leaving:
        copy.wait()


def call(kernel, grid, ins, outs, args, flops, mib, scratch=()):
    moved = sum(a.size * a.dtype.itemsize for a in args)
    moved += sum(math.prod(s.shape) * s.dtype.itemsize for _, s in outs)
    return pl.pallas_call(
        kernel,
        grid=(grid,) if grid else (),
        in_specs=ins,
        out_specs=[spec for spec, _ in outs],
        out_shape=[shape for _, shape in outs],
        scratch_shapes=list(scratch),
        compiler_params=pltpu.CompilerParams(
            dimension_semantics=("arbitrary",) if grid else None, vmem_limit_bytes=mib * MIB
        ),
        cost_estimate=pl.CostEstimate(flops=flops, bytes_accessed=moved, transcendentals=0),
    )(*args)


def far(*arrays):
    return [pltpu.with_memory_space_constraint(a, pltpu.HBM) for a in arrays]


def near(*arrays):
    return [pltpu.with_memory_space_constraint(a, pltpu.VMEM) for a in arrays]


def f32(*shape):
    return pltpu.HBM(shape, F32)


def bf16(*shape):
    return pltpu.HBM(shape, BF16)


def f32_near(*shape):
    return pltpu.VMEM(shape, F32)


WIDE_COLS = pl.BlockSpec((T, WIDE), lambda g: (0, g))
MAP_COLS = pl.BlockSpec((T, N), lambda g: (0, g))
HEAD_ROWS = pl.BlockSpec((PER, T), lambda g: (g, 0))
HEAD_LANES = pl.BlockSpec((PER, N), lambda g: (g, 0))
HEAD_ALL = pl.BlockSpec((1, H), lambda g: (0, 0))
STATE_COLS = pl.BlockSpec((WIDE, T), lambda g: (g, 0))
STATE_ROWS = pl.BlockSpec((WIDE, N), lambda g: (g, 0))


ELSEWHERE = pl.BlockSpec(memory_space=pl.ANY)
HERE = pl.BlockSpec(memory_space=pltpu.VMEM)
COPIES = pltpu.SemaphoreType.DMA


def send_states(cot, out_map, raw, decay_row, bias_row, blocks):
    rows = H * D // blocks + 8
    return call(
        state_kernel,
        0,
        [ELSEWHERE] * 5,
        [(HERE, f32_near(blocks, rows, N))],
        far(cot, out_map, raw, decay_row, bias_row),
        4 * H * D * N * T,
        24,
        [
            pltpu.VMEM((T, H * D), BF16),
            pltpu.VMEM((T, G * N), BF16),
            pltpu.VMEM((H, T), F32),
            pltpu.VMEM((1, H), F32),
            pltpu.VMEM((1, H), F32),
            COPIES((2 * G + 3,)),
        ],
    )[0]


def scan_states(states):
    blocks, rows, _ = states.shape
    rows -= 8
    return call(
        scan_kernel,
        0,
        [HERE],
        [(ELSEWHERE, f32(blocks, rows, N))],
        near(states),
        2 * H * D * N,
        16,
        [pltpu.VMEM((blocks, rows, N), F32), COPIES((rows // D,))],
    )[0]


def inner_part(sig, cot, in_map, out_map, raw, decay_row, bias_row, skip_row, start):
    return call(
        inner_kernel,
        G,
        [
            WIDE_COLS,
            WIDE_COLS,
            MAP_COLS,
            MAP_COLS,
            HEAD_ROWS,
            HEAD_ALL,
            HEAD_ALL,
            HEAD_ALL,
            STATE_ROWS,
        ],
        [
            (WIDE_COLS, f32(T, H * D)),
            (MAP_COLS, f32(T, G * N)),
            (MAP_COLS, f32(T, G * N)),
            (HEAD_ROWS, f32_near(H, T)),
            (STATE_ROWS, f32(H * D, N)),
            (STATE_ROWS, f32(H * D, N)),
            (HEAD_LANES, f32_near(H, N)),
            (HEAD_ROWS, f32_near(H, T)),
            (HEAD_ROWS, f32_near(H, T)),
            (HEAD_ROWS, f32_near(H, T)),
            (WIDE_COLS, bf16(T, H * D)),
            (WIDE_COLS, bf16(T, H * D)),
            (STATE_COLS, bf16(H * D, T)),
        ],
        far(sig, cot, in_map, out_map, raw, decay_row, bias_row, skip_row, start),
        H * T * T * N * 20,
        24,
    )


def local_sums(end, by_decay, by_bias, sums):
    return call(
        sums_kernel,
        0,
        [HERE, HERE, ELSEWHERE, ELSEWHERE],
        [(HERE, f32_near(8, N))],
        near(end, sums) + far(by_decay, by_bias),
        4 * H * D * N,
        16,
        [
            pltpu.VMEM((H * D, N), F32),
            pltpu.VMEM((H * D, N), F32),
            pltpu.VMEM((N, N), F32),
            COPIES((2 * (G // SUMS_BATCH),)),
        ],
    )[0]


def finish_part(
    end,
    sums,
    carry,
    leave,
    slope,
    step_part,
    in_map,
    sig_turned,
    start,
    sig_part,
    sig_high,
    sig_low,
    in_part,
):
    wide_float, narrow_float = pltpu.VMEM((T, H * D), F32), pltpu.VMEM((T, G * N), F32)
    wide_half = pltpu.VMEM((T, H * D), BF16)
    return call(
        finish_kernel,
        0,
        [HERE] * 6 + [ELSEWHERE] * 7,
        [
            (ELSEWHERE, f32(H, T)),
            (ELSEWHERE, f32(T, H * D)),
            (ELSEWHERE, f32(T, G * N)),
        ],
        near(end, sums, carry, leave, slope, step_part)
        + far(in_map, sig_turned, start, sig_part, sig_high, sig_low, in_part),
        14 * H * D * N * T,
        36,
        [
            pltpu.VMEM((T, G * N), BF16),
            pltpu.VMEM((H * D, T), BF16),
            pltpu.VMEM((H * D, N), BF16),
            wide_float,
            wide_half,
            wide_half,
            narrow_float,
            pltpu.VMEM((H, T), F32),
            wide_float,
            narrow_float,
            COPIES((7 * G,)),
            COPIES((2 * G + 1,)),
        ],
    )


def local(
    signal, cotangent, input_map, output_map, step_raw, decay_log, step_bias, skip_gain, checkpoints
):
    sig, cot, in_map, out_map, raw = (
        signal[0],
        cotangent[0],
        input_map[0],
        output_map[0],
        step_raw[0],
    )
    decay_row, bias_row, skip_row = decay_log[None], step_bias[None], skip_gain[None]
    start = checkpoints.reshape(H * D, N)
    blocks, deals = lax.axis_size("ctx"), lax.axis_size("dp")

    sent = send_states(cot, out_map, raw, decay_row, bias_row, blocks)
    ends = scan_states(lax.all_to_all(sent, "ctx", 0, 0))
    end = lax.all_to_all(ends, "ctx", 0, 0).reshape(H * D, N)
    (
        sig_part,
        in_part,
        out_grad,
        step_part,
        by_decay,
        by_bias,
        sums_here,
        carry,
        leave,
        slope,
        sig_high,
        sig_low,
        sig_turned,
    ) = inner_part(sig, cot, in_map, out_map, raw, decay_row, bias_row, skip_row, start)

    devices = blocks * deals
    sums = local_sums(end, by_decay, by_bias, sums_here)[:2]
    sums = sums + lax.ppermute(sums, "dp", [(i, i ^ 1) for i in range(deals)])
    cores = [
        [d * blocks + c for d in range(core, deals, 2) for c in range(blocks)] for core in range(2)
    ]
    sent = jnp.broadcast_to(sums[None], (devices // 2, 2, N))
    received = lax.all_to_all(sent, ("dp", "ctx"), 0, 0, axis_index_groups=cores)
    step_grad, sig_grad, in_grad = finish_part(
        end,
        sums_here,
        carry,
        leave,
        slope,
        step_part,
        in_map,
        sig_turned,
        start,
        sig_part,
        sig_high,
        sig_low,
        in_part,
    )
    summed = jnp.sum(received, axis=0) * (1.0 / (devices * T))
    return (
        sig_grad[None],
        in_grad[None],
        out_grad[None],
        step_grad[None],
        summed[0, :H],
        summed[1, :H],
        summed[0, H:],
    )


def solution(mesh):
    rows = P("dp", "ctx", None)
    placed = (rows, rows, rows, rows, P("dp", None, "ctx"), P(), P(), P())
    return jax.shard_map(
        local,
        mesh=mesh,
        in_specs=placed + (P("dp", "ctx", None, None, None),),
        out_specs=(rows, rows, rows, P("dp", None, "ctx"), P(), P(), P()),
        check_vma=False,
    )
```

```python
import functools
import math

import jax
import jax.numpy as jnp
from jax import lax
from jax.experimental import pallas as pl
from jax.experimental.pallas import tpu as pltpu
from jax.sharding import PartitionSpec as P

T = 256
H = 64
G = 8
D = 64
N = 128
PER = H // G
WIDE = PER * D
F32 = jnp.float32
BF16 = jnp.bfloat16
MIB = 1024 * 1024
STATE_BATCH = 4
INNER_FIRST = 4
SUMS_BATCH = 2
FINISH_BATCH = 3


def split(x, parts):
    pieces = []
    for _ in range(parts):
        piece = x.astype(BF16)
        pieces.append(piece)
        x = x - piece.astype(F32)
    return pieces


def mm(a, b):
    return lax.dot_general(a, b, (((1,), (0,)), ((), ())), preferred_element_type=F32)


def mm_nt(a, b):
    return lax.dot_general(a, b, (((1,), (1,)), ((), ())), preferred_element_type=F32)


def mm_tn(a, b):
    return lax.dot_general(a, b, (((0,), (0,)), ((), ())), preferred_element_type=F32)


def rows_times_mask(rows, mask):
    n = rows.shape[0]
    out = mm(jnp.concatenate(split(rows, 3), axis=0), mask)
    return out[:n] + out[n : 2 * n] + out[2 * n :]


def mask_of(relation):
    i = lax.broadcasted_iota(jnp.int32, (T, T), 0)
    j = lax.broadcasted_iota(jnp.int32, (T, T), 1)
    return jnp.where(relation(i, j), 1.0, 0.0).astype(BF16)


def column_of(row, first, count):
    i = lax.broadcasted_iota(jnp.int32, (count, H), 0) + first
    j = lax.broadcasted_iota(jnp.int32, (count, H), 1)
    return jnp.sum(jnp.where(i == j, row, 0.0), axis=1, keepdims=True)


def steps_of(raw, bias, decay_log):
    pre_act = raw + bias
    step = jnp.maximum(pre_act, 0.0) + jnp.log1p(jnp.exp(-jnp.abs(pre_act)))
    decay = jnp.exp(decay_log)
    rate = -decay * step
    cumul = rows_times_mask(rate, mask_of(lambda i, j: i <= j))
    return pre_act, step, decay, cumul


def spread(rows):
    head = lax.broadcasted_iota(jnp.int32, (PER, WIDE), 0)
    column = lax.broadcasted_iota(jnp.int32, (PER, WIDE), 1)
    own = jnp.where(column // D == head, 1.0, 0.0).astype(BF16)
    return mm_tn(jnp.concatenate(split(rows, 3), axis=0), jnp.concatenate([own] * 3, axis=0))


def columns(rows):
    pad = jnp.zeros((128 - PER * len(rows), T), F32)
    return jnp.transpose(jnp.concatenate(list(rows) + [pad], axis=0))


def fetch(sems, pairs):
    copies = [pltpu.make_async_copy(a, b, sems.at[k]) for k, (a, b) in enumerate(pairs)]
    for copy in copies:
        copy.start()
    return copies


def batches(size):
    return [range(g, min(g + size, G)) for g in range(0, G, size)]


def group_of(slot, odd):
    if slot in (0, 1):
        return slot + 2 * odd
    if slot in (2, 3):
        return slot + 4 - 2 * odd
    if slot in (4, 5):
        return slot - 2 - 2 * odd
    return slot - 2 + 2 * odd


def chosen(g, size):
    return pl.ds(pl.multiple_of(g * size, size), size)


def wide(g):
    return pl.ds(g * WIDE, WIDE)


def narrow(g):
    return pl.ds(g * N, N)


def state_kernel(
    odd_ref,
    cot_ref,
    out_ref,
    raw_ref,
    decay_ref,
    bias_ref,
    own_ref,
    own_total_ref,
    first_ref,
    second_ref,
    cot,
    out,
    raw,
    decay,
    bias,
    entries,
    got,
):
    odd = odd_ref[0]
    order = (4, 5, 6, 7, 0, 1, 2, 3)
    pairs = [(raw_ref, raw), (decay_ref, decay), (bias_ref, bias)]
    for slot in order:
        g = group_of(slot, odd)
        pairs.append((cot_ref.at[:, chosen(g, WIDE)], cot.at[:, wide(slot)]))
        pairs.append((out_ref.at[:, chosen(g, N)], out.at[:, narrow(slot)]))
    copies = fetch(got, pairs)
    for copy in copies[:3]:
        copy.wait()
    bias_column = column_of(bias[...], 0, H)
    decay_log = column_of(decay[...], 0, H)
    entries[...] = jnp.exp(steps_of(raw[...], bias_column, decay_log)[3])
    for batch in batches(STATE_BATCH):
        for k in batch:
            copies[2 * k + 3].wait()
            copies[2 * k + 4].wait()
        for slot in [order[k] for k in batch]:
            entry = entries[chosen(group_of(slot, odd), PER), :]
            turned = jnp.transpose(cot[:, wide(slot)]).astype(F32)
            weighted = (turned.reshape(PER, D, T) * entry[:, None, :]).reshape(WIDE, T)
            out_map = out[:, narrow(slot)]
            high, low = split(weighted, 2)
            state = mm(high, out_map) + mm(low, out_map)
            total = jnp.broadcast_to(entry[:, T - 1 :], (PER, N))
            if slot < 4:
                own_ref[wide(slot), :] = state
                own_total_ref[slot * PER : (slot + 1) * PER, :] = total
            else:
                ref, k = (first_ref, slot - 4) if slot < 6 else (second_ref, slot - 6)
                ref[wide(k), :] = state
                ref[2 * WIDE + k * PER : 2 * WIDE + (k + 1) * PER, :] = total


def flag_rows(flags_ref):
    keep = flags_ref[2:3, :]
    return (flags_ref[0:1, :], jnp.ones_like(keep)), (flags_ref[1:2, :], keep)


def combine_kernel(
    flags_ref,
    own_ref,
    own_total_ref,
    first_ref,
    second_ref,
    after_ref,
    sent_ref,
    other_total_ref,
    other_ref,
    other,
    gone,
):
    halves = flag_rows(flags_ref)
    per_half = 2 * PER
    each = sent_ref.shape[0]
    got = per_half // each
    totals = [[] for _ in range(each)]
    other_totals = []
    for half, ref in enumerate((first_ref, second_ref)):
        earlier, keep = halves[half]
        for h in range(per_half):
            mine = half * per_half + h
            state = own_ref[mine * D : (mine + 1) * D, :]
            total = own_total_ref[mine : mine + 1, :]
            met = ref[h * D : (h + 1) * D, :]
            met_total = ref[per_half * D + h : per_half * D + h + 1, :]
            by_own = jnp.where(earlier > 0, 1.0, met_total * keep)
            by_met = jnp.where(earlier > 0, total * keep, 1.0)
            at, q = h // got, half * got + h % got
            sent_ref[at, q * D : (q + 1) * D, :] = by_own * state + by_met * met
            totals[at].append(total * met_total)
            other[mine * D : (mine + 1) * D, :] = jnp.where(earlier > 0, met, state)
            other_totals.append(jnp.where(earlier > 0, met_total, total))
    rows = 2 * got
    for at in range(each):
        pad = [jnp.zeros((8 - rows, N), F32)]
        sent_ref[at, rows * D :, :] = jnp.concatenate(totals[at] + pad, axis=0)
    other_total_ref[...] = jnp.concatenate(other_totals, axis=0)
    copy = pltpu.make_async_copy(other, other_ref, gone.at[0])
    copy.start()
    copy.wait()


def scan_kernel(odd_ref, state_ref, after_ref, end_ref, end, gone):
    pairs, rows, _ = end.shape
    heads = rows // D
    leaving = []
    for h in range(heads):
        at = pl.ds(h * D, D)
        carry = jnp.zeros((D, N), F32)
        if h < heads // 2:
            for b in reversed(range(pairs)):
                end[b, at, :] = carry
                carry = state_ref[b, at, :] + state_ref[b, rows + h : rows + h + 1, :] * carry
        else:
            for k in reversed(range(pairs)):
                b = lax.rem(k + 1 - odd_ref[0], pairs)
                if k < pairs - 1:
                    end[b, at, :] = carry
                total = state_ref[b, rows + h : rows + h + 1, :]
                carry = state_ref[b, at, :] + total * carry
            end[lax.rem(pairs - odd_ref[0], pairs), at, :] = carry
        leaving.append(pltpu.make_async_copy(end.at[:, at], end_ref.at[:, at], gone.at[h]))
        leaving[-1].start()
    for copy in leaving:
        copy.wait()


def expand_kernel(
    flags_ref,
    end_ref,
    other_total_ref,
    other_ref,
    after_ref,
    own_ref,
    first_ref,
    second_ref,
    other,
    got,
):
    per_half = 2 * PER
    pairs = [(other_ref.at[wide(k)], other.at[wide(k)]) for k in range(4)]
    copies = fetch(got, pairs)
    halves = flag_rows(flags_ref)
    each = end_ref.shape[0]
    share = per_half // each
    for half, ref in enumerate((first_ref, second_ref)):
        earlier, keep = halves[half]
        later = 1.0 - earlier
        for h in range(per_half):
            mine = half * per_half + h
            if h % PER == 0:
                copies[mine // PER].wait()
            q = half * share + h % share
            end = end_ref[h // share, q * D : (q + 1) * D, :]
            beside = other[mine * D : (mine + 1) * D, :]
            total = other_total_ref[mine : mine + 1, :] * keep
            own_ref[mine * D : (mine + 1) * D, :] = (earlier * keep) * beside + jnp.where(
                earlier > 0, total, 1.0
            ) * end
            ref[h * D : (h + 1) * D, :] = (later * keep) * beside + jnp.where(
                earlier > 0, 1.0, total
            ) * end


def inner_kernel(
    first_group,
    sig_ref,
    cot_ref,
    in_ref,
    out_ref,
    raw_ref,
    decay_ref,
    bias_ref,
    skip_ref,
    start_ref,
    after_ref,
    *refs,
):
    (
        sig_grad_ref,
        in_grad_ref,
        out_grad_ref,
        step_grad_ref,
        sums_ref,
        carry_ref,
        leave_ref,
        slope_ref,
        token_ref,
    ) = refs[-9:]
    token_ref[...] = jnp.zeros_like(token_ref)
    head = (pl.program_id(0) + first_group) * PER
    bias = column_of(bias_ref[...], head, PER)
    decay_log = column_of(decay_ref[...], head, PER)
    pre_act, step, decay, cumul = steps_of(raw_ref[...], bias, decay_log)
    slope = jax.nn.sigmoid(pre_act)
    entry = jnp.exp(cumul)
    final = cumul[:, T - 1 :]
    total = jnp.exp(final)
    leave = jnp.exp(final - cumul)
    carry = leave * step
    carry_ref[...] = carry
    leave_ref[...] = leave
    slope_ref[...] = slope
    cols = columns([cumul - jnp.log(step), entry])
    in_map = in_ref[...]
    out_map = out_ref[...]
    out_float = out_map.astype(F32)
    scores = mm_nt(in_map, out_map)
    valid = lax.broadcasted_iota(jnp.int32, (T, T), 0) <= lax.broadcasted_iota(jnp.int32, (T, T), 1)
    lane = lax.broadcasted_iota(jnp.int32, (T, N), 1)
    first = lane < D
    score_grad = jnp.zeros((T, T), F32)
    out_grad = jnp.zeros((T, N), F32)
    found = jnp.zeros((T, N), F32)
    row_sums = []
    for pair in range(PER // 2):
        at = slice(pair * N, (pair + 1) * N)
        sig = sig_ref[:, at]
        cot = cot_ref[:, at]
        zero = jnp.zeros_like(sig)
        sig_grad = jnp.zeros((T, N), F32)
        start = start_ref[at, :]
        top = lax.broadcasted_iota(jnp.int32, (N, N), 0) < D
        none = jnp.zeros_like(start)
        both = jnp.concatenate(
            [jnp.where(top, start, none), jnp.where(top, none, start)], axis=1
        )
        began = mm(cot, both)
        for k in range(2):
            j = 2 * pair + k
            mine = first if k == 0 else jnp.logical_not(first)
            own_sig = jnp.where(mine, sig, zero)
            own_cot = jnp.where(mine, cot, zero)
            mix_grad = mm_nt(own_sig, cot)
            fade = jnp.where(valid, jnp.exp(cumul[j : j + 1, :] - cols[:, j : j + 1]), 0.0)
            mixing = fade * scores
            high, low = split(mixing, 2)
            sig_grad = sig_grad + (mm(high, own_cot) + mm(low, own_cot))
            score_grad = score_grad + mix_grad * fade
            product = mix_grad * mixing
            row_sums.append(jnp.sum(product, axis=0, keepdims=True))
            found = jnp.where(lane == j, jnp.sum(product, axis=1, keepdims=True), found)
            own = began[:, k * N : (k + 1) * N]
            out_grad = out_grad + own * cols[:, PER + j : PER + j + 1]
            found = jnp.where(
                lane == PER + j, jnp.sum(own * out_float, axis=1, keepdims=True), found
            )
        sig_grad_ref[:, at] = sig_grad
    sig_float = sig_ref[...].astype(F32)
    cot_float = cot_ref[...].astype(F32)
    own = jnp.where(
        lax.broadcasted_iota(jnp.int32, (PER, WIDE), 1) // D
        == lax.broadcasted_iota(jnp.int32, (PER, WIDE), 0),
        1.0,
        0.0,
    )
    skip = jnp.sum(own * column_of(skip_ref[...], head, PER), axis=0, keepdims=True)
    sig_grad_ref[...] = sig_grad_ref[...] + skip * cot_float
    high, low = split(score_grad, 2)
    in_grad_ref[...] = mm(high, out_map) + mm(low, out_map)
    out_grad_ref[...] = out_grad + (mm_tn(high, in_map) + mm_tn(low, in_map))
    found = jnp.transpose(found)
    col_sum = found[:PER]
    from_start = found[PER : 2 * PER]
    cumul_grad = jnp.concatenate(row_sums, axis=0) - col_sum + entry * from_start
    rate_grad = rows_times_mask(cumul_grad, mask_of(lambda i, j: i >= j))
    step_grad = col_sum / step - rate_grad * decay
    step_grad_ref[...] = step_grad
    skip_sum = jnp.sum(
        own * jnp.sum(sig_float * cot_float, axis=0, keepdims=True), axis=1, keepdims=True
    )
    decay_sum = -decay * jnp.sum(rate_grad * step, axis=1, keepdims=True)
    bias_sum = jnp.sum(step_grad * slope, axis=1, keepdims=True)
    which = lax.broadcasted_iota(jnp.int32, (PER, N), 1)
    sums = jnp.zeros((PER, N), F32)
    for k, column in enumerate((decay_sum, bias_sum, skip_sum, total, decay)):
        sums = jnp.where(which == k, column, sums)
    sums_ref[...] = sums


def prepare_kernel(
    sig_ref,
    in_ref,
    raw_ref,
    decay_ref,
    bias_ref,
    start_ref,
    after_ref,
    by_decay_ref,
    by_bias_ref,
    sig_high_ref,
    sig_low_ref,
    sig_turned_ref,
):
    head = pl.program_id(0) * PER
    bias = column_of(bias_ref[...], head, PER)
    decay_log = column_of(decay_ref[...], head, PER)
    pre_act, step, decay, cumul = steps_of(raw_ref[...], bias, decay_log)
    slope = jax.nn.sigmoid(pre_act)
    final = cumul[:, T - 1 :]
    total = jnp.exp(final)
    leave = jnp.exp(final - cumul)
    carry = leave * step
    later = rows_times_mask(slope, mask_of(lambda i, j: i > j))
    in_map = in_ref[...]
    sig_float = sig_ref[...].astype(F32)
    sig_turned_ref[...] = jnp.transpose(sig_ref[...])
    sig_high_ref[...], sig_low_ref[...] = split(sig_float * spread(carry), 2)
    into_decay = (final - cumul) * carry
    into_bias = leave * (slope - decay * step * later)
    start = start_ref[...].astype(F32).reshape(PER, D, N)
    turned = jnp.transpose(sig_ref[...]).astype(F32).reshape(PER, D, T)
    for rows, weight, ref in (
        (into_decay, final * total, by_decay_ref),
        (into_bias, -decay * total * jnp.sum(slope, axis=1, keepdims=True), by_bias_ref),
    ):
        high, low = split((turned * rows[:, None, :]).reshape(WIDE, T), 2)
        grown = mm(high, in_map) + mm(low, in_map)
        ref[...] = grown + (start * weight[:, :, None]).reshape(WIDE, N)


def end_of(slot, own_ref, first_ref, second_ref):
    if slot < 4:
        return own_ref[wide(slot), :]
    return first_ref[wide(slot - 4), :] if slot < 6 else second_ref[wide(slot - 6), :]


def sums_kernel(
    odd_ref,
    own_ref,
    first_ref,
    second_ref,
    sums_ref,
    by_decay_ref,
    by_bias_ref,
    sent_ref,
    by_decay,
    by_bias,
    kept,
    got,
):
    odd = odd_ref[0]
    pairs = []
    for slot in range(G):
        at = chosen(group_of(slot, odd), WIDE)
        pairs.append((by_decay_ref.at[at], by_decay.at[wide(slot)]))
        pairs.append((by_bias_ref.at[at], by_bias.at[wide(slot)]))
    copies = fetch(got, pairs)
    which = lax.broadcasted_iota(jnp.int32, (PER, N), 1)
    kept[...] = jnp.zeros_like(kept)
    for batch in batches(SUMS_BATCH):
        for slot in batch:
            copies[2 * slot].wait()
            copies[2 * slot + 1].wait()
        for slot in batch:
            end = end_of(slot, own_ref, first_ref, second_ref)
            head = chosen(group_of(slot, odd), PER)
            sums = sums_ref[head, :]
            for k, held in enumerate((by_decay, by_bias)):
                partial = jnp.sum((end * held[wide(slot), :]).reshape(PER, D, N), axis=1)
                sums = sums + jnp.where(which == k, jnp.sum(partial, axis=1, keepdims=True), 0.0)
            kept[head, :] = sums
    rows = jnp.transpose(kept[...])
    first = jnp.concatenate([rows[0:1, :H], rows[1:2, :H]], axis=1)
    odd = lax.broadcasted_iota(jnp.int32, (8, N), 0) % 2 == 1
    sent_ref[...] = jnp.where(odd, rows[2:3], first)


def finish_kernel(
    odd_ref,
    own_ref,
    first_ref,
    second_ref,
    sums_ref,
    carry_ref,
    leave_ref,
    slope_ref,
    step_part_ref,
    in_ref,
    sig_turned_ref,
    start_ref,
    sig_part_ref,
    sig_high_ref,
    sig_low_ref,
    in_part_ref,
    step_grad_ref,
    sig_grad_ref,
    in_grad_ref,
    in_maps,
    sig_turned,
    start,
    sig_part,
    sig_high,
    sig_low,
    in_part,
    step_grads,
    sig_grad,
    in_grad,
    got,
    gone,
):
    odd = odd_ref[0]
    pairs = []
    every = slice(None)
    for slot in range(G):
        g = group_of(slot, odd)
        cols = ((every, chosen(g, WIDE)), (every, wide(slot)))
        rows = ((chosen(g, WIDE),), (wide(slot),))
        few = ((every, chosen(g, N)), (every, narrow(slot)))
        for (there, here), source, target in (
            (few, in_ref, in_maps),
            (cols, sig_part_ref, sig_part),
            (rows, sig_turned_ref, sig_turned),
            (rows, start_ref, start),
            (cols, sig_high_ref, sig_high),
            (cols, sig_low_ref, sig_low),
            (few, in_part_ref, in_part),
        ):
            pairs.append((source.at[there], target.at[here]))
    each = len(pairs) // G
    copies = fetch(got, pairs)
    earlier = mask_of(lambda i, j: i < j)
    leaving = []
    for batch in batches(FINISH_BATCH):
        for g in batch:
            for copy in copies[each * g : each * (g + 1)]:
                copy.wait()
        for g in batch:
            head = chosen(group_of(g, odd), PER)
            end = end_of(g, own_ref, first_ref, second_ref)
            in_map = in_maps[:, narrow(g)]
            carry = carry_ref[head, :]
            columns_here = sums_ref[head, :]
            total = columns_here[:, 3:4]
            decay = columns_here[:, 4:5]
            in_twice = jnp.concatenate([in_map, in_map], axis=1)
            end_high, end_low = split(end, 2)
            pieces = jnp.concatenate([end_high, end_low], axis=1)
            sig_grad[:, wide(g)] = sig_part[:, wide(g)] + spread(carry) * mm_nt(in_twice, pieces)
            both = mm(sig_high[:, wide(g)], pieces)
            in_grad[:, narrow(g)] = in_part[:, narrow(g)] + (
                both[:, :N] + (both[:, N:] + mm(sig_low[:, wide(g)], end_high))
            )
            turned = mm_nt(pieces, in_twice)
            pushed = (sig_turned[wide(g), :].astype(F32) * turned).reshape(PER, D, T)
            pushed = jnp.sum(pushed, axis=1)
            before = rows_times_mask(carry * pushed, earlier)
            held = jnp.sum((end * start[wide(g), :].astype(F32)).reshape(PER, D, N), axis=1)
            held = total * jnp.sum(held, axis=1, keepdims=True)
            step_grad = leave_ref[head, :] * pushed - decay * (before + held)
            step_grads[head, :] = (step_part_ref[head, :] + step_grad) * slope_ref[head, :]
        for g in batch:
            there = group_of(g, odd)
            for k, (source, target) in enumerate(
                (
                    (sig_grad.at[:, wide(g)], sig_grad_ref.at[:, chosen(there, WIDE)]),
                    (in_grad.at[:, narrow(g)], in_grad_ref.at[:, chosen(there, N)]),
                )
            ):
                leaving.append(pltpu.make_async_copy(source, target, gone.at[2 * g + k]))
                leaving[-1].start()
    leaving.append(pltpu.make_async_copy(step_grads, step_grad_ref, gone.at[2 * G]))
    leaving[-1].start()
    for copy in leaving:
        copy.wait()


def call(kernel, grid, ins, outs, args, flops, mib, scratch=(), aliases={}):
    moved = sum(a.size * a.dtype.itemsize for a in args)
    moved += sum(math.prod(s.shape) * s.dtype.itemsize for _, s in outs)
    return pl.pallas_call(
        kernel,
        grid=(grid,) if grid else (),
        in_specs=ins,
        out_specs=[spec for spec, _ in outs],
        out_shape=[shape for _, shape in outs],
        scratch_shapes=list(scratch),
        input_output_aliases=aliases,
        compiler_params=pltpu.CompilerParams(
            dimension_semantics=("arbitrary",) if grid else None, vmem_limit_bytes=mib * MIB
        ),
        cost_estimate=pl.CostEstimate(flops=flops, bytes_accessed=moved, transcendentals=0),
    )(*args)


def far(*arrays):
    return [pltpu.with_memory_space_constraint(a, pltpu.HBM) for a in arrays]


def near(*arrays):
    return [pltpu.with_memory_space_constraint(a, pltpu.VMEM) for a in arrays]


def f32(*shape):
    return pltpu.HBM(shape, F32)


def bf16(*shape):
    return pltpu.HBM(shape, BF16)


def f32_near(*shape):
    return pltpu.VMEM(shape, F32)


WIDE_COLS = pl.BlockSpec((T, WIDE), lambda g: (0, g))
MAP_COLS = pl.BlockSpec((T, N), lambda g: (0, g))
HEAD_ROWS = pl.BlockSpec((PER, T), lambda g: (g, 0))
HEAD_LANES = pl.BlockSpec((PER, N), lambda g: (g, 0))
HEAD_ALL = pl.BlockSpec((1, H), lambda g: (0, 0))
STATE_COLS = pl.BlockSpec((WIDE, T), lambda g: (g, 0))
STATE_ROWS = pl.BlockSpec((WIDE, N), lambda g: (g, 0))


ELSEWHERE = pl.BlockSpec(memory_space=pl.ANY)
HERE = pl.BlockSpec(memory_space=pltpu.VMEM)
SCALAR = pl.BlockSpec(memory_space=pltpu.SMEM)
COPIES = pltpu.SemaphoreType.DMA


def block_states(odd, cot, out_map, raw, decay_row, bias_row):
    halves = f32_near(H * D // 4 + H // 4, N)
    return call(
        state_kernel,
        0,
        [SCALAR] + [ELSEWHERE] * 5,
        [
            (HERE, f32_near(H * D // 2, N)),
            (HERE, f32_near(H // 2, N)),
            (HERE, halves),
            (HERE, halves),
        ],
        [odd] + far(cot, out_map, raw, decay_row, bias_row),
        4 * H * D * N * T,
        24,
        [
            pltpu.VMEM((T, H * D), BF16),
            pltpu.VMEM((T, G * N), BF16),
            pltpu.VMEM((H, T), F32),
            pltpu.VMEM((1, H), F32),
            pltpu.VMEM((1, H), F32),
            pltpu.VMEM((H, T), F32),
            COPIES((2 * G + 3,)),
        ],
    )


def combine_states(flags, own, own_total, first, second, after, pairs):
    return call(
        combine_kernel,
        0,
        [HERE] * 5 + [ELSEWHERE],
        [
            (HERE, f32_near(pairs, H * D // 2 // pairs + 8, N)),
            (HERE, f32_near(H // 2, N)),
            (ELSEWHERE, f32(H * D // 2, N)),
        ],
        near(flags, own, own_total, first, second) + far(after),
        4 * H * D * N,
        16,
        [pltpu.VMEM((H * D // 2, N), F32), COPIES((1,))],
    )


def scan_states(odd, states, after):
    pairs, rows, _ = states.shape
    rows -= 8
    return call(
        scan_kernel,
        0,
        [SCALAR, HERE, ELSEWHERE],
        [(ELSEWHERE, f32(pairs, rows, N))],
        [odd] + near(states) + far(after),
        H * D * N,
        16,
        [pltpu.VMEM((pairs, rows, N), F32), COPIES((rows // D,))],
    )[0]


def expand_ends(flags, ends, other_total, other, after):
    quarter = f32_near(H * D // 4, N)
    return call(
        expand_kernel,
        0,
        [HERE] * 3 + [ELSEWHERE] * 2,
        [(HERE, f32_near(H * D // 2, N)), (HERE, quarter), (HERE, quarter)],
        near(flags, ends, other_total) + far(other, after),
        4 * H * D * N,
        16,
        [pltpu.VMEM((H * D // 2, N), F32), COPIES((4,))],
    )


def inner_part(
    groups, sig, cot, in_map, out_map, raw, decay_row, bias_row, skip_row, start, after, begun=()
):
    first = groups[0]
    wide_cols = pl.BlockSpec((T, WIDE), lambda g: (0, g + first))
    map_cols = pl.BlockSpec((T, N), lambda g: (0, g + first))
    head_rows = pl.BlockSpec((PER, T), lambda g: (g + first, 0))
    head_lanes = pl.BlockSpec((PER, N), lambda g: (g + first, 0))
    state_rows = pl.BlockSpec((WIDE, N), lambda g: (g + first, 0))
    ins = [wide_cols, wide_cols, map_cols, map_cols, head_rows] + [HEAD_ALL] * 3
    ins += [state_rows] + [ELSEWHERE] * (1 + len(begun))
    return call(
        functools.partial(inner_kernel, first),
        len(groups),
        ins,
        [
            (wide_cols, f32(T, H * D)),
            (map_cols, f32(T, G * N)),
            (map_cols, f32(T, G * N)),
            (head_rows, f32_near(H, T)),
            (head_lanes, f32_near(H, N)),
            (head_rows, f32_near(H, T)),
            (head_rows, f32_near(H, T)),
            (head_rows, f32_near(H, T)),
            (pl.BlockSpec((8, N), lambda g: (0, 0)), f32(8, N)),
        ],
        far(sig, cot, in_map, out_map, raw, decay_row, bias_row, skip_row, start, after)
        + far(*begun[:3])
        + near(*begun[3:]),
        len(groups) * PER * T * T * N * 15,
        24,
        aliases={10 + k: k for k in range(len(begun))},
    )


def prepared_part(sig, in_map, raw, decay_row, bias_row, start, after):
    return call(
        prepare_kernel,
        G,
        [WIDE_COLS, MAP_COLS, HEAD_ROWS, HEAD_ALL, HEAD_ALL, STATE_ROWS]
        + [pl.BlockSpec((H // 2, N), lambda g: (0, 0))],
        [
            (STATE_ROWS, f32(H * D, N)),
            (STATE_ROWS, f32(H * D, N)),
            (WIDE_COLS, bf16(T, H * D)),
            (WIDE_COLS, bf16(T, H * D)),
            (STATE_COLS, bf16(H * D, T)),
        ],
        far(sig, in_map, raw, decay_row, bias_row, start) + near(after),
        H * T * T * N * 5,
        24,
    )


def local_sums(odd, own, first, second, sums, by_decay, by_bias):
    return call(
        sums_kernel,
        0,
        [SCALAR] + [HERE] * 4 + [ELSEWHERE] * 2,
        [(HERE, f32_near(8, N))],
        [odd] + near(own, first, second, sums) + far(by_decay, by_bias),
        4 * H * D * N,
        16,
        [
            pltpu.VMEM((H * D, N), F32),
            pltpu.VMEM((H * D, N), F32),
            pltpu.VMEM((N, N), F32),
            COPIES((2 * G,)),
        ],
    )[0]


def finish_part(
    odd,
    own,
    first,
    second,
    sums,
    carry,
    leave,
    slope,
    step_part,
    in_map,
    sig_turned,
    start,
    sig_part,
    sig_high,
    sig_low,
    in_part,
):
    wide_float, narrow_float = pltpu.VMEM((T, H * D), F32), pltpu.VMEM((T, G * N), F32)
    wide_half = pltpu.VMEM((T, H * D), BF16)
    return call(
        finish_kernel,
        0,
        [SCALAR] + [HERE] * 8 + [ELSEWHERE] * 7,
        [
            (ELSEWHERE, f32(H, T)),
            (ELSEWHERE, f32(T, H * D)),
            (ELSEWHERE, f32(T, G * N)),
        ],
        [odd]
        + near(own, first, second, sums, carry, leave, slope, step_part)
        + far(in_map, sig_turned, start, sig_part, sig_high, sig_low, in_part),
        14 * H * D * N * T,
        36,
        [
            pltpu.VMEM((T, G * N), BF16),
            pltpu.VMEM((H * D, T), BF16),
            pltpu.VMEM((H * D, N), BF16),
            wide_float,
            wide_half,
            wide_half,
            narrow_float,
            pltpu.VMEM((H, T), F32),
            wide_float,
            narrow_float,
            COPIES((7 * G,)),
            COPIES((2 * G + 1,)),
        ],
    )


def local(
    signal, cotangent, input_map, output_map, step_raw, decay_log, step_bias, skip_gain, checkpoints
):
    sig, cot, in_map, out_map, raw = (
        signal[0],
        cotangent[0],
        input_map[0],
        output_map[0],
        step_raw[0],
    )
    decay_row, bias_row, skip_row = decay_log[None], step_bias[None], skip_gain[None]
    start = checkpoints.reshape(H * D, N)
    blocks, deals = lax.axis_size("ctx"), lax.axis_size("dp")

    at = lax.axis_index("ctx")
    odd = lax.rem(at, 2)
    edge = jnp.logical_or(at == 0, at == blocks - 1)
    flags = jnp.stack([1 - odd, odd, 1 - edge.astype(jnp.int32)]).astype(F32)
    flags = jnp.broadcast_to(jnp.pad(flags, (0, 5))[:, None], (8, N))
    odd = odd[None]
    inward = [(i, i ^ 1) for i in range(blocks)]
    across = [(i, (i + 1 if i % 2 else i - 1) % blocks) for i in range(blocks)]
    alike = [list(range(0, blocks, 2)), list(range(1, blocks, 2))]

    own, own_total, first, second = block_states(odd, cot, out_map, raw, decay_row, bias_row)
    first = lax.ppermute(first, "ctx", inward)
    second = lax.ppermute(second, "ctx", across)
    by_decay, by_bias, sig_high, sig_low, sig_turned = prepared_part(
        sig, in_map, raw, decay_row, bias_row, start, own_total
    )
    sent, other_total, other = combine_states(
        flags, own, own_total, first, second, sig_turned, blocks // 2
    )
    states = lax.all_to_all(sent, "ctx", 0, 0, axis_index_groups=alike)
    operands = (sig, cot, in_map, out_map, raw, decay_row, bias_row, skip_row, start)
    *begun, token = inner_part(range(INNER_FIRST), *operands, other)
    ends = scan_states(odd, states, token)
    (
        sig_part,
        in_part,
        out_grad,
        step_part,
        sums_here,
        carry,
        leave,
        slope,
        token,
    ) = inner_part(range(INNER_FIRST, G), *operands, ends, begun)
    ends = lax.all_to_all(ends, "ctx", 0, 0, axis_index_groups=alike)
    own, first, second = expand_ends(flags, ends, other_total, other, token)
    first = lax.ppermute(first, "ctx", inward)
    second = lax.ppermute(second, "ctx", across)

    devices = blocks * deals
    sums = local_sums(odd, own, first, second, sums_here, by_decay, by_bias)[:2]
    sums = sums + lax.ppermute(sums, "dp", [(i, i ^ 1) for i in range(deals)])
    cores = [
        [d * blocks + c for d in range(core, deals, 2) for c in range(blocks)] for core in range(2)
    ]
    sent = jnp.broadcast_to(sums[None], (devices // 2, 2, N))
    received = lax.all_to_all(sent, ("dp", "ctx"), 0, 0, axis_index_groups=cores)
    step_grad, sig_grad, in_grad = finish_part(
        odd,
        own,
        first,
        second,
        sums_here,
        carry,
        leave,
        slope,
        step_part,
        in_map,
        sig_turned,
        start,
        sig_part,
        sig_high,
        sig_low,
        in_part,
    )
    summed = jnp.sum(received, axis=0) * (1.0 / (devices * T))
    return (
        sig_grad[None],
        in_grad[None],
        out_grad[None],
        step_grad[None],
        summed[0, :H],
        summed[1, :H],
        summed[0, H:],
    )


def solution(mesh):
    rows = P("dp", "ctx", None)
    placed = (rows, rows, rows, rows, P("dp", None, "ctx"), P(), P(), P())
    return jax.shard_map(
        local,
        mesh=mesh,
        in_specs=placed + (P("dp", "ctx", None, None, None),),
        out_specs=(rows, rows, rows, P("dp", None, "ctx"), P(), P(), P()),
        check_vma=False,
    )
```

```python
import functools
import math

import jax
import jax.numpy as jnp
from jax import lax
from jax.experimental import pallas as pl
from jax.experimental.pallas import tpu as pltpu
from jax.sharding import PartitionSpec as P

T = 256
H = 64
G = 8
D = 64
N = 128
PER = H // G
WIDE = PER * D
F32 = jnp.float32
BF16 = jnp.bfloat16
MIB = 1024 * 1024
STATE_BATCH = 4
OWN = (0, 1, 2, 3)
MET = (4, 5, 6, 7)
INNER_FIRST = 4
SUMS_BATCH = 2
FINISH_BATCH = 2


def split(x, parts):
    pieces = []
    for _ in range(parts):
        piece = x.astype(BF16)
        pieces.append(piece)
        x = x - piece.astype(F32)
    return pieces


def mm(a, b):
    return lax.dot_general(a, b, (((1,), (0,)), ((), ())), preferred_element_type=F32)


def mm_nt(a, b):
    return lax.dot_general(a, b, (((1,), (1,)), ((), ())), preferred_element_type=F32)


def mm_tn(a, b):
    return lax.dot_general(a, b, (((0,), (0,)), ((), ())), preferred_element_type=F32)


def rows_times_mask(rows, mask):
    n = rows.shape[0]
    out = mm(jnp.concatenate(split(rows, 3), axis=0), mask)
    return out[:n] + out[n : 2 * n] + out[2 * n :]


def mask_of(relation):
    i = lax.broadcasted_iota(jnp.int32, (T, T), 0)
    j = lax.broadcasted_iota(jnp.int32, (T, T), 1)
    return jnp.where(relation(i, j), 1.0, 0.0).astype(BF16)


def column_of(row, first, count):
    i = lax.broadcasted_iota(jnp.int32, (count, H), 0) + first
    j = lax.broadcasted_iota(jnp.int32, (count, H), 1)
    return jnp.sum(jnp.where(i == j, row, 0.0), axis=1, keepdims=True)


def steps_of(raw, bias, decay_log):
    pre_act = raw + bias
    step = jnp.maximum(pre_act, 0.0) + jnp.log1p(jnp.exp(-jnp.abs(pre_act)))
    decay = jnp.exp(decay_log)
    rate = -decay * step
    cumul = rows_times_mask(rate, mask_of(lambda i, j: i <= j))
    return pre_act, step, decay, cumul


def spread(rows):
    head = lax.broadcasted_iota(jnp.int32, (PER, WIDE), 0)
    column = lax.broadcasted_iota(jnp.int32, (PER, WIDE), 1)
    own = jnp.where(column // D == head, 1.0, 0.0).astype(BF16)
    return mm_tn(jnp.concatenate(split(rows, 3), axis=0), jnp.concatenate([own] * 3, axis=0))


def columns(rows):
    pad = jnp.zeros((128 - PER * len(rows), T), F32)
    return jnp.transpose(jnp.concatenate(list(rows) + [pad], axis=0))


def fetch(sems, pairs):
    copies = [pltpu.make_async_copy(a, b, sems.at[k]) for k, (a, b) in enumerate(pairs)]
    for copy in copies:
        copy.start()
    return copies


def batches(size, count):
    return [range(k, min(k + size, count)) for k in range(0, count, size)]


def group_of(slot, odd):
    if slot in (0, 1):
        return slot + 2 * odd
    if slot in (2, 3):
        return slot + 4 - 2 * odd
    if slot in (4, 5):
        return slot - 2 - 2 * odd
    return slot - 2 + 2 * odd


def chosen(g, size):
    return pl.ds(pl.multiple_of(g * size, size), size)


def wide(g):
    return pl.ds(g * WIDE, WIDE)


def narrow(g):
    return pl.ds(g * N, N)


def state_kernel(
    odd_ref,
    cot_ref,
    out_ref,
    raw_ref,
    decay_ref,
    bias_ref,
    own_ref,
    own_total_ref,
    first_ref,
    second_ref,
    cot,
    out,
    raw,
    decay,
    bias,
    entries,
    got,
):
    odd = odd_ref[0]
    order = (4, 5, 6, 7, 0, 1, 2, 3)
    pairs = [(raw_ref, raw), (decay_ref, decay), (bias_ref, bias)]
    for slot in order:
        g = group_of(slot, odd)
        pairs.append((cot_ref.at[:, chosen(g, WIDE)], cot.at[:, wide(slot)]))
        pairs.append((out_ref.at[:, chosen(g, N)], out.at[:, narrow(slot)]))
    copies = fetch(got, pairs)
    for copy in copies[:3]:
        copy.wait()
    bias_column = column_of(bias[...], 0, H)
    decay_log = column_of(decay[...], 0, H)
    entries[...] = jnp.exp(steps_of(raw[...], bias_column, decay_log)[3])
    for batch in batches(STATE_BATCH, G):
        for k in batch:
            copies[2 * k + 3].wait()
            copies[2 * k + 4].wait()
        for slot in [order[k] for k in batch]:
            entry = entries[chosen(group_of(slot, odd), PER), :]
            turned = jnp.transpose(cot[:, wide(slot)]).astype(F32)
            weighted = (turned.reshape(PER, D, T) * entry[:, None, :]).reshape(WIDE, T)
            out_map = out[:, narrow(slot)]
            high, low = split(weighted, 2)
            state = mm(high, out_map) + mm(low, out_map)
            total = jnp.broadcast_to(entry[:, T - 1 :], (PER, N))
            if slot < 4:
                own_ref[wide(slot), :] = state
                own_total_ref[slot * PER : (slot + 1) * PER, :] = total
            else:
                ref, k = (first_ref, slot - 4) if slot < 6 else (second_ref, slot - 6)
                ref[wide(k), :] = state
                ref[2 * WIDE + k * PER : 2 * WIDE + (k + 1) * PER, :] = total


def flag_rows(flags_ref):
    keep = flags_ref[2:3, :]
    return (flags_ref[0:1, :], jnp.ones_like(keep)), (flags_ref[1:2, :], keep)


def combine_kernel(
    flags_ref,
    own_ref,
    own_total_ref,
    second_ref,
    first_ref,
    after_ref,
    sent_ref,
    other_total_ref,
    other_ref,
    other,
    gone,
):
    halves = flag_rows(flags_ref)
    per_half = 2 * PER
    each = sent_ref.shape[0]
    got = per_half // each
    totals = [[] for _ in range(each)]
    other_totals = []
    leaving = []
    for half, ref in enumerate((first_ref, second_ref)):
        earlier, keep = halves[half]
        for h in range(per_half):
            mine = half * per_half + h
            state = own_ref[mine * D : (mine + 1) * D, :]
            total = own_total_ref[mine : mine + 1, :]
            met = ref[h * D : (h + 1) * D, :]
            met_total = ref[per_half * D + h : per_half * D + h + 1, :]
            by_own = jnp.where(earlier > 0, 1.0, met_total * keep)
            by_met = jnp.where(earlier > 0, total * keep, 1.0)
            at, q = h // got, half * got + h % got
            sent_ref[at, q * D : (q + 1) * D, :] = by_own * state + by_met * met
            totals[at].append(total * met_total)
            other[mine * D : (mine + 1) * D, :] = jnp.where(earlier > 0, met, state)
            other_totals.append(jnp.where(earlier > 0, met_total, total))
            if h % PER == PER - 1:
                part = wide(mine // PER)
                copy = pltpu.make_async_copy(
                    other.at[part], other_ref.at[part], gone.at[mine // PER]
                )
                copy.start()
                leaving.append(copy)
    rows = 2 * got
    for at in range(each):
        pad = [jnp.zeros((8 - rows, N), F32)]
        sent_ref[at, rows * D :, :] = jnp.concatenate(totals[at] + pad, axis=0)
    other_total_ref[...] = jnp.concatenate(other_totals, axis=0)
    for copy in leaving:
        copy.wait()


def scan_kernel(odd_ref, state_ref, after_ref, end_ref, end, gone):
    pairs, rows, _ = end.shape
    heads = rows // D
    leaving = []
    for h in range(heads):
        at = pl.ds(h * D, D)
        carry = jnp.zeros((D, N), F32)
        if h < heads // 2:
            for b in reversed(range(pairs)):
                end[b, at, :] = carry
                carry = state_ref[b, at, :] + state_ref[b, rows + h : rows + h + 1, :] * carry
        else:
            for k in reversed(range(pairs)):
                b = lax.rem(k + 1 - odd_ref[0], pairs)
                if k < pairs - 1:
                    end[b, at, :] = carry
                total = state_ref[b, rows + h : rows + h + 1, :]
                carry = state_ref[b, at, :] + total * carry
            end[lax.rem(pairs - odd_ref[0], pairs), at, :] = carry
        leaving.append(pltpu.make_async_copy(end.at[:, at], end_ref.at[:, at], gone.at[h]))
        leaving[-1].start()
    for copy in leaving:
        copy.wait()


def expand_kernel(
    flags_ref,
    end_ref,
    other_total_ref,
    other_ref,
    after_ref,
    own_ref,
    first_ref,
    second_ref,
    other,
    got,
):
    per_half = 2 * PER
    pairs = [(other_ref.at[wide(k)], other.at[wide(k)]) for k in range(4)]
    copies = fetch(got, pairs)
    halves = flag_rows(flags_ref)
    each = end_ref.shape[0]
    share = per_half // each
    for half, ref in enumerate((first_ref, second_ref)):
        earlier, keep = halves[half]
        later = 1.0 - earlier
        for h in range(per_half):
            mine = half * per_half + h
            if h % PER == 0:
                copies[mine // PER].wait()
            q = half * share + h % share
            end = end_ref[h // share, q * D : (q + 1) * D, :]
            beside = other[mine * D : (mine + 1) * D, :]
            total = other_total_ref[mine : mine + 1, :] * keep
            own_ref[mine * D : (mine + 1) * D, :] = (earlier * keep) * beside + jnp.where(
                earlier > 0, total, 1.0
            ) * end
            ref[h * D : (h + 1) * D, :] = (later * keep) * beside + jnp.where(
                earlier > 0, 1.0, total
            ) * end


def inner_kernel(
    first_group,
    sig_ref,
    cot_ref,
    in_ref,
    out_ref,
    raw_ref,
    decay_ref,
    bias_ref,
    skip_ref,
    start_ref,
    after_ref,
    *refs,
):
    (
        sig_grad_ref,
        in_grad_ref,
        out_grad_ref,
        step_grad_ref,
        sums_ref,
        carry_ref,
        leave_ref,
        slope_ref,
        token_ref,
    ) = refs[-9:]
    token_ref[...] = jnp.zeros_like(token_ref)
    head = (pl.program_id(0) + first_group) * PER
    bias = column_of(bias_ref[...], head, PER)
    decay_log = column_of(decay_ref[...], head, PER)
    pre_act, step, decay, cumul = steps_of(raw_ref[...], bias, decay_log)
    slope = jax.nn.sigmoid(pre_act)
    entry = jnp.exp(cumul)
    final = cumul[:, T - 1 :]
    total = jnp.exp(final)
    leave = jnp.exp(final - cumul)
    carry = leave * step
    carry_ref[...] = carry
    leave_ref[...] = leave
    slope_ref[...] = slope
    cols = columns([cumul - jnp.log(step), entry])
    in_map = in_ref[...]
    out_map = out_ref[...]
    out_float = out_map.astype(F32)
    scores = mm_nt(in_map, out_map)
    valid = lax.broadcasted_iota(jnp.int32, (T, T), 0) <= lax.broadcasted_iota(jnp.int32, (T, T), 1)
    lane = lax.broadcasted_iota(jnp.int32, (T, N), 1)
    first = lane < D
    score_grad = jnp.zeros((T, T), F32)
    out_grad = jnp.zeros((T, N), F32)
    found = jnp.zeros((T, N), F32)
    row_sums = []
    for pair in range(PER // 2):
        at = slice(pair * N, (pair + 1) * N)
        sig = sig_ref[:, at]
        cot = cot_ref[:, at]
        zero = jnp.zeros_like(sig)
        sig_grad = jnp.zeros((T, N), F32)
        start = start_ref[at, :]
        top = lax.broadcasted_iota(jnp.int32, (N, N), 0) < D
        none = jnp.zeros_like(start)
        both = jnp.concatenate(
            [jnp.where(top, start, none), jnp.where(top, none, start)], axis=1
        )
        began = mm(cot, both)
        for k in range(2):
            j = 2 * pair + k
            mine = first if k == 0 else jnp.logical_not(first)
            own_sig = jnp.where(mine, sig, zero)
            own_cot = jnp.where(mine, cot, zero)
            mix_grad = mm_nt(own_sig, cot)
            fade = jnp.where(valid, jnp.exp(cumul[j : j + 1, :] - cols[:, j : j + 1]), 0.0)
            mixing = fade * scores
            high, low = split(mixing, 2)
            sig_grad = sig_grad + (mm(high, own_cot) + mm(low, own_cot))
            score_grad = score_grad + mix_grad * fade
            product = mix_grad * mixing
            row_sums.append(jnp.sum(product, axis=0, keepdims=True))
            found = jnp.where(lane == j, jnp.sum(product, axis=1, keepdims=True), found)
            own = began[:, k * N : (k + 1) * N]
            out_grad = out_grad + own * cols[:, PER + j : PER + j + 1]
            found = jnp.where(
                lane == PER + j, jnp.sum(own * out_float, axis=1, keepdims=True), found
            )
        sig_grad_ref[:, at] = sig_grad
    sig_float = sig_ref[...].astype(F32)
    cot_float = cot_ref[...].astype(F32)
    own = jnp.where(
        lax.broadcasted_iota(jnp.int32, (PER, WIDE), 1) // D
        == lax.broadcasted_iota(jnp.int32, (PER, WIDE), 0),
        1.0,
        0.0,
    )
    skip = jnp.sum(own * column_of(skip_ref[...], head, PER), axis=0, keepdims=True)
    sig_grad_ref[...] = sig_grad_ref[...] + skip * cot_float
    high, low = split(score_grad, 2)
    in_grad_ref[...] = mm(high, out_map) + mm(low, out_map)
    out_grad_ref[...] = out_grad + (mm_tn(high, in_map) + mm_tn(low, in_map))
    found = jnp.transpose(found)
    col_sum = found[:PER]
    from_start = found[PER : 2 * PER]
    cumul_grad = jnp.concatenate(row_sums, axis=0) - col_sum + entry * from_start
    rate_grad = rows_times_mask(cumul_grad, mask_of(lambda i, j: i >= j))
    step_grad = col_sum / step - rate_grad * decay
    step_grad_ref[...] = step_grad
    skip_sum = jnp.sum(
        own * jnp.sum(sig_float * cot_float, axis=0, keepdims=True), axis=1, keepdims=True
    )
    decay_sum = -decay * jnp.sum(rate_grad * step, axis=1, keepdims=True)
    bias_sum = jnp.sum(step_grad * slope, axis=1, keepdims=True)
    which = lax.broadcasted_iota(jnp.int32, (PER, N), 1)
    sums = jnp.zeros((PER, N), F32)
    for k, column in enumerate((decay_sum, bias_sum, skip_sum, total, decay)):
        sums = jnp.where(which == k, column, sums)
    sums_ref[...] = sums


def prepare_kernel(
    sig_ref,
    in_ref,
    raw_ref,
    decay_ref,
    bias_ref,
    start_ref,
    after_ref,
    by_decay_ref,
    by_bias_ref,
    sig_high_ref,
    sig_low_ref,
    sig_turned_ref,
):
    head = pl.program_id(0) * PER
    bias = column_of(bias_ref[...], head, PER)
    decay_log = column_of(decay_ref[...], head, PER)
    pre_act, step, decay, cumul = steps_of(raw_ref[...], bias, decay_log)
    slope = jax.nn.sigmoid(pre_act)
    final = cumul[:, T - 1 :]
    total = jnp.exp(final)
    leave = jnp.exp(final - cumul)
    carry = leave * step
    later = rows_times_mask(slope, mask_of(lambda i, j: i > j))
    in_map = in_ref[...]
    sig_float = sig_ref[...].astype(F32)
    sig_turned_ref[...] = jnp.transpose(sig_ref[...])
    sig_high_ref[...], sig_low_ref[...] = split(sig_float * spread(carry), 2)
    into_decay = (final - cumul) * carry
    into_bias = leave * (slope - decay * step * later)
    start = start_ref[...].astype(F32).reshape(PER, D, N)
    turned = jnp.transpose(sig_ref[...]).astype(F32).reshape(PER, D, T)
    for rows, weight, ref in (
        (into_decay, final * total, by_decay_ref),
        (into_bias, -decay * total * jnp.sum(slope, axis=1, keepdims=True), by_bias_ref),
    ):
        high, low = split((turned * rows[:, None, :]).reshape(WIDE, T), 2)
        grown = mm(high, in_map) + mm(low, in_map)
        ref[...] = grown + (start * weight[:, :, None]).reshape(WIDE, N)


def add_sums(slots, odd, ends, sums_ref, sources, targets, kept, got):
    pairs = []
    for k, slot in enumerate(slots):
        at = chosen(group_of(slot, odd), WIDE)
        for source, target in zip(sources, targets, strict=True):
            pairs.append((source.at[at], target.at[wide(k)]))
    copies = fetch(got, pairs)
    which = lax.broadcasted_iota(jnp.int32, (PER, N), 1)
    for batch in batches(SUMS_BATCH, len(slots)):
        for k in batch:
            copies[2 * k].wait()
            copies[2 * k + 1].wait()
        for k in batch:
            end = ends[k][...]
            head = chosen(group_of(slots[k], odd), PER)
            sums = sums_ref[head, :]
            for column, held in enumerate(targets):
                partial = jnp.sum((end * held[wide(k), :]).reshape(PER, D, N), axis=1)
                partial = jnp.sum(partial, axis=1, keepdims=True)
                sums = sums + jnp.where(which == column, partial, 0.0)
            kept[head, :] = sums


def own_sums_kernel(
    odd_ref, own_ref, sums_ref, by_decay_ref, by_bias_ref, kept_ref, by_decay, by_bias, got
):
    ends = [own_ref.at[wide(k)] for k in range(4)]
    kept_ref[...] = jnp.zeros_like(kept_ref)
    sources, targets = (by_decay_ref, by_bias_ref), (by_decay, by_bias)
    add_sums(OWN, odd_ref[0], ends, sums_ref, sources, targets, kept_ref, got)


def sums_kernel(
    odd_ref,
    second_ref,
    first_ref,
    kept_ref,
    sums_ref,
    by_decay_ref,
    by_bias_ref,
    sent_ref,
    by_decay,
    by_bias,
    kept,
    got,
):
    ends = [ref.at[wide(k)] for ref in (first_ref, second_ref) for k in range(2)]
    kept[...] = kept_ref[...]
    sources, targets = (by_decay_ref, by_bias_ref), (by_decay, by_bias)
    add_sums(MET, odd_ref[0], ends, sums_ref, sources, targets, kept, got)
    rows = jnp.transpose(kept[...])
    first = jnp.concatenate([rows[0:1, :H], rows[1:2, :H]], axis=1)
    odd = lax.broadcasted_iota(jnp.int32, (8, N), 0) % 2 == 1
    sent_ref[...] = jnp.where(odd, rows[2:3], first)


def finish_kernel(odd_ref, own_ref, second_ref, first_ref, *refs):
    slots = OWN + MET
    ends = [own_ref.at[wide(k)] for k in range(4)]
    ends += [ref.at[wide(k)] for ref in (first_ref, second_ref) for k in range(2)]
    sums_ref, carry_ref, leave_ref, slope_ref, step_part_ref = refs[:5]
    in_ref, sig_turned_ref, start_ref, sig_part_ref, sig_high_ref, sig_low_ref, in_part_ref = refs[
        5:12
    ]
    step_grad_ref, sig_grad_ref, in_grad_ref = refs[-15:-12]
    in_maps, sig_turned, start, sig_part, sig_high, sig_low, in_part = refs[-12:-5]
    step_grads, sig_grad, in_grad, got, gone = refs[-5:]
    odd = odd_ref[0]
    pairs = []
    every = slice(None)
    for k, slot in enumerate(slots):
        g = group_of(slot, odd)
        cols = ((every, chosen(g, WIDE)), (every, wide(k)))
        rows = ((chosen(g, WIDE),), (wide(k),))
        few = ((every, chosen(g, N)), (every, narrow(k)))
        for (there, here), source, target in (
            (few, in_ref, in_maps),
            (cols, sig_part_ref, sig_part),
            (rows, sig_turned_ref, sig_turned),
            (rows, start_ref, start),
            (cols, sig_high_ref, sig_high),
            (cols, sig_low_ref, sig_low),
            (few, in_part_ref, in_part),
        ):
            pairs.append((source.at[there], target.at[here]))
    each = len(pairs) // len(slots)
    copies = fetch(got, pairs)
    earlier = mask_of(lambda i, j: i < j)
    leaving = []
    for batch in batches(FINISH_BATCH, len(slots)):
        for k in batch:
            for copy in copies[each * k : each * (k + 1)]:
                copy.wait()
        for k in batch:
            head = chosen(group_of(slots[k], odd), PER)
            end = ends[k][...]
            in_map = in_maps[:, narrow(k)]
            carry = carry_ref[head, :]
            columns_here = sums_ref[head, :]
            total = columns_here[:, 3:4]
            decay = columns_here[:, 4:5]
            in_twice = jnp.concatenate([in_map, in_map], axis=1)
            end_high, end_low = split(end, 2)
            pieces = jnp.concatenate([end_high, end_low], axis=1)
            sig_grad[:, wide(k)] = sig_part[:, wide(k)] + spread(carry) * mm_nt(in_twice, pieces)
            both = mm(sig_high[:, wide(k)], pieces)
            in_grad[:, narrow(k)] = in_part[:, narrow(k)] + (
                both[:, :N] + (both[:, N:] + mm(sig_low[:, wide(k)], end_high))
            )
            turned = mm_nt(pieces, in_twice)
            pushed = (sig_turned[wide(k), :].astype(F32) * turned).reshape(PER, D, T)
            pushed = jnp.sum(pushed, axis=1)
            before = rows_times_mask(carry * pushed, earlier)
            held = jnp.sum((end * start[wide(k), :].astype(F32)).reshape(PER, D, N), axis=1)
            held = total * jnp.sum(held, axis=1, keepdims=True)
            step_grad = leave_ref[head, :] * pushed - decay * (before + held)
            step_grads[k * PER : (k + 1) * PER, :] = (
                step_part_ref[head, :] + step_grad
            ) * slope_ref[head, :]
        for k in batch:
            g = group_of(slots[k], odd)
            for at, (source, target) in enumerate(
                (
                    (sig_grad.at[:, wide(k)], sig_grad_ref.at[:, chosen(g, WIDE)]),
                    (in_grad.at[:, narrow(k)], in_grad_ref.at[:, chosen(g, N)]),
                    (step_grads.at[pl.ds(k * PER, PER)], step_grad_ref.at[chosen(g, PER)]),
                )
            ):
                leaving.append(pltpu.make_async_copy(source, target, gone.at[3 * k + at]))
                leaving[-1].start()
    for copy in leaving:
        copy.wait()


def call(kernel, grid, ins, outs, args, flops, mib, scratch=(), aliases={}):
    moved = sum(a.size * a.dtype.itemsize for a in args)
    moved += sum(math.prod(s.shape) * s.dtype.itemsize for _, s in outs)
    return pl.pallas_call(
        kernel,
        grid=(grid,) if grid else (),
        in_specs=ins,
        out_specs=[spec for spec, _ in outs],
        out_shape=[shape for _, shape in outs],
        scratch_shapes=list(scratch),
        input_output_aliases=aliases,
        compiler_params=pltpu.CompilerParams(
            dimension_semantics=("arbitrary",) if grid else None, vmem_limit_bytes=mib * MIB
        ),
        cost_estimate=pl.CostEstimate(flops=flops, bytes_accessed=moved, transcendentals=0),
    )(*args)


def far(*arrays):
    return [pltpu.with_memory_space_constraint(a, pltpu.HBM) for a in arrays]


def near(*arrays):
    return [pltpu.with_memory_space_constraint(a, pltpu.VMEM) for a in arrays]


def f32(*shape):
    return pltpu.HBM(shape, F32)


def bf16(*shape):
    return pltpu.HBM(shape, BF16)


def f32_near(*shape):
    return pltpu.VMEM(shape, F32)


WIDE_COLS = pl.BlockSpec((T, WIDE), lambda g: (0, g))
MAP_COLS = pl.BlockSpec((T, N), lambda g: (0, g))
HEAD_ROWS = pl.BlockSpec((PER, T), lambda g: (g, 0))
HEAD_LANES = pl.BlockSpec((PER, N), lambda g: (g, 0))
HEAD_ALL = pl.BlockSpec((1, H), lambda g: (0, 0))
STATE_COLS = pl.BlockSpec((WIDE, T), lambda g: (g, 0))
STATE_ROWS = pl.BlockSpec((WIDE, N), lambda g: (g, 0))


ELSEWHERE = pl.BlockSpec(memory_space=pl.ANY)
HERE = pl.BlockSpec(memory_space=pltpu.VMEM)
SCALAR = pl.BlockSpec(memory_space=pltpu.SMEM)
COPIES = pltpu.SemaphoreType.DMA


def block_states(odd, cot, out_map, raw, decay_row, bias_row):
    halves = f32_near(H * D // 4 + H // 4, N)
    return call(
        state_kernel,
        0,
        [SCALAR] + [ELSEWHERE] * 5,
        [
            (HERE, f32_near(H * D // 2, N)),
            (HERE, f32_near(H // 2, N)),
            (HERE, halves),
            (HERE, halves),
        ],
        [odd] + far(cot, out_map, raw, decay_row, bias_row),
        4 * H * D * N * T,
        24,
        [
            pltpu.VMEM((T, H * D), BF16),
            pltpu.VMEM((T, G * N), BF16),
            pltpu.VMEM((H, T), F32),
            pltpu.VMEM((1, H), F32),
            pltpu.VMEM((1, H), F32),
            pltpu.VMEM((H, T), F32),
            COPIES((2 * G + 3,)),
        ],
    )


def combine_states(flags, own, own_total, first, second, after, pairs):
    return call(
        combine_kernel,
        0,
        [HERE] * 5 + [ELSEWHERE],
        [
            (HERE, f32_near(pairs, H * D // 2 // pairs + 8, N)),
            (HERE, f32_near(H // 2, N)),
            (ELSEWHERE, f32(H * D // 2, N)),
        ],
        near(flags, own, own_total, second, first) + far(after),
        4 * H * D * N,
        16,
        [pltpu.VMEM((H * D // 2, N), F32), COPIES((4,))],
    )


def scan_states(odd, states, after):
    pairs, rows, _ = states.shape
    rows -= 8
    return call(
        scan_kernel,
        0,
        [SCALAR, HERE, ELSEWHERE],
        [(ELSEWHERE, f32(pairs, rows, N))],
        [odd] + near(states) + far(after),
        H * D * N,
        16,
        [pltpu.VMEM((pairs, rows, N), F32), COPIES((rows // D,))],
    )[0]


def expand_ends(flags, ends, other_total, other, after):
    quarter = f32_near(H * D // 4, N)
    return call(
        expand_kernel,
        0,
        [HERE] * 3 + [ELSEWHERE] * 2,
        [(HERE, f32_near(H * D // 2, N)), (HERE, quarter), (HERE, quarter)],
        near(flags, ends, other_total) + far(other, after),
        4 * H * D * N,
        16,
        [pltpu.VMEM((H * D // 2, N), F32), COPIES((4,))],
    )


def inner_part(
    groups, sig, cot, in_map, out_map, raw, decay_row, bias_row, skip_row, start, after, begun=()
):
    first = groups[0]
    wide_cols = pl.BlockSpec((T, WIDE), lambda g: (0, g + first))
    map_cols = pl.BlockSpec((T, N), lambda g: (0, g + first))
    head_rows = pl.BlockSpec((PER, T), lambda g: (g + first, 0))
    head_lanes = pl.BlockSpec((PER, N), lambda g: (g + first, 0))
    state_rows = pl.BlockSpec((WIDE, N), lambda g: (g + first, 0))
    ins = [wide_cols, wide_cols, map_cols, map_cols, head_rows] + [HEAD_ALL] * 3
    ins += [state_rows] + [ELSEWHERE] * (1 + len(begun))
    return call(
        functools.partial(inner_kernel, first),
        len(groups),
        ins,
        [
            (wide_cols, f32(T, H * D)),
            (map_cols, f32(T, G * N)),
            (map_cols, f32(T, G * N)),
            (head_rows, f32_near(H, T)),
            (head_lanes, f32_near(H, N)),
            (head_rows, f32_near(H, T)),
            (head_rows, f32_near(H, T)),
            (head_rows, f32_near(H, T)),
            (pl.BlockSpec((8, N), lambda g: (0, 0)), f32(8, N)),
        ],
        far(sig, cot, in_map, out_map, raw, decay_row, bias_row, skip_row, start, after)
        + far(*begun[:3])
        + near(*begun[3:]),
        len(groups) * PER * T * T * N * 15,
        24,
        aliases={10 + k: k for k in range(len(begun))},
    )


def prepared_part(sig, in_map, raw, decay_row, bias_row, start, after):
    return call(
        prepare_kernel,
        G,
        [WIDE_COLS, MAP_COLS, HEAD_ROWS, HEAD_ALL, HEAD_ALL, STATE_ROWS]
        + [pl.BlockSpec((H // 2, N), lambda g: (0, 0))],
        [
            (STATE_ROWS, f32(H * D, N)),
            (STATE_ROWS, f32(H * D, N)),
            (WIDE_COLS, bf16(T, H * D)),
            (WIDE_COLS, bf16(T, H * D)),
            (STATE_COLS, bf16(H * D, T)),
        ],
        far(sig, in_map, raw, decay_row, bias_row, start) + near(after),
        H * T * T * N * 5,
        24,
    )


def own_sums(odd, own, sums, by_decay, by_bias):
    return call(
        own_sums_kernel,
        0,
        [SCALAR, HERE, HERE, ELSEWHERE, ELSEWHERE],
        [(HERE, f32_near(N, N))],
        [odd] + near(own, sums) + far(by_decay, by_bias),
        2 * H * D * N,
        12,
        [pltpu.VMEM((H * D // 2, N), F32), pltpu.VMEM((H * D // 2, N), F32), COPIES((G,))],
    )[0]


def all_sums(odd, first, second, kept, sums, by_decay, by_bias):
    return call(
        sums_kernel,
        0,
        [SCALAR] + [HERE] * 4 + [ELSEWHERE] * 2,
        [(HERE, f32_near(8, N))],
        [odd] + near(second, first, kept, sums) + far(by_decay, by_bias),
        2 * H * D * N,
        12,
        [
            pltpu.VMEM((H * D // 2, N), F32),
            pltpu.VMEM((H * D // 2, N), F32),
            pltpu.VMEM((N, N), F32),
            COPIES((G,)),
        ],
    )[0]


def finish_part(odd, ends, rows, elsewhere):
    wide_float, narrow_float = pltpu.VMEM((T, H * D), F32), pltpu.VMEM((T, G * N), F32)
    wide_half = pltpu.VMEM((T, H * D), BF16)
    return call(
        finish_kernel,
        0,
        [SCALAR] + [HERE] * (len(ends) + len(rows)) + [ELSEWHERE] * len(elsewhere),
        [
            (ELSEWHERE, f32(H, T)),
            (ELSEWHERE, f32(T, H * D)),
            (ELSEWHERE, f32(T, G * N)),
        ],
        [odd] + near(*ends, *rows) + far(*elsewhere),
        14 * H * D * N * T,
        36,
        [
            pltpu.VMEM((T, G * N), BF16),
            pltpu.VMEM((H * D, T), BF16),
            pltpu.VMEM((H * D, N), BF16),
            wide_float,
            wide_half,
            wide_half,
            narrow_float,
            pltpu.VMEM((H, T), F32),
            wide_float,
            narrow_float,
            COPIES((7 * G,)),
            COPIES((3 * G,)),
        ],
    )


def local(
    signal, cotangent, input_map, output_map, step_raw, decay_log, step_bias, skip_gain, checkpoints
):
    sig, cot, in_map, out_map, raw = (
        signal[0],
        cotangent[0],
        input_map[0],
        output_map[0],
        step_raw[0],
    )
    decay_row, bias_row, skip_row = decay_log[None], step_bias[None], skip_gain[None]
    start = checkpoints.reshape(H * D, N)
    blocks, deals = lax.axis_size("ctx"), lax.axis_size("dp")

    at = lax.axis_index("ctx")
    odd = lax.rem(at, 2)
    edge = jnp.logical_or(at == 0, at == blocks - 1)
    flags = jnp.stack([1 - odd, odd, 1 - edge.astype(jnp.int32)]).astype(F32)
    flags = jnp.broadcast_to(jnp.pad(flags, (0, 5))[:, None], (8, N))
    odd = odd[None]
    inward = [(i, i ^ 1) for i in range(blocks)]
    across = [(i, (i + 1 if i % 2 else i - 1) % blocks) for i in range(blocks)]
    alike = [list(range(0, blocks, 2)), list(range(1, blocks, 2))]

    own, own_total, first, second = block_states(odd, cot, out_map, raw, decay_row, bias_row)
    second = lax.ppermute(second, "ctx", across)
    first = lax.ppermute(first, "ctx", inward)
    by_decay, by_bias, sig_high, sig_low, sig_turned = prepared_part(
        sig, in_map, raw, decay_row, bias_row, start, own_total
    )
    sent, other_total, other = combine_states(
        flags, own, own_total, first, second, sig_turned, blocks // 2
    )
    states = lax.all_to_all(sent, "ctx", 0, 0, axis_index_groups=alike)
    operands = (sig, cot, in_map, out_map, raw, decay_row, bias_row, skip_row, start)
    *begun, token = inner_part(range(INNER_FIRST), *operands, other)
    ends = scan_states(odd, states, token)
    (
        sig_part,
        in_part,
        out_grad,
        step_part,
        sums_here,
        carry,
        leave,
        slope,
        token,
    ) = inner_part(range(INNER_FIRST, G), *operands, ends, begun)
    ends = lax.all_to_all(ends, "ctx", 0, 0, axis_index_groups=alike)
    own, first, second = expand_ends(flags, ends, other_total, other, token)
    second = lax.ppermute(second, "ctx", across)
    first = lax.ppermute(first, "ctx", inward)

    kept = own_sums(odd, own, sums_here, by_decay, by_bias)

    sums = all_sums(odd, first, second, kept, sums_here, by_decay, by_bias)[:2]
    sums = sums + lax.ppermute(sums, "dp", [(i, i ^ 1) for i in range(deals)])
    devices = blocks * deals
    equal = [[d * blocks + c for d in range(k, deals, 2) for c in range(blocks)] for k in range(2)]
    sent = jnp.broadcast_to(sums[None], (devices // 2, 2, N))
    received = lax.all_to_all(sent, ("dp", "ctx"), 0, 0, axis_index_groups=equal)
    step_grad, sig_grad, in_grad = finish_part(
        odd,
        (own, second, first),
        (sums_here, carry, leave, slope, step_part),
        (in_map, sig_turned, start, sig_part, sig_high, sig_low, in_part),
    )
    summed = jnp.sum(received, axis=0) * (1.0 / (devices * T))
    return (
        sig_grad[None],
        in_grad[None],
        out_grad[None],
        step_grad[None],
        summed[0, :H],
        summed[1, :H],
        summed[0, H:],
    )


def solution(mesh):
    rows = P("dp", "ctx", None)
    placed = (rows, rows, rows, rows, P("dp", None, "ctx"), P(), P(), P())
    return jax.shard_map(
        local,
        mesh=mesh,
        in_specs=placed + (P("dp", "ctx", None, None, None),),
        out_specs=(rows, rows, rows, P("dp", None, "ctx"), P(), P(), P()),
        check_vma=False,
    )
```

```python
import functools
import math

import jax
import jax.numpy as jnp
from jax import lax
from jax.experimental import pallas as pl
from jax.experimental.pallas import tpu as pltpu
from jax.sharding import PartitionSpec as P

T = 256
H = 64
G = 8
D = 64
N = 128
PER = H // G
WIDE = PER * D
F32 = jnp.float32
BF16 = jnp.bfloat16
MIB = 1024 * 1024
STATE_BATCH = 4
OWN = (0, 1, 2, 3)
MET = (4, 5, 6, 7)
INNER_FIRST = 4
SUMS_BATCH = 2
FINISH_BATCH = 2


def split(x, parts):
    pieces = []
    for _ in range(parts):
        piece = x.astype(BF16)
        pieces.append(piece)
        x = x - piece.astype(F32)
    return pieces


def mm(a, b):
    return lax.dot_general(a, b, (((1,), (0,)), ((), ())), preferred_element_type=F32)


def mm_nt(a, b):
    return lax.dot_general(a, b, (((1,), (1,)), ((), ())), preferred_element_type=F32)


def mm_tn(a, b):
    return lax.dot_general(a, b, (((0,), (0,)), ((), ())), preferred_element_type=F32)


def rows_times_mask(rows, mask):
    n = rows.shape[0]
    out = mm(jnp.concatenate(split(rows, 3), axis=0), mask)
    return out[:n] + out[n : 2 * n] + out[2 * n :]


def mask_of(relation):
    i = lax.broadcasted_iota(jnp.int32, (T, T), 0)
    j = lax.broadcasted_iota(jnp.int32, (T, T), 1)
    return jnp.where(relation(i, j), 1.0, 0.0).astype(BF16)


def column_of(row, first, count):
    i = lax.broadcasted_iota(jnp.int32, (count, H), 0) + first
    j = lax.broadcasted_iota(jnp.int32, (count, H), 1)
    return jnp.sum(jnp.where(i == j, row, 0.0), axis=1, keepdims=True)


def steps_of(raw, bias, decay_log):
    pre_act = raw + bias
    step = jnp.maximum(pre_act, 0.0) + jnp.log1p(jnp.exp(-jnp.abs(pre_act)))
    decay = jnp.exp(decay_log)
    rate = -decay * step
    cumul = rows_times_mask(rate, mask_of(lambda i, j: i <= j))
    return pre_act, step, decay, cumul


def spread(rows):
    head = lax.broadcasted_iota(jnp.int32, (PER, WIDE), 0)
    column = lax.broadcasted_iota(jnp.int32, (PER, WIDE), 1)
    own = jnp.where(column // D == head, 1.0, 0.0).astype(BF16)
    return mm_tn(jnp.concatenate(split(rows, 3), axis=0), jnp.concatenate([own] * 3, axis=0))


def columns(rows):
    pad = jnp.zeros((128 - PER * len(rows), T), F32)
    return jnp.transpose(jnp.concatenate(list(rows) + [pad], axis=0))


def fetch(sems, pairs):
    copies = [pltpu.make_async_copy(a, b, sems.at[k]) for k, (a, b) in enumerate(pairs)]
    for copy in copies:
        copy.start()
    return copies


def batches(size, count):
    return [range(k, min(k + size, count)) for k in range(0, count, size)]


def group_of(slot, odd):
    if slot in (0, 1):
        return slot + 2 * odd
    if slot in (2, 3):
        return slot + 4 - 2 * odd
    if slot in (4, 5):
        return slot - 2 - 2 * odd
    return slot - 2 + 2 * odd


def chosen(g, size):
    return pl.ds(pl.multiple_of(g * size, size), size)


def wide(g):
    return pl.ds(g * WIDE, WIDE)


def narrow(g):
    return pl.ds(g * N, N)


def state_kernel(
    odd_ref,
    cot_ref,
    out_ref,
    raw_ref,
    decay_ref,
    bias_ref,
    own_ref,
    own_total_ref,
    first_ref,
    second_ref,
    cot,
    out,
    raw,
    decay,
    bias,
    entries,
    got,
):
    odd = odd_ref[0]
    order = (4, 5, 6, 7, 0, 1, 2, 3)
    pairs = [(raw_ref, raw), (decay_ref, decay), (bias_ref, bias)]
    for slot in order:
        g = group_of(slot, odd)
        pairs.append((cot_ref.at[:, chosen(g, WIDE)], cot.at[:, wide(slot)]))
        pairs.append((out_ref.at[:, chosen(g, N)], out.at[:, narrow(slot)]))
    copies = fetch(got, pairs)
    for copy in copies[:3]:
        copy.wait()
    bias_column = column_of(bias[...], 0, H)
    decay_log = column_of(decay[...], 0, H)
    entries[...] = jnp.exp(steps_of(raw[...], bias_column, decay_log)[3])
    for batch in batches(STATE_BATCH, G):
        for k in batch:
            copies[2 * k + 3].wait()
            copies[2 * k + 4].wait()
        for slot in [order[k] for k in batch]:
            entry = entries[chosen(group_of(slot, odd), PER), :]
            turned = jnp.transpose(cot[:, wide(slot)]).astype(F32)
            weighted = (turned.reshape(PER, D, T) * entry[:, None, :]).reshape(WIDE, T)
            out_map = out[:, narrow(slot)]
            high, low = split(weighted, 2)
            state = mm(high, out_map) + mm(low, out_map)
            total = jnp.broadcast_to(entry[:, T - 1 :], (PER, N))
            if slot < 4:
                own_ref[wide(slot), :] = state
                own_total_ref[slot * PER : (slot + 1) * PER, :] = total
            else:
                ref, k = (first_ref, slot - 4) if slot < 6 else (second_ref, slot - 6)
                ref[wide(k), :] = state
                ref[2 * WIDE + k * PER : 2 * WIDE + (k + 1) * PER, :] = total


def flag_rows(flags_ref):
    keep = flags_ref[2:3, :]
    return (flags_ref[0:1, :], jnp.ones_like(keep)), (flags_ref[1:2, :], keep)


def combine_kernel(
    flags_ref, own_ref, own_total_ref, second_ref, first_ref, after_ref, sent_ref, token_ref
):
    token_ref[...] = jnp.zeros_like(token_ref)
    halves = flag_rows(flags_ref)
    per_half = 2 * PER
    each = sent_ref.shape[0]
    got = per_half // each
    totals = [[] for _ in range(each)]
    for half, ref in enumerate((first_ref, second_ref)):
        earlier, keep = halves[half]
        for h in range(per_half):
            mine = half * per_half + h
            state = own_ref[mine * D : (mine + 1) * D, :]
            total = own_total_ref[mine : mine + 1, :]
            met = ref[h * D : (h + 1) * D, :]
            met_total = ref[per_half * D + h : per_half * D + h + 1, :]
            by_own = jnp.where(earlier > 0, 1.0, met_total * keep)
            by_met = jnp.where(earlier > 0, total * keep, 1.0)
            at, q = h // got, half * got + h % got
            sent_ref[at, q * D : (q + 1) * D, :] = by_own * state + by_met * met
            totals[at].append(total * met_total)
    rows = 2 * got
    for at in range(each):
        pad = [jnp.zeros((8 - rows, N), F32)]
        sent_ref[at, rows * D :, :] = jnp.concatenate(totals[at] + pad, axis=0)


def later_kernel(
    flags_ref,
    own_ref,
    own_total_ref,
    second_ref,
    first_ref,
    token_ref,
    other_total_ref,
    other_ref,
    other,
    gone,
):
    halves = flag_rows(flags_ref)
    per_half = 2 * PER
    other_totals = []
    leaving = []
    for half, ref in enumerate((first_ref, second_ref)):
        earlier, _ = halves[half]
        for k in range(2):
            part = wide(2 * half + k)
            other[part, :] = jnp.where(earlier > 0, ref[wide(k), :], own_ref[part, :])
            leaving.append(
                pltpu.make_async_copy(other.at[part], other_ref.at[part], gone.at[2 * half + k])
            )
            leaving[-1].start()
        mine = slice(half * per_half, (half + 1) * per_half)
        met_totals = ref[per_half * D : per_half * D + per_half, :]
        other_totals.append(jnp.where(earlier > 0, met_totals, own_total_ref[mine, :]))
    other_total_ref[...] = jnp.concatenate(other_totals, axis=0)
    for copy in leaving:
        copy.wait()


def scan_kernel(odd_ref, state_ref, after_ref, end_ref, end, gone):
    pairs, rows, _ = end.shape
    heads = rows // D
    leaving = []
    for h in range(heads):
        at = pl.ds(h * D, D)
        carry = jnp.zeros((D, N), F32)
        if h < heads // 2:
            for b in reversed(range(pairs)):
                end[b, at, :] = carry
                carry = state_ref[b, at, :] + state_ref[b, rows + h : rows + h + 1, :] * carry
        else:
            for k in reversed(range(pairs)):
                b = lax.rem(k + 1 - odd_ref[0], pairs)
                if k < pairs - 1:
                    end[b, at, :] = carry
                total = state_ref[b, rows + h : rows + h + 1, :]
                carry = state_ref[b, at, :] + total * carry
            end[lax.rem(pairs - odd_ref[0], pairs), at, :] = carry
        leaving.append(pltpu.make_async_copy(end.at[:, at], end_ref.at[:, at], gone.at[h]))
        leaving[-1].start()
    for copy in leaving:
        copy.wait()


def expand_kernel(
    flags_ref,
    end_ref,
    other_total_ref,
    other_ref,
    after_ref,
    own_ref,
    first_ref,
    second_ref,
    other,
    got,
):
    per_half = 2 * PER
    pairs = [(other_ref.at[wide(k)], other.at[wide(k)]) for k in range(4)]
    copies = fetch(got, pairs)
    halves = flag_rows(flags_ref)
    each = end_ref.shape[0]
    share = per_half // each
    for half, ref in enumerate((first_ref, second_ref)):
        earlier, keep = halves[half]
        later = 1.0 - earlier
        for h in range(per_half):
            mine = half * per_half + h
            if h % PER == 0:
                copies[mine // PER].wait()
            q = half * share + h % share
            end = end_ref[h // share, q * D : (q + 1) * D, :]
            beside = other[mine * D : (mine + 1) * D, :]
            total = other_total_ref[mine : mine + 1, :] * keep
            own_ref[mine * D : (mine + 1) * D, :] = (earlier * keep) * beside + jnp.where(
                earlier > 0, total, 1.0
            ) * end
            ref[h * D : (h + 1) * D, :] = (later * keep) * beside + jnp.where(
                earlier > 0, 1.0, total
            ) * end


def inner_kernel(
    first_group,
    sig_ref,
    cot_ref,
    in_ref,
    out_ref,
    raw_ref,
    decay_ref,
    bias_ref,
    skip_ref,
    start_ref,
    after_ref,
    *refs,
):
    (
        sig_grad_ref,
        in_grad_ref,
        out_grad_ref,
        step_grad_ref,
        sums_ref,
        carry_ref,
        leave_ref,
        slope_ref,
        token_ref,
    ) = refs[-9:]
    token_ref[...] = jnp.zeros_like(token_ref)
    head = (pl.program_id(0) + first_group) * PER
    bias = column_of(bias_ref[...], head, PER)
    decay_log = column_of(decay_ref[...], head, PER)
    pre_act, step, decay, cumul = steps_of(raw_ref[...], bias, decay_log)
    slope = jax.nn.sigmoid(pre_act)
    entry = jnp.exp(cumul)
    final = cumul[:, T - 1 :]
    total = jnp.exp(final)
    leave = jnp.exp(final - cumul)
    carry = leave * step
    carry_ref[...] = carry
    leave_ref[...] = leave
    slope_ref[...] = slope
    cols = columns([cumul - jnp.log(step), entry])
    in_map = in_ref[...]
    out_map = out_ref[...]
    out_float = out_map.astype(F32)
    scores = mm_nt(in_map, out_map)
    valid = lax.broadcasted_iota(jnp.int32, (T, T), 0) <= lax.broadcasted_iota(jnp.int32, (T, T), 1)
    lane = lax.broadcasted_iota(jnp.int32, (T, N), 1)
    first = lane < D
    score_grad = jnp.zeros((T, T), F32)
    out_grad = jnp.zeros((T, N), F32)
    found = jnp.zeros((T, N), F32)
    row_sums = []
    for pair in range(PER // 2):
        at = slice(pair * N, (pair + 1) * N)
        sig = sig_ref[:, at]
        cot = cot_ref[:, at]
        zero = jnp.zeros_like(sig)
        sig_grad = jnp.zeros((T, N), F32)
        start = start_ref[at, :]
        top = lax.broadcasted_iota(jnp.int32, (N, N), 0) < D
        none = jnp.zeros_like(start)
        both = jnp.concatenate(
            [jnp.where(top, start, none), jnp.where(top, none, start)], axis=1
        )
        began = mm(cot, both)
        for k in range(2):
            j = 2 * pair + k
            mine = first if k == 0 else jnp.logical_not(first)
            own_sig = jnp.where(mine, sig, zero)
            own_cot = jnp.where(mine, cot, zero)
            mix_grad = mm_nt(own_sig, cot)
            fade = jnp.where(valid, jnp.exp(cumul[j : j + 1, :] - cols[:, j : j + 1]), 0.0)
            mixing = fade * scores
            high, low = split(mixing, 2)
            sig_grad = sig_grad + (mm(high, own_cot) + mm(low, own_cot))
            score_grad = score_grad + mix_grad * fade
            product = mix_grad * mixing
            row_sums.append(jnp.sum(product, axis=0, keepdims=True))
            found = jnp.where(lane == j, jnp.sum(product, axis=1, keepdims=True), found)
            own = began[:, k * N : (k + 1) * N]
            out_grad = out_grad + own * cols[:, PER + j : PER + j + 1]
            found = jnp.where(
                lane == PER + j, jnp.sum(own * out_float, axis=1, keepdims=True), found
            )
        sig_grad_ref[:, at] = sig_grad
    sig_float = sig_ref[...].astype(F32)
    cot_float = cot_ref[...].astype(F32)
    own = jnp.where(
        lax.broadcasted_iota(jnp.int32, (PER, WIDE), 1) // D
        == lax.broadcasted_iota(jnp.int32, (PER, WIDE), 0),
        1.0,
        0.0,
    )
    skip = jnp.sum(own * column_of(skip_ref[...], head, PER), axis=0, keepdims=True)
    sig_grad_ref[...] = sig_grad_ref[...] + skip * cot_float
    high, low = split(score_grad, 2)
    in_grad_ref[...] = mm(high, out_map) + mm(low, out_map)
    out_grad_ref[...] = out_grad + (mm_tn(high, in_map) + mm_tn(low, in_map))
    found = jnp.transpose(found)
    col_sum = found[:PER]
    from_start = found[PER : 2 * PER]
    cumul_grad = jnp.concatenate(row_sums, axis=0) - col_sum + entry * from_start
    rate_grad = rows_times_mask(cumul_grad, mask_of(lambda i, j: i >= j))
    step_grad = col_sum / step - rate_grad * decay
    step_grad_ref[...] = step_grad
    skip_sum = jnp.sum(
        own * jnp.sum(sig_float * cot_float, axis=0, keepdims=True), axis=1, keepdims=True
    )
    decay_sum = -decay * jnp.sum(rate_grad * step, axis=1, keepdims=True)
    bias_sum = jnp.sum(step_grad * slope, axis=1, keepdims=True)
    which = lax.broadcasted_iota(jnp.int32, (PER, N), 1)
    sums = jnp.zeros((PER, N), F32)
    for k, column in enumerate((decay_sum, bias_sum, skip_sum, total, decay)):
        sums = jnp.where(which == k, column, sums)
    sums_ref[...] = sums


def prepare_kernel(
    sig_ref,
    in_ref,
    raw_ref,
    decay_ref,
    bias_ref,
    start_ref,
    after_ref,
    by_decay_ref,
    by_bias_ref,
    sig_high_ref,
    sig_low_ref,
    sig_turned_ref,
):
    head = pl.program_id(0) * PER
    bias = column_of(bias_ref[...], head, PER)
    decay_log = column_of(decay_ref[...], head, PER)
    pre_act, step, decay, cumul = steps_of(raw_ref[...], bias, decay_log)
    slope = jax.nn.sigmoid(pre_act)
    final = cumul[:, T - 1 :]
    total = jnp.exp(final)
    leave = jnp.exp(final - cumul)
    carry = leave * step
    later = rows_times_mask(slope, mask_of(lambda i, j: i > j))
    in_map = in_ref[...]
    sig_float = sig_ref[...].astype(F32)
    sig_turned_ref[...] = jnp.transpose(sig_ref[...])
    sig_high_ref[...], sig_low_ref[...] = split(sig_float * spread(carry), 2)
    into_decay = (final - cumul) * carry
    into_bias = leave * (slope - decay * step * later)
    start = start_ref[...].astype(F32).reshape(PER, D, N)
    turned = jnp.transpose(sig_ref[...]).astype(F32).reshape(PER, D, T)
    for rows, weight, ref in (
        (into_decay, final * total, by_decay_ref),
        (into_bias, -decay * total * jnp.sum(slope, axis=1, keepdims=True), by_bias_ref),
    ):
        high, low = split((turned * rows[:, None, :]).reshape(WIDE, T), 2)
        grown = mm(high, in_map) + mm(low, in_map)
        ref[...] = grown + (start * weight[:, :, None]).reshape(WIDE, N)


def add_sums(slots, odd, ends, sums_ref, sources, targets, kept, got):
    pairs = []
    for k, slot in enumerate(slots):
        at = chosen(group_of(slot, odd), WIDE)
        for source, target in zip(sources, targets, strict=True):
            pairs.append((source.at[at], target.at[wide(k)]))
    copies = fetch(got, pairs)
    which = lax.broadcasted_iota(jnp.int32, (PER, N), 1)
    for batch in batches(SUMS_BATCH, len(slots)):
        for k in batch:
            copies[2 * k].wait()
            copies[2 * k + 1].wait()
        for k in batch:
            end = ends[k][...]
            head = chosen(group_of(slots[k], odd), PER)
            sums = sums_ref[head, :]
            for column, held in enumerate(targets):
                partial = jnp.sum((end * held[wide(k), :]).reshape(PER, D, N), axis=1)
                partial = jnp.sum(partial, axis=1, keepdims=True)
                sums = sums + jnp.where(which == column, partial, 0.0)
            kept[head, :] = sums


def own_sums_kernel(
    odd_ref, own_ref, sums_ref, by_decay_ref, by_bias_ref, kept_ref, by_decay, by_bias, got
):
    ends = [own_ref.at[wide(k)] for k in range(4)]
    kept_ref[...] = jnp.zeros_like(kept_ref)
    sources, targets = (by_decay_ref, by_bias_ref), (by_decay, by_bias)
    add_sums(OWN, odd_ref[0], ends, sums_ref, sources, targets, kept_ref, got)


def sums_kernel(
    odd_ref,
    second_ref,
    first_ref,
    kept_ref,
    sums_ref,
    by_decay_ref,
    by_bias_ref,
    sent_ref,
    by_decay,
    by_bias,
    kept,
    got,
):
    ends = [ref.at[wide(k)] for ref in (first_ref, second_ref) for k in range(2)]
    kept[...] = kept_ref[...]
    sources, targets = (by_decay_ref, by_bias_ref), (by_decay, by_bias)
    add_sums(MET, odd_ref[0], ends, sums_ref, sources, targets, kept, got)
    rows = jnp.transpose(kept[...])
    first = jnp.concatenate([rows[0:1, :H], rows[1:2, :H]], axis=1)
    odd = lax.broadcasted_iota(jnp.int32, (8, N), 0) % 2 == 1
    sent_ref[...] = jnp.where(odd, rows[2:3], first)


def finish_kernel(odd_ref, own_ref, second_ref, first_ref, *refs):
    slots = OWN + MET
    ends = [own_ref.at[wide(k)] for k in range(4)]
    ends += [ref.at[wide(k)] for ref in (first_ref, second_ref) for k in range(2)]
    sums_ref, carry_ref, leave_ref, slope_ref, step_part_ref = refs[:5]
    in_ref, sig_turned_ref, start_ref, sig_part_ref, sig_high_ref, sig_low_ref, in_part_ref = refs[
        5:12
    ]
    step_grad_ref, sig_grad_ref, in_grad_ref = refs[-15:-12]
    in_maps, sig_turned, start, sig_part, sig_high, sig_low, in_part = refs[-12:-5]
    step_grads, sig_grad, in_grad, got, gone = refs[-5:]
    odd = odd_ref[0]
    pairs = []
    every = slice(None)
    for k, slot in enumerate(slots):
        g = group_of(slot, odd)
        cols = ((every, chosen(g, WIDE)), (every, wide(k)))
        rows = ((chosen(g, WIDE),), (wide(k),))
        few = ((every, chosen(g, N)), (every, narrow(k)))
        for (there, here), source, target in (
            (few, in_ref, in_maps),
            (cols, sig_part_ref, sig_part),
            (rows, sig_turned_ref, sig_turned),
            (rows, start_ref, start),
            (cols, sig_high_ref, sig_high),
            (cols, sig_low_ref, sig_low),
            (few, in_part_ref, in_part),
        ):
            pairs.append((source.at[there], target.at[here]))
    each = len(pairs) // len(slots)
    copies = fetch(got, pairs)
    earlier = mask_of(lambda i, j: i < j)
    leaving = []
    for batch in batches(FINISH_BATCH, len(slots)):
        for k in batch:
            for copy in copies[each * k : each * (k + 1)]:
                copy.wait()
        for k in batch:
            head = chosen(group_of(slots[k], odd), PER)
            end = ends[k][...]
            in_map = in_maps[:, narrow(k)]
            carry = carry_ref[head, :]
            columns_here = sums_ref[head, :]
            total = columns_here[:, 3:4]
            decay = columns_here[:, 4:5]
            in_twice = jnp.concatenate([in_map, in_map], axis=1)
            end_high, end_low = split(end, 2)
            pieces = jnp.concatenate([end_high, end_low], axis=1)
            sig_grad[:, wide(k)] = sig_part[:, wide(k)] + spread(carry) * mm_nt(in_twice, pieces)
            both = mm(sig_high[:, wide(k)], pieces)
            in_grad[:, narrow(k)] = in_part[:, narrow(k)] + (
                both[:, :N] + (both[:, N:] + mm(sig_low[:, wide(k)], end_high))
            )
            turned = mm_nt(pieces, in_twice)
            pushed = (sig_turned[wide(k), :].astype(F32) * turned).reshape(PER, D, T)
            pushed = jnp.sum(pushed, axis=1)
            before = rows_times_mask(carry * pushed, earlier)
            held = jnp.sum((end * start[wide(k), :].astype(F32)).reshape(PER, D, N), axis=1)
            held = total * jnp.sum(held, axis=1, keepdims=True)
            step_grad = leave_ref[head, :] * pushed - decay * (before + held)
            step_grads[k * PER : (k + 1) * PER, :] = (
                step_part_ref[head, :] + step_grad
            ) * slope_ref[head, :]
        for k in batch:
            g = group_of(slots[k], odd)
            for at, (source, target) in enumerate(
                (
                    (sig_grad.at[:, wide(k)], sig_grad_ref.at[:, chosen(g, WIDE)]),
                    (in_grad.at[:, narrow(k)], in_grad_ref.at[:, chosen(g, N)]),
                    (step_grads.at[pl.ds(k * PER, PER)], step_grad_ref.at[chosen(g, PER)]),
                )
            ):
                leaving.append(pltpu.make_async_copy(source, target, gone.at[3 * k + at]))
                leaving[-1].start()
    for copy in leaving:
        copy.wait()


def call(kernel, grid, ins, outs, args, flops, mib, scratch=(), aliases={}):
    moved = sum(a.size * a.dtype.itemsize for a in args)
    moved += sum(math.prod(s.shape) * s.dtype.itemsize for _, s in outs)
    return pl.pallas_call(
        kernel,
        grid=(grid,) if grid else (),
        in_specs=ins,
        out_specs=[spec for spec, _ in outs],
        out_shape=[shape for _, shape in outs],
        scratch_shapes=list(scratch),
        input_output_aliases=aliases,
        compiler_params=pltpu.CompilerParams(
            dimension_semantics=("arbitrary",) if grid else None, vmem_limit_bytes=mib * MIB
        ),
        cost_estimate=pl.CostEstimate(flops=flops, bytes_accessed=moved, transcendentals=0),
    )(*args)


def far(*arrays):
    return [pltpu.with_memory_space_constraint(a, pltpu.HBM) for a in arrays]


def near(*arrays):
    return [pltpu.with_memory_space_constraint(a, pltpu.VMEM) for a in arrays]


def f32(*shape):
    return pltpu.HBM(shape, F32)


def bf16(*shape):
    return pltpu.HBM(shape, BF16)


def f32_near(*shape):
    return pltpu.VMEM(shape, F32)


WIDE_COLS = pl.BlockSpec((T, WIDE), lambda g: (0, g))
MAP_COLS = pl.BlockSpec((T, N), lambda g: (0, g))
HEAD_ROWS = pl.BlockSpec((PER, T), lambda g: (g, 0))
HEAD_LANES = pl.BlockSpec((PER, N), lambda g: (g, 0))
HEAD_ALL = pl.BlockSpec((1, H), lambda g: (0, 0))
STATE_COLS = pl.BlockSpec((WIDE, T), lambda g: (g, 0))
STATE_ROWS = pl.BlockSpec((WIDE, N), lambda g: (g, 0))


ELSEWHERE = pl.BlockSpec(memory_space=pl.ANY)
HERE = pl.BlockSpec(memory_space=pltpu.VMEM)
SCALAR = pl.BlockSpec(memory_space=pltpu.SMEM)
COPIES = pltpu.SemaphoreType.DMA


def block_states(odd, cot, out_map, raw, decay_row, bias_row):
    halves = f32_near(H * D // 4 + H // 4, N)
    return call(
        state_kernel,
        0,
        [SCALAR] + [ELSEWHERE] * 5,
        [
            (HERE, f32_near(H * D // 2, N)),
            (HERE, f32_near(H // 2, N)),
            (HERE, halves),
            (HERE, halves),
        ],
        [odd] + far(cot, out_map, raw, decay_row, bias_row),
        4 * H * D * N * T,
        24,
        [
            pltpu.VMEM((T, H * D), BF16),
            pltpu.VMEM((T, G * N), BF16),
            pltpu.VMEM((H, T), F32),
            pltpu.VMEM((1, H), F32),
            pltpu.VMEM((1, H), F32),
            pltpu.VMEM((H, T), F32),
            COPIES((2 * G + 3,)),
        ],
    )


def combine_states(flags, own, own_total, first, second, after, pairs):
    return call(
        combine_kernel,
        0,
        [HERE] * 5 + [ELSEWHERE],
        [
            (HERE, f32_near(pairs, H * D // 2 // pairs + 8, N)),
            (HERE, f32_near(8, N)),
        ],
        near(flags, own, own_total, second, first) + far(after),
        4 * H * D * N,
        12,
    )


def later_states(flags, own, own_total, first, second, token):
    return call(
        later_kernel,
        0,
        [HERE] * 6,
        [(HERE, f32_near(H // 2, N)), (ELSEWHERE, f32(H * D // 2, N))],
        near(flags, own, own_total, second, first, token),
        H * D * N,
        12,
        [pltpu.VMEM((H * D // 2, N), F32), COPIES((4,))],
    )


def scan_states(odd, states, after):
    pairs, rows, _ = states.shape
    rows -= 8
    return call(
        scan_kernel,
        0,
        [SCALAR, HERE, ELSEWHERE],
        [(ELSEWHERE, f32(pairs, rows, N))],
        [odd] + near(states) + far(after),
        H * D * N,
        16,
        [pltpu.VMEM((pairs, rows, N), F32), COPIES((rows // D,))],
    )[0]


def expand_ends(flags, ends, other_total, other, after):
    quarter = f32_near(H * D // 4, N)
    return call(
        expand_kernel,
        0,
        [HERE] * 3 + [ELSEWHERE] * 2,
        [(HERE, f32_near(H * D // 2, N)), (HERE, quarter), (HERE, quarter)],
        near(flags, ends, other_total) + far(other, after),
        4 * H * D * N,
        16,
        [pltpu.VMEM((H * D // 2, N), F32), COPIES((4,))],
    )


def inner_part(
    groups, sig, cot, in_map, out_map, raw, decay_row, bias_row, skip_row, start, after, begun=()
):
    first = groups[0]
    wide_cols = pl.BlockSpec((T, WIDE), lambda g: (0, g + first))
    map_cols = pl.BlockSpec((T, N), lambda g: (0, g + first))
    head_rows = pl.BlockSpec((PER, T), lambda g: (g + first, 0))
    head_lanes = pl.BlockSpec((PER, N), lambda g: (g + first, 0))
    state_rows = pl.BlockSpec((WIDE, N), lambda g: (g + first, 0))
    ins = [wide_cols, wide_cols, map_cols, map_cols, head_rows] + [HEAD_ALL] * 3
    ins += [state_rows] + [ELSEWHERE] * (1 + len(begun))
    return call(
        functools.partial(inner_kernel, first),
        len(groups),
        ins,
        [
            (wide_cols, f32(T, H * D)),
            (map_cols, f32(T, G * N)),
            (map_cols, f32(T, G * N)),
            (head_rows, f32_near(H, T)),
            (head_lanes, f32_near(H, N)),
            (head_rows, f32_near(H, T)),
            (head_rows, f32_near(H, T)),
            (head_rows, f32_near(H, T)),
            (pl.BlockSpec((8, N), lambda g: (0, 0)), f32(8, N)),
        ],
        far(sig, cot, in_map, out_map, raw, decay_row, bias_row, skip_row, start, after)
        + far(*begun[:3])
        + near(*begun[3:]),
        len(groups) * PER * T * T * N * 15,
        24,
        aliases={10 + k: k for k in range(len(begun))},
    )


def prepared_part(sig, in_map, raw, decay_row, bias_row, start, after):
    return call(
        prepare_kernel,
        G,
        [WIDE_COLS, MAP_COLS, HEAD_ROWS, HEAD_ALL, HEAD_ALL, STATE_ROWS]
        + [pl.BlockSpec((H // 2, N), lambda g: (0, 0))],
        [
            (STATE_ROWS, f32(H * D, N)),
            (STATE_ROWS, f32(H * D, N)),
            (WIDE_COLS, bf16(T, H * D)),
            (WIDE_COLS, bf16(T, H * D)),
            (STATE_COLS, bf16(H * D, T)),
        ],
        far(sig, in_map, raw, decay_row, bias_row, start) + near(after),
        H * T * T * N * 5,
        24,
    )


def own_sums(odd, own, sums, by_decay, by_bias):
    return call(
        own_sums_kernel,
        0,
        [SCALAR, HERE, HERE, ELSEWHERE, ELSEWHERE],
        [(HERE, f32_near(N, N))],
        [odd] + near(own, sums) + far(by_decay, by_bias),
        2 * H * D * N,
        12,
        [pltpu.VMEM((H * D // 2, N), F32), pltpu.VMEM((H * D // 2, N), F32), COPIES((G,))],
    )[0]


def all_sums(odd, first, second, kept, sums, by_decay, by_bias):
    return call(
        sums_kernel,
        0,
        [SCALAR] + [HERE] * 4 + [ELSEWHERE] * 2,
        [(HERE, f32_near(8, N))],
        [odd] + near(second, first, kept, sums) + far(by_decay, by_bias),
        2 * H * D * N,
        12,
        [
            pltpu.VMEM((H * D // 2, N), F32),
            pltpu.VMEM((H * D // 2, N), F32),
            pltpu.VMEM((N, N), F32),
            COPIES((G,)),
        ],
    )[0]


def finish_part(odd, ends, rows, elsewhere):
    wide_float, narrow_float = pltpu.VMEM((T, H * D), F32), pltpu.VMEM((T, G * N), F32)
    wide_half = pltpu.VMEM((T, H * D), BF16)
    return call(
        finish_kernel,
        0,
        [SCALAR] + [HERE] * (len(ends) + len(rows)) + [ELSEWHERE] * len(elsewhere),
        [
            (ELSEWHERE, f32(H, T)),
            (ELSEWHERE, f32(T, H * D)),
            (ELSEWHERE, f32(T, G * N)),
        ],
        [odd] + near(*ends, *rows) + far(*elsewhere),
        14 * H * D * N * T,
        36,
        [
            pltpu.VMEM((T, G * N), BF16),
            pltpu.VMEM((H * D, T), BF16),
            pltpu.VMEM((H * D, N), BF16),
            wide_float,
            wide_half,
            wide_half,
            narrow_float,
            pltpu.VMEM((H, T), F32),
            wide_float,
            narrow_float,
            COPIES((7 * G,)),
            COPIES((3 * G,)),
        ],
    )


def local(
    signal, cotangent, input_map, output_map, step_raw, decay_log, step_bias, skip_gain, checkpoints
):
    sig, cot, in_map, out_map, raw = (
        signal[0],
        cotangent[0],
        input_map[0],
        output_map[0],
        step_raw[0],
    )
    decay_row, bias_row, skip_row = decay_log[None], step_bias[None], skip_gain[None]
    start = checkpoints.reshape(H * D, N)
    blocks, deals = lax.axis_size("ctx"), lax.axis_size("dp")

    at = lax.axis_index("ctx")
    odd = lax.rem(at, 2)
    edge = jnp.logical_or(at == 0, at == blocks - 1)
    flags = jnp.stack([1 - odd, odd, 1 - edge.astype(jnp.int32)]).astype(F32)
    flags = jnp.broadcast_to(jnp.pad(flags, (0, 5))[:, None], (8, N))
    odd = odd[None]
    inward = [(i, i ^ 1) for i in range(blocks)]
    across = [(i, (i + 1 if i % 2 else i - 1) % blocks) for i in range(blocks)]
    alike = [list(range(0, blocks, 2)), list(range(1, blocks, 2))]

    own, own_total, first, second = block_states(odd, cot, out_map, raw, decay_row, bias_row)
    second = lax.ppermute(second, "ctx", across)
    first = lax.ppermute(first, "ctx", inward)
    by_decay, by_bias, sig_high, sig_low, sig_turned = prepared_part(
        sig, in_map, raw, decay_row, bias_row, start, own_total
    )
    sent, token = combine_states(flags, own, own_total, first, second, sig_turned, blocks // 2)
    states = lax.all_to_all(sent, "ctx", 0, 0, axis_index_groups=alike)
    operands = (sig, cot, in_map, out_map, raw, decay_row, bias_row, skip_row, start)
    other_total, other = later_states(flags, own, own_total, first, second, token)
    *begun, token = inner_part(range(INNER_FIRST), *operands, other)
    ends = scan_states(odd, states, token)
    (
        sig_part,
        in_part,
        out_grad,
        step_part,
        sums_here,
        carry,
        leave,
        slope,
        token,
    ) = inner_part(range(INNER_FIRST, G), *operands, ends, begun)
    ends = lax.all_to_all(ends, "ctx", 0, 0, axis_index_groups=alike)
    own, first, second = expand_ends(flags, ends, other_total, other, token)
    second = lax.ppermute(second, "ctx", across)
    first = lax.ppermute(first, "ctx", inward)

    kept = own_sums(odd, own, sums_here, by_decay, by_bias)

    sums = all_sums(odd, first, second, kept, sums_here, by_decay, by_bias)[:2]
    sums = sums + lax.ppermute(sums, "dp", [(i, i ^ 1) for i in range(deals)])
    devices = blocks * deals
    equal = [[d * blocks + c for d in range(k, deals, 2) for c in range(blocks)] for k in range(2)]
    sent = jnp.broadcast_to(sums[None], (devices // 2, 2, N))
    received = lax.all_to_all(sent, ("dp", "ctx"), 0, 0, axis_index_groups=equal)
    step_grad, sig_grad, in_grad = finish_part(
        odd,
        (own, second, first),
        (sums_here, carry, leave, slope, step_part),
        (in_map, sig_turned, start, sig_part, sig_high, sig_low, in_part),
    )
    summed = jnp.sum(received, axis=0) * (1.0 / (devices * T))
    return (
        sig_grad[None],
        in_grad[None],
        out_grad[None],
        step_grad[None],
        summed[0, :H],
        summed[1, :H],
        summed[0, H:],
    )


def solution(mesh):
    rows = P("dp", "ctx", None)
    placed = (rows, rows, rows, rows, P("dp", None, "ctx"), P(), P(), P())
    return jax.shard_map(
        local,
        mesh=mesh,
        in_specs=placed + (P("dp", "ctx", None, None, None),),
        out_specs=(rows, rows, rows, P("dp", None, "ctx"), P(), P(), P()),
        check_vma=False,
    )
```

```python
import functools
import math

import jax
import jax.numpy as jnp
from jax import lax
from jax.experimental import pallas as pl
from jax.experimental.pallas import tpu as pltpu
from jax.sharding import PartitionSpec as P

T = 256
H = 64
G = 8
D = 64
N = 128
PER = H // G
WIDE = PER * D
F32 = jnp.float32
BF16 = jnp.bfloat16
MIB = 1024 * 1024
STATE_BATCH = 4
OWN = (0, 1, 2, 3)
MET = (4, 5, 6, 7)
INNER_FIRST = 4
SUMS_BATCH = 2
FINISH_BATCH = 3


def split(x, parts):
    pieces = []
    for _ in range(parts):
        piece = x.astype(BF16)
        pieces.append(piece)
        x = x - piece.astype(F32)
    return pieces


def mm(a, b):
    return lax.dot_general(a, b, (((1,), (0,)), ((), ())), preferred_element_type=F32)


def mm_nt(a, b):
    return lax.dot_general(a, b, (((1,), (1,)), ((), ())), preferred_element_type=F32)


def mm_tn(a, b):
    return lax.dot_general(a, b, (((0,), (0,)), ((), ())), preferred_element_type=F32)


def rows_times_mask(rows, mask):
    n = rows.shape[0]
    out = mm(jnp.concatenate(split(rows, 3), axis=0), mask)
    return out[:n] + out[n : 2 * n] + out[2 * n :]


def mask_of(relation):
    i = lax.broadcasted_iota(jnp.int32, (T, T), 0)
    j = lax.broadcasted_iota(jnp.int32, (T, T), 1)
    return jnp.where(relation(i, j), 1.0, 0.0).astype(BF16)


def column_of(row, first, count):
    i = lax.broadcasted_iota(jnp.int32, (count, H), 0) + first
    j = lax.broadcasted_iota(jnp.int32, (count, H), 1)
    return jnp.sum(jnp.where(i == j, row, 0.0), axis=1, keepdims=True)


def steps_of(raw, bias, decay_log):
    pre_act = raw + bias
    step = jnp.maximum(pre_act, 0.0) + jnp.log1p(jnp.exp(-jnp.abs(pre_act)))
    decay = jnp.exp(decay_log)
    rate = -decay * step
    cumul = rows_times_mask(rate, mask_of(lambda i, j: i <= j))
    return pre_act, step, decay, cumul


def spread(rows):
    head = lax.broadcasted_iota(jnp.int32, (PER, WIDE), 0)
    column = lax.broadcasted_iota(jnp.int32, (PER, WIDE), 1)
    own = jnp.where(column // D == head, 1.0, 0.0).astype(BF16)
    return mm_tn(jnp.concatenate(split(rows, 3), axis=0), jnp.concatenate([own] * 3, axis=0))


def columns(rows):
    pad = jnp.zeros((128 - PER * len(rows), T), F32)
    return jnp.transpose(jnp.concatenate(list(rows) + [pad], axis=0))


def fetch(sems, pairs):
    copies = [pltpu.make_async_copy(a, b, sems.at[k]) for k, (a, b) in enumerate(pairs)]
    for copy in copies:
        copy.start()
    return copies


def batches(size, count):
    return [range(k, min(k + size, count)) for k in range(0, count, size)]


def group_of(slot, odd):
    if slot in (0, 1):
        return slot + 2 * odd
    if slot in (2, 3):
        return slot + 4 - 2 * odd
    if slot in (4, 5):
        return slot - 2 - 2 * odd
    return slot - 2 + 2 * odd


def chosen(g, size):
    return pl.ds(pl.multiple_of(g * size, size), size)


def wide(g):
    return pl.ds(g * WIDE, WIDE)


def narrow(g):
    return pl.ds(g * N, N)


def state_kernel(
    odd_ref,
    cot_ref,
    out_ref,
    raw_ref,
    decay_ref,
    bias_ref,
    own_ref,
    own_total_ref,
    first_ref,
    second_ref,
    cot,
    out,
    raw,
    decay,
    bias,
    entries,
    got,
):
    odd = odd_ref[0]
    order = (4, 5, 6, 7, 0, 1, 2, 3)
    pairs = [(raw_ref, raw), (decay_ref, decay), (bias_ref, bias)]
    for slot in order:
        g = group_of(slot, odd)
        pairs.append((cot_ref.at[:, chosen(g, WIDE)], cot.at[:, wide(slot)]))
        pairs.append((out_ref.at[:, chosen(g, N)], out.at[:, narrow(slot)]))
    copies = fetch(got, pairs)
    for copy in copies[:3]:
        copy.wait()
    bias_column = column_of(bias[...], 0, H)
    decay_log = column_of(decay[...], 0, H)
    entries[...] = jnp.exp(steps_of(raw[...], bias_column, decay_log)[3])
    for batch in batches(STATE_BATCH, G):
        for k in batch:
            copies[2 * k + 3].wait()
            copies[2 * k + 4].wait()
        for slot in [order[k] for k in batch]:
            entry = entries[chosen(group_of(slot, odd), PER), :]
            turned = jnp.transpose(cot[:, wide(slot)]).astype(F32)
            weighted = (turned.reshape(PER, D, T) * entry[:, None, :]).reshape(WIDE, T)
            out_map = out[:, narrow(slot)]
            high, low = split(weighted, 2)
            state = mm(high, out_map) + mm(low, out_map)
            total = jnp.broadcast_to(entry[:, T - 1 :], (PER, N))
            if slot < 4:
                own_ref[wide(slot), :] = state
                own_total_ref[slot * PER : (slot + 1) * PER, :] = total
            else:
                ref, k = (first_ref, slot - 4) if slot < 6 else (second_ref, slot - 6)
                ref[wide(k), :] = state
                ref[2 * WIDE + k * PER : 2 * WIDE + (k + 1) * PER, :] = total


def flag_rows(flags_ref):
    keep = flags_ref[2:3, :]
    return (flags_ref[0:1, :], jnp.ones_like(keep)), (flags_ref[1:2, :], keep)


def combine_kernel(
    flags_ref, own_ref, own_total_ref, second_ref, first_ref, after_ref, sent_ref, token_ref
):
    token_ref[...] = jnp.zeros_like(token_ref)
    halves = flag_rows(flags_ref)
    per_half = 2 * PER
    each = sent_ref.shape[0]
    got = per_half // each
    totals = [[] for _ in range(each)]
    for half, ref in enumerate((first_ref, second_ref)):
        earlier, keep = halves[half]
        for h in range(per_half):
            mine = half * per_half + h
            state = own_ref[mine * D : (mine + 1) * D, :]
            total = own_total_ref[mine : mine + 1, :]
            met = ref[h * D : (h + 1) * D, :]
            met_total = ref[per_half * D + h : per_half * D + h + 1, :]
            by_own = jnp.where(earlier > 0, 1.0, met_total * keep)
            by_met = jnp.where(earlier > 0, total * keep, 1.0)
            at, q = h // got, half * got + h % got
            sent_ref[at, q * D : (q + 1) * D, :] = by_own * state + by_met * met
            totals[at].append(total * met_total)
    rows = 2 * got
    for at in range(each):
        pad = [jnp.zeros((8 - rows, N), F32)]
        sent_ref[at, rows * D :, :] = jnp.concatenate(totals[at] + pad, axis=0)


def later_kernel(
    flags_ref,
    own_ref,
    own_total_ref,
    second_ref,
    first_ref,
    token_ref,
    other_total_ref,
    other_ref,
    other,
    gone,
):
    halves = flag_rows(flags_ref)
    per_half = 2 * PER
    other_totals = []
    leaving = []
    for half, ref in enumerate((first_ref, second_ref)):
        earlier, _ = halves[half]
        for k in range(2):
            part = wide(2 * half + k)
            other[part, :] = jnp.where(earlier > 0, ref[wide(k), :], own_ref[part, :])
            leaving.append(
                pltpu.make_async_copy(other.at[part], other_ref.at[part], gone.at[2 * half + k])
            )
            leaving[-1].start()
        mine = slice(half * per_half, (half + 1) * per_half)
        met_totals = ref[per_half * D : per_half * D + per_half, :]
        other_totals.append(jnp.where(earlier > 0, met_totals, own_total_ref[mine, :]))
    other_total_ref[...] = jnp.concatenate(other_totals, axis=0)
    for copy in leaving:
        copy.wait()


def scan_kernel(odd_ref, state_ref, after_ref, end_ref, end, gone):
    pairs, rows, _ = end.shape
    heads = rows // D
    leaving = []
    for h in range(heads):
        at = pl.ds(h * D, D)
        carry = jnp.zeros((D, N), F32)
        if h < heads // 2:
            for b in reversed(range(pairs)):
                end[b, at, :] = carry
                carry = state_ref[b, at, :] + state_ref[b, rows + h : rows + h + 1, :] * carry
        else:
            for k in reversed(range(pairs)):
                b = lax.rem(k + 1 - odd_ref[0], pairs)
                if k < pairs - 1:
                    end[b, at, :] = carry
                total = state_ref[b, rows + h : rows + h + 1, :]
                carry = state_ref[b, at, :] + total * carry
            end[lax.rem(pairs - odd_ref[0], pairs), at, :] = carry
        leaving.append(pltpu.make_async_copy(end.at[:, at], end_ref.at[:, at], gone.at[h]))
        leaving[-1].start()
    for copy in leaving:
        copy.wait()


def expand_kernel(
    flags_ref,
    end_ref,
    other_total_ref,
    other_ref,
    after_ref,
    own_ref,
    first_ref,
    second_ref,
    other,
    got,
):
    per_half = 2 * PER
    pairs = [(other_ref.at[wide(k)], other.at[wide(k)]) for k in range(4)]
    copies = fetch(got, pairs)
    halves = flag_rows(flags_ref)
    each = end_ref.shape[0]
    share = per_half // each
    for half, ref in enumerate((first_ref, second_ref)):
        earlier, keep = halves[half]
        later = 1.0 - earlier
        for h in range(per_half):
            mine = half * per_half + h
            if h % PER == 0:
                copies[mine // PER].wait()
            q = half * share + h % share
            end = end_ref[h // share, q * D : (q + 1) * D, :]
            beside = other[mine * D : (mine + 1) * D, :]
            total = other_total_ref[mine : mine + 1, :] * keep
            own_ref[mine * D : (mine + 1) * D, :] = (earlier * keep) * beside + jnp.where(
                earlier > 0, total, 1.0
            ) * end
            ref[h * D : (h + 1) * D, :] = (later * keep) * beside + jnp.where(
                earlier > 0, 1.0, total
            ) * end


def inner_kernel(
    first_group,
    sig_ref,
    cot_ref,
    in_ref,
    out_ref,
    raw_ref,
    decay_ref,
    bias_ref,
    skip_ref,
    start_ref,
    after_ref,
    *refs,
):
    (
        sig_grad_ref,
        in_grad_ref,
        out_grad_ref,
        step_grad_ref,
        sums_ref,
        carry_ref,
        leave_ref,
        slope_ref,
        token_ref,
    ) = refs[-9:]
    token_ref[...] = jnp.zeros_like(token_ref)
    head = (pl.program_id(0) + first_group) * PER
    bias = column_of(bias_ref[...], head, PER)
    decay_log = column_of(decay_ref[...], head, PER)
    pre_act, step, decay, cumul = steps_of(raw_ref[...], bias, decay_log)
    slope = jax.nn.sigmoid(pre_act)
    entry = jnp.exp(cumul)
    final = cumul[:, T - 1 :]
    total = jnp.exp(final)
    leave = jnp.exp(final - cumul)
    carry = leave * step
    carry_ref[...] = carry
    leave_ref[...] = leave
    slope_ref[...] = slope
    cols = columns([cumul - jnp.log(step), entry])
    in_map = in_ref[...]
    out_map = out_ref[...]
    out_float = out_map.astype(F32)
    scores = mm_nt(in_map, out_map)
    valid = lax.broadcasted_iota(jnp.int32, (T, T), 0) <= lax.broadcasted_iota(jnp.int32, (T, T), 1)
    lane = lax.broadcasted_iota(jnp.int32, (T, N), 1)
    first = lane < D
    score_grad = jnp.zeros((T, T), F32)
    out_grad = jnp.zeros((T, N), F32)
    found = jnp.zeros((T, N), F32)
    row_sums = []
    for pair in range(PER // 2):
        at = slice(pair * N, (pair + 1) * N)
        sig = sig_ref[:, at]
        cot = cot_ref[:, at]
        zero = jnp.zeros_like(sig)
        sig_grad = jnp.zeros((T, N), F32)
        start = start_ref[at, :]
        top = lax.broadcasted_iota(jnp.int32, (N, N), 0) < D
        none = jnp.zeros_like(start)
        both = jnp.concatenate(
            [jnp.where(top, start, none), jnp.where(top, none, start)], axis=1
        )
        began = mm(cot, both)
        for k in range(2):
            j = 2 * pair + k
            mine = first if k == 0 else jnp.logical_not(first)
            own_sig = jnp.where(mine, sig, zero)
            own_cot = jnp.where(mine, cot, zero)
            mix_grad = mm_nt(own_sig, cot)
            fade = jnp.where(valid, jnp.exp(cumul[j : j + 1, :] - cols[:, j : j + 1]), 0.0)
            mixing = fade * scores
            high, low = split(mixing, 2)
            sig_grad = sig_grad + (mm(high, own_cot) + mm(low, own_cot))
            score_grad = score_grad + mix_grad * fade
            product = mix_grad * mixing
            row_sums.append(jnp.sum(product, axis=0, keepdims=True))
            found = jnp.where(lane == j, jnp.sum(product, axis=1, keepdims=True), found)
            own = began[:, k * N : (k + 1) * N]
            out_grad = out_grad + own * cols[:, PER + j : PER + j + 1]
            found = jnp.where(
                lane == PER + j, jnp.sum(own * out_float, axis=1, keepdims=True), found
            )
        sig_grad_ref[:, at] = sig_grad
    sig_float = sig_ref[...].astype(F32)
    cot_float = cot_ref[...].astype(F32)
    own = jnp.where(
        lax.broadcasted_iota(jnp.int32, (PER, WIDE), 1) // D
        == lax.broadcasted_iota(jnp.int32, (PER, WIDE), 0),
        1.0,
        0.0,
    )
    skip = jnp.sum(own * column_of(skip_ref[...], head, PER), axis=0, keepdims=True)
    sig_grad_ref[...] = sig_grad_ref[...] + skip * cot_float
    high, low = split(score_grad, 2)
    in_grad_ref[...] = mm(high, out_map) + mm(low, out_map)
    out_grad_ref[...] = out_grad + (mm_tn(high, in_map) + mm_tn(low, in_map))
    found = jnp.transpose(found)
    col_sum = found[:PER]
    from_start = found[PER : 2 * PER]
    cumul_grad = jnp.concatenate(row_sums, axis=0) - col_sum + entry * from_start
    rate_grad = rows_times_mask(cumul_grad, mask_of(lambda i, j: i >= j))
    step_grad = col_sum / step - rate_grad * decay
    step_grad_ref[...] = step_grad
    skip_sum = jnp.sum(
        own * jnp.sum(sig_float * cot_float, axis=0, keepdims=True), axis=1, keepdims=True
    )
    decay_sum = -decay * jnp.sum(rate_grad * step, axis=1, keepdims=True)
    bias_sum = jnp.sum(step_grad * slope, axis=1, keepdims=True)
    which = lax.broadcasted_iota(jnp.int32, (PER, N), 1)
    sums = jnp.zeros((PER, N), F32)
    for k, column in enumerate((decay_sum, bias_sum, skip_sum, total, decay)):
        sums = jnp.where(which == k, column, sums)
    sums_ref[...] = sums


def prepare_kernel(
    sig_ref,
    in_ref,
    raw_ref,
    decay_ref,
    bias_ref,
    start_ref,
    after_ref,
    by_decay_ref,
    by_bias_ref,
    sig_high_ref,
    sig_low_ref,
    sig_turned_ref,
):
    head = pl.program_id(0) * PER
    bias = column_of(bias_ref[...], head, PER)
    decay_log = column_of(decay_ref[...], head, PER)
    pre_act, step, decay, cumul = steps_of(raw_ref[...], bias, decay_log)
    slope = jax.nn.sigmoid(pre_act)
    final = cumul[:, T - 1 :]
    total = jnp.exp(final)
    leave = jnp.exp(final - cumul)
    carry = leave * step
    later = rows_times_mask(slope, mask_of(lambda i, j: i > j))
    in_map = in_ref[...]
    sig_float = sig_ref[...].astype(F32)
    sig_turned_ref[...] = jnp.transpose(sig_ref[...])
    sig_high_ref[...], sig_low_ref[...] = split(sig_float * spread(carry), 2)
    into_decay = (final - cumul) * carry
    into_bias = leave * (slope - decay * step * later)
    start = start_ref[...].astype(F32).reshape(PER, D, N)
    turned = jnp.transpose(sig_ref[...]).astype(F32).reshape(PER, D, T)
    for rows, weight, ref in (
        (into_decay, final * total, by_decay_ref),
        (into_bias, -decay * total * jnp.sum(slope, axis=1, keepdims=True), by_bias_ref),
    ):
        high, low = split((turned * rows[:, None, :]).reshape(WIDE, T), 2)
        grown = mm(high, in_map) + mm(low, in_map)
        ref[...] = grown + (start * weight[:, :, None]).reshape(WIDE, N)


def add_sums(slots, odd, ends, sums_ref, sources, targets, kept, got):
    pairs = []
    for k, slot in enumerate(slots):
        at = chosen(group_of(slot, odd), WIDE)
        for source, target in zip(sources, targets, strict=True):
            pairs.append((source.at[at], target.at[wide(k)]))
    copies = fetch(got, pairs)
    which = lax.broadcasted_iota(jnp.int32, (PER, N), 1)
    for batch in batches(SUMS_BATCH, len(slots)):
        for k in batch:
            copies[2 * k].wait()
            copies[2 * k + 1].wait()
        for k in batch:
            end = ends[k][...]
            head = chosen(group_of(slots[k], odd), PER)
            sums = sums_ref[head, :]
            for column, held in enumerate(targets):
                partial = jnp.sum((end * held[wide(k), :]).reshape(PER, D, N), axis=1)
                partial = jnp.sum(partial, axis=1, keepdims=True)
                sums = sums + jnp.where(which == column, partial, 0.0)
            kept[head, :] = sums


def own_sums_kernel(
    odd_ref, own_ref, sums_ref, by_decay_ref, by_bias_ref, kept_ref, by_decay, by_bias, got
):
    ends = [own_ref.at[wide(k)] for k in range(4)]
    kept_ref[...] = jnp.zeros_like(kept_ref)
    sources, targets = (by_decay_ref, by_bias_ref), (by_decay, by_bias)
    add_sums(OWN, odd_ref[0], ends, sums_ref, sources, targets, kept_ref, got)


def sums_kernel(
    odd_ref,
    second_ref,
    first_ref,
    kept_ref,
    sums_ref,
    by_decay_ref,
    by_bias_ref,
    sent_ref,
    by_decay,
    by_bias,
    kept,
    got,
):
    ends = [ref.at[wide(k)] for ref in (first_ref, second_ref) for k in range(2)]
    kept[...] = kept_ref[...]
    sources, targets = (by_decay_ref, by_bias_ref), (by_decay, by_bias)
    add_sums(MET, odd_ref[0], ends, sums_ref, sources, targets, kept, got)
    rows = jnp.transpose(kept[...])
    first = jnp.concatenate([rows[0:1, :H], rows[1:2, :H]], axis=1)
    odd = lax.broadcasted_iota(jnp.int32, (8, N), 0) % 2 == 1
    sent_ref[...] = jnp.where(odd, rows[2:3], first)


def finish_kernel(odd_ref, own_ref, second_ref, first_ref, *refs):
    slots = OWN + MET
    ends = [own_ref.at[wide(k)] for k in range(4)]
    ends += [ref.at[wide(k)] for ref in (first_ref, second_ref) for k in range(2)]
    sums_ref, carry_ref, leave_ref, slope_ref, step_part_ref = refs[:5]
    in_ref, sig_turned_ref, start_ref, sig_part_ref, sig_high_ref, sig_low_ref, in_part_ref = refs[
        5:12
    ]
    step_grad_ref, sig_grad_ref, in_grad_ref = refs[-15:-12]
    in_maps, sig_turned, start, sig_part, sig_high, sig_low, in_part = refs[-12:-5]
    step_grads, sig_grad, in_grad, got, gone = refs[-5:]
    odd = odd_ref[0]
    pairs = []
    every = slice(None)
    for k, slot in enumerate(slots):
        g = group_of(slot, odd)
        cols = ((every, chosen(g, WIDE)), (every, wide(k)))
        rows = ((chosen(g, WIDE),), (wide(k),))
        few = ((every, chosen(g, N)), (every, narrow(k)))
        for (there, here), source, target in (
            (few, in_ref, in_maps),
            (cols, sig_part_ref, sig_part),
            (rows, sig_turned_ref, sig_turned),
            (rows, start_ref, start),
            (cols, sig_high_ref, sig_high),
            (cols, sig_low_ref, sig_low),
            (few, in_part_ref, in_part),
        ):
            pairs.append((source.at[there], target.at[here]))
    each = len(pairs) // len(slots)
    copies = fetch(got, pairs)
    earlier = mask_of(lambda i, j: i < j)
    leaving = []
    for batch in batches(FINISH_BATCH, len(slots)):
        for k in batch:
            for copy in copies[each * k : each * (k + 1)]:
                copy.wait()
        for k in batch:
            head = chosen(group_of(slots[k], odd), PER)
            end = ends[k][...]
            in_map = in_maps[:, narrow(k)]
            carry = carry_ref[head, :]
            columns_here = sums_ref[head, :]
            total = columns_here[:, 3:4]
            decay = columns_here[:, 4:5]
            in_twice = jnp.concatenate([in_map, in_map], axis=1)
            end_high, end_low = split(end, 2)
            pieces = jnp.concatenate([end_high, end_low], axis=1)
            sig_grad[:, wide(k)] = sig_part[:, wide(k)] + spread(carry) * mm_nt(in_twice, pieces)
            both = mm(sig_high[:, wide(k)], pieces)
            in_grad[:, narrow(k)] = in_part[:, narrow(k)] + (
                both[:, :N] + (both[:, N:] + mm(sig_low[:, wide(k)], end_high))
            )
            turned = mm_nt(pieces, in_twice)
            pushed = (sig_turned[wide(k), :].astype(F32) * turned).reshape(PER, D, T)
            pushed = jnp.sum(pushed, axis=1)
            before = rows_times_mask(carry * pushed, earlier)
            held = jnp.sum((end * start[wide(k), :].astype(F32)).reshape(PER, D, N), axis=1)
            held = total * jnp.sum(held, axis=1, keepdims=True)
            step_grad = leave_ref[head, :] * pushed - decay * (before + held)
            step_grads[k * PER : (k + 1) * PER, :] = (
                step_part_ref[head, :] + step_grad
            ) * slope_ref[head, :]
        for k in batch:
            g = group_of(slots[k], odd)
            for at, (source, target) in enumerate(
                (
                    (sig_grad.at[:, wide(k)], sig_grad_ref.at[:, chosen(g, WIDE)]),
                    (in_grad.at[:, narrow(k)], in_grad_ref.at[:, chosen(g, N)]),
                    (step_grads.at[pl.ds(k * PER, PER)], step_grad_ref.at[chosen(g, PER)]),
                )
            ):
                leaving.append(pltpu.make_async_copy(source, target, gone.at[3 * k + at]))
                leaving[-1].start()
    for copy in leaving:
        copy.wait()


def call(kernel, grid, ins, outs, args, flops, mib, scratch=(), aliases={}):
    moved = sum(a.size * a.dtype.itemsize for a in args)
    moved += sum(math.prod(s.shape) * s.dtype.itemsize for _, s in outs)
    return pl.pallas_call(
        kernel,
        grid=(grid,) if grid else (),
        in_specs=ins,
        out_specs=[spec for spec, _ in outs],
        out_shape=[shape for _, shape in outs],
        scratch_shapes=list(scratch),
        input_output_aliases=aliases,
        compiler_params=pltpu.CompilerParams(
            dimension_semantics=("arbitrary",) if grid else None, vmem_limit_bytes=mib * MIB
        ),
        cost_estimate=pl.CostEstimate(flops=flops, bytes_accessed=moved, transcendentals=0),
    )(*args)


def far(*arrays):
    return [pltpu.with_memory_space_constraint(a, pltpu.HBM) for a in arrays]


def near(*arrays):
    return [pltpu.with_memory_space_constraint(a, pltpu.VMEM) for a in arrays]


def f32(*shape):
    return pltpu.HBM(shape, F32)


def bf16(*shape):
    return pltpu.HBM(shape, BF16)


def f32_near(*shape):
    return pltpu.VMEM(shape, F32)


WIDE_COLS = pl.BlockSpec((T, WIDE), lambda g: (0, g))
MAP_COLS = pl.BlockSpec((T, N), lambda g: (0, g))
HEAD_ROWS = pl.BlockSpec((PER, T), lambda g: (g, 0))
HEAD_LANES = pl.BlockSpec((PER, N), lambda g: (g, 0))
HEAD_ALL = pl.BlockSpec((1, H), lambda g: (0, 0))
STATE_COLS = pl.BlockSpec((WIDE, T), lambda g: (g, 0))
STATE_ROWS = pl.BlockSpec((WIDE, N), lambda g: (g, 0))


ELSEWHERE = pl.BlockSpec(memory_space=pl.ANY)
HERE = pl.BlockSpec(memory_space=pltpu.VMEM)
SCALAR = pl.BlockSpec(memory_space=pltpu.SMEM)
COPIES = pltpu.SemaphoreType.DMA


def block_states(odd, cot, out_map, raw, decay_row, bias_row):
    halves = f32_near(H * D // 4 + H // 4, N)
    return call(
        state_kernel,
        0,
        [SCALAR] + [ELSEWHERE] * 5,
        [
            (HERE, f32_near(H * D // 2, N)),
            (HERE, f32_near(H // 2, N)),
            (HERE, halves),
            (HERE, halves),
        ],
        [odd] + far(cot, out_map, raw, decay_row, bias_row),
        4 * H * D * N * T,
        24,
        [
            pltpu.VMEM((T, H * D), BF16),
            pltpu.VMEM((T, G * N), BF16),
            pltpu.VMEM((H, T), F32),
            pltpu.VMEM((1, H), F32),
            pltpu.VMEM((1, H), F32),
            pltpu.VMEM((H, T), F32),
            COPIES((2 * G + 3,)),
        ],
    )


def combine_states(flags, own, own_total, first, second, after, pairs):
    return call(
        combine_kernel,
        0,
        [HERE] * 5 + [ELSEWHERE],
        [
            (HERE, f32_near(pairs, H * D // 2 // pairs + 8, N)),
            (HERE, f32_near(8, N)),
        ],
        near(flags, own, own_total, second, first) + far(after),
        4 * H * D * N,
        12,
    )


def later_states(flags, own, own_total, first, second, token):
    return call(
        later_kernel,
        0,
        [HERE] * 6,
        [(HERE, f32_near(H // 2, N)), (ELSEWHERE, f32(H * D // 2, N))],
        near(flags, own, own_total, second, first, token),
        H * D * N,
        12,
        [pltpu.VMEM((H * D // 2, N), F32), COPIES((4,))],
    )


def scan_states(odd, states, after):
    pairs, rows, _ = states.shape
    rows -= 8
    return call(
        scan_kernel,
        0,
        [SCALAR, HERE, ELSEWHERE],
        [(ELSEWHERE, f32(pairs, rows, N))],
        [odd] + near(states) + far(after),
        H * D * N,
        16,
        [pltpu.VMEM((pairs, rows, N), F32), COPIES((rows // D,))],
    )[0]


def expand_ends(flags, ends, other_total, other, after):
    quarter = f32_near(H * D // 4, N)
    return call(
        expand_kernel,
        0,
        [HERE] * 3 + [ELSEWHERE] * 2,
        [(HERE, f32_near(H * D // 2, N)), (HERE, quarter), (HERE, quarter)],
        near(flags, ends, other_total) + far(other, after),
        4 * H * D * N,
        16,
        [pltpu.VMEM((H * D // 2, N), F32), COPIES((4,))],
    )


def inner_part(
    groups, sig, cot, in_map, out_map, raw, decay_row, bias_row, skip_row, start, after, begun=()
):
    first = groups[0]
    wide_cols = pl.BlockSpec((T, WIDE), lambda g: (0, g + first))
    map_cols = pl.BlockSpec((T, N), lambda g: (0, g + first))
    head_rows = pl.BlockSpec((PER, T), lambda g: (g + first, 0))
    head_lanes = pl.BlockSpec((PER, N), lambda g: (g + first, 0))
    state_rows = pl.BlockSpec((WIDE, N), lambda g: (g + first, 0))
    ins = [wide_cols, wide_cols, map_cols, map_cols, head_rows] + [HEAD_ALL] * 3
    ins += [state_rows] + [ELSEWHERE] * (1 + len(begun))
    return call(
        functools.partial(inner_kernel, first),
        len(groups),
        ins,
        [
            (wide_cols, f32(T, H * D)),
            (map_cols, f32(T, G * N)),
            (map_cols, f32(T, G * N)),
            (head_rows, f32_near(H, T)),
            (head_lanes, f32_near(H, N)),
            (head_rows, f32_near(H, T)),
            (head_rows, f32_near(H, T)),
            (head_rows, f32_near(H, T)),
            (pl.BlockSpec((8, N), lambda g: (0, 0)), f32(8, N)),
        ],
        far(sig, cot, in_map, out_map, raw, decay_row, bias_row, skip_row, start, after)
        + far(*begun[:3])
        + near(*begun[3:]),
        len(groups) * PER * T * T * N * 15,
        24,
        aliases={10 + k: k for k in range(len(begun))},
    )


def prepared_part(sig, in_map, raw, decay_row, bias_row, start, after):
    return call(
        prepare_kernel,
        G,
        [WIDE_COLS, MAP_COLS, HEAD_ROWS, HEAD_ALL, HEAD_ALL, STATE_ROWS]
        + [pl.BlockSpec((H // 2, N), lambda g: (0, 0))],
        [
            (STATE_ROWS, f32(H * D, N)),
            (STATE_ROWS, f32(H * D, N)),
            (WIDE_COLS, bf16(T, H * D)),
            (WIDE_COLS, bf16(T, H * D)),
            (STATE_COLS, bf16(H * D, T)),
        ],
        far(sig, in_map, raw, decay_row, bias_row, start) + near(after),
        H * T * T * N * 5,
        24,
    )


def own_sums(odd, own, sums, by_decay, by_bias):
    return call(
        own_sums_kernel,
        0,
        [SCALAR, HERE, HERE, ELSEWHERE, ELSEWHERE],
        [(HERE, f32_near(N, N))],
        [odd] + near(own, sums) + far(by_decay, by_bias),
        2 * H * D * N,
        12,
        [pltpu.VMEM((H * D // 2, N), F32), pltpu.VMEM((H * D // 2, N), F32), COPIES((G,))],
    )[0]


def all_sums(odd, first, second, kept, sums, by_decay, by_bias):
    return call(
        sums_kernel,
        0,
        [SCALAR] + [HERE] * 4 + [ELSEWHERE] * 2,
        [(HERE, f32_near(8, N))],
        [odd] + near(second, first, kept, sums) + far(by_decay, by_bias),
        2 * H * D * N,
        12,
        [
            pltpu.VMEM((H * D // 2, N), F32),
            pltpu.VMEM((H * D // 2, N), F32),
            pltpu.VMEM((N, N), F32),
            COPIES((G,)),
        ],
    )[0]


def finish_part(odd, ends, rows, elsewhere):
    wide_float, narrow_float = pltpu.VMEM((T, H * D), F32), pltpu.VMEM((T, G * N), F32)
    wide_half = pltpu.VMEM((T, H * D), BF16)
    return call(
        finish_kernel,
        0,
        [SCALAR] + [HERE] * (len(ends) + len(rows)) + [ELSEWHERE] * len(elsewhere),
        [
            (ELSEWHERE, f32(H, T)),
            (ELSEWHERE, f32(T, H * D)),
            (ELSEWHERE, f32(T, G * N)),
        ],
        [odd] + near(*ends, *rows) + far(*elsewhere),
        14 * H * D * N * T,
        36,
        [
            pltpu.VMEM((T, G * N), BF16),
            pltpu.VMEM((H * D, T), BF16),
            pltpu.VMEM((H * D, N), BF16),
            wide_float,
            wide_half,
            wide_half,
            narrow_float,
            pltpu.VMEM((H, T), F32),
            wide_float,
            narrow_float,
            COPIES((7 * G,)),
            COPIES((3 * G,)),
        ],
    )


def local(
    signal, cotangent, input_map, output_map, step_raw, decay_log, step_bias, skip_gain, checkpoints
):
    sig, cot, in_map, out_map, raw = (
        signal[0],
        cotangent[0],
        input_map[0],
        output_map[0],
        step_raw[0],
    )
    decay_row, bias_row, skip_row = decay_log[None], step_bias[None], skip_gain[None]
    start = checkpoints.reshape(H * D, N)
    blocks, deals = lax.axis_size("ctx"), lax.axis_size("dp")

    at = lax.axis_index("ctx")
    odd = lax.rem(at, 2)
    edge = jnp.logical_or(at == 0, at == blocks - 1)
    flags = jnp.stack([1 - odd, odd, 1 - edge.astype(jnp.int32)]).astype(F32)
    flags = jnp.broadcast_to(jnp.pad(flags, (0, 5))[:, None], (8, N))
    odd = odd[None]
    inward = [(i, i ^ 1) for i in range(blocks)]
    across = [(i, (i + 1 if i % 2 else i - 1) % blocks) for i in range(blocks)]
    alike = [list(range(0, blocks, 2)), list(range(1, blocks, 2))]

    own, own_total, first, second = block_states(odd, cot, out_map, raw, decay_row, bias_row)
    second = lax.ppermute(second, "ctx", across)
    first = lax.ppermute(first, "ctx", inward)
    by_decay, by_bias, sig_high, sig_low, sig_turned = prepared_part(
        sig, in_map, raw, decay_row, bias_row, start, own_total
    )
    sent, token = combine_states(flags, own, own_total, first, second, sig_turned, blocks // 2)
    states = lax.all_to_all(sent, "ctx", 0, 0, axis_index_groups=alike)
    operands = (sig, cot, in_map, out_map, raw, decay_row, bias_row, skip_row, start)
    other_total, other = later_states(flags, own, own_total, first, second, token)
    *begun, token = inner_part(range(INNER_FIRST), *operands, other)
    ends = scan_states(odd, states, token)
    (
        sig_part,
        in_part,
        out_grad,
        step_part,
        sums_here,
        carry,
        leave,
        slope,
        token,
    ) = inner_part(range(INNER_FIRST, G), *operands, ends, begun)
    ends = lax.all_to_all(ends, "ctx", 0, 0, axis_index_groups=alike)
    own, first, second = expand_ends(flags, ends, other_total, other, token)
    second = lax.ppermute(second, "ctx", across)
    first = lax.ppermute(first, "ctx", inward)

    kept = own_sums(odd, own, sums_here, by_decay, by_bias)

    sums = all_sums(odd, first, second, kept, sums_here, by_decay, by_bias)[:2]
    sums = sums + lax.ppermute(sums, "dp", [(i, i ^ 1) for i in range(deals)])
    devices = blocks * deals
    equal = [[d * blocks + c for d in range(k, deals, 2) for c in range(blocks)] for k in range(2)]
    sent = jnp.broadcast_to(sums[None], (devices // 2, 2, N))
    received = lax.all_to_all(sent, ("dp", "ctx"), 0, 0, axis_index_groups=equal)
    step_grad, sig_grad, in_grad = finish_part(
        odd,
        (own, second, first),
        (sums_here, carry, leave, slope, step_part),
        (in_map, sig_turned, start, sig_part, sig_high, sig_low, in_part),
    )
    summed = jnp.sum(received, axis=0) * (1.0 / (devices * T))
    return (
        sig_grad[None],
        in_grad[None],
        out_grad[None],
        step_grad[None],
        summed[0, :H],
        summed[1, :H],
        summed[0, H:],
    )


def solution(mesh):
    rows = P("dp", "ctx", None)
    placed = (rows, rows, rows, rows, P("dp", None, "ctx"), P(), P(), P())
    return jax.shard_map(
        local,
        mesh=mesh,
        in_specs=placed + (P("dp", "ctx", None, None, None),),
        out_specs=(rows, rows, rows, P("dp", None, "ctx"), P(), P(), P()),
        check_vma=False,
    )
```
